32 devices in a mesh: wide: 8 (over z, y), narrow: 4 (over x, core).
Axes of the slice: x: 2, y: 2, z: 4, core: 2. Of those that a mesh axis runs over, the one named last changes fastest.
Arguments:
- tokens: bfloat16 [16384, 768], P(('wide', 'narrow')), may hold values from -6 to 6
- memory: bfloat16 [16384, 768], P(('wide', 'narrow')), may hold values from -6 to 6
- cotangent: bfloat16 [16384, 768], P(('wide', 'narrow')), may hold values from -6 to 6
- dec_segments: int32 [32, 512], P(('wide', 'narrow')), may hold values from 0 to 15, never falling along the last dimension, each value on 1 to 256 neighbouring positions
- enc_segments: int32 [32, 512], P(('wide', 'narrow')), may hold values from 0 to 15, never falling along the last dimension, each value on 1 to 256 neighbouring positions
- dec_valid: int32 [32, 512], P(('wide', 'narrow')), may hold values 0 or 1
- attn_weights: bfloat16 [8, 768, 768], P(None, ('wide', 'narrow')), may hold values from -0.3125 to 0.3125
- w_in: bfloat16 [768, 3072], P(('wide', 'narrow')), may hold values from -0.21875 to 0.21875
- w_out: bfloat16 [3072, 768], P(('wide', 'narrow')), may hold values from -0.109375 to 0.109375
- norm_gains: bfloat16 [3, 768], P(None, ('wide', 'narrow')), may hold values from 0.5 to 1.5
- rel_table: bfloat16 [32, 12], replicated, may hold values from -4 to 4
- row_main: float32 [9, 768], P(None, ('wide', 'narrow')), may hold values from 1 to 1000
- row_out: float32 [3072], P(('wide', 'narrow')), may hold values from 1 to 1000
- col_main: float32 [9, 768], replicated, may hold values from 1 to 1000
- col_in: float32 [3072], replicated, may hold values from 1 to 1000
Outputs:
- layer_out: bfloat16 [16384, 768], P(('wide', 'narrow'))
- grad_tokens: float32 [16384, 768], P(('wide', 'narrow'))
- grad_memory: float32 [16384, 768], P(('wide', 'narrow'))
- grad_attn: float32 [8, 768, 768], P(None, ('wide', 'narrow'))
- grad_in: float32 [768, 3072], P(('wide', 'narrow'))
- grad_out: float32 [3072, 768], P(('wide', 'narrow'))
- grad_gains: float32 [3, 768], P(None, ('wide', 'narrow'))
- grad_table: float32 [32, 12], replicated
- new_row_main: float32 [9, 768], P(None, ('wide', 'narrow'))
- new_row_out: float32 [3072], P(('wide', 'narrow'))
- new_col_main: float32 [9, 768], replicated
- new_col_in: float32 [3072], replicated
The draws below stay inside these ranges and needn't reach their ends.
Inputs may be any that keep to these rules, and one draw needn't show every extreme that they name: `dec_segments`: in each row the ids never fall, every id 0 to 15 appears, and a document has 1 to 256 positions. `enc_segments`: in each row the ids never fall, every id 0 to 15 appears, and a document has 1 to 256 positions.
All inputs are finite; a program needn't handle non-finite values. No bound on the sum of `dec_valid` on one device may be relied on, other than what follows from the above.
Results may differ from the reference program's by a relative error of at most 0.018.
The reference program's roundings to bfloat16 on the way count: a program that leaves them out, or rounds other values in their place, can miss the bound.
Values may be sent and summed in bfloat16 or wider, within the bound.
No kernel may reach another device: no remote copies, remote signals or barrier semaphores. Data moves between devices by JAX's collectives and lax.ppermute only.
A program may use at most 256 MiB of HBM per device.

```python
import math
import jax
import jax.numpy as jnp
import numpy as np
from jax import lax

D = 768
HEADS = 12
HEAD = 64
FF = 3072
BUCKETS = 32
MAXDIST = 128
TOK_DEV = 512
ROWS = 32
TOKENS = 16384
BLOCK = 512
MOST = 256
SEGS = 16


def set_ends(drawn, rng, least, high):
    spot = [jax.random.randint(jax.random.fold_in(rng, axis), (), 0, length) for axis, length in enumerate(drawn.shape)]
    longest = drawn.shape.index(max(drawn.shape))
    beside = spot[:longest] + [(spot[longest] + 1) % drawn.shape[longest]] + spot[longest + 1:]
    return drawn.at[tuple(spot)].set(least).at[tuple(beside)].set(high)


def level_of(stream_key, extent, cuts, smallest, top_value):
    def one(axis_at, parts):
        heights = jax.random.uniform(jax.random.fold_in(jax.random.fold_in(stream_key, 6), axis_at), (parts,), jnp.float32, smallest / len(cuts), top_value / len(cuts))
        return jnp.repeat(jnp.exp(heights), extent[axis_at] // parts).reshape((-1,) + (1,) * (len(extent) - axis_at - 1))

    level = one(*cuts[0])
    for cut in cuts[1:]:
        level = level * one(*cut)
    return level


def profile(amount, total, most, lean):
    weights = [(1 << 20) // math.isqrt(grade ** lean) + 1 for grade in range(2, amount + 1)]
    rest, counts = total - most - (amount - 1), [1] * (amount - 1)
    while rest > 0:
        movable = [i for i in range(amount - 1) if counts[i] < most]
        mass, left = sum([weights[i] for i in movable]), rest
        for i in movable:
            extra = min(most - counts[i], max(1, left * weights[i] // mass), rest)
            counts[i] = counts[i] + extra
            rest = rest - extra
    return np.array([most] + counts)


def ragged_sizes(key, count, total, most, lean):
    if count == 2:
        one = jax.random.randint(key, (), max(1, total - most), min(most, total - 1) + 1)
        return jnp.stack([one, total - one])
    sizes = jnp.asarray(profile(count, total, most, lean), jnp.int32)
    twos = (count - 1) // 2
    donor, taker = sizes[1:1 + 2 * twos:2], sizes[2:2 + 2 * twos:2]
    slack = jnp.minimum(donor - 1, most - taker)
    shifted = jax.random.randint(jax.random.fold_in(key, 1), (twos,), 0, 1 << 20) % (slack + 1)
    sizes = sizes.at[1:1 + 2 * twos:2].set(donor - shifted).at[2:2 + 2 * twos:2].set(taker + shifted)
    return sizes[jax.random.permutation(jax.random.fold_in(key, 2), count)]


def gaussian(stream_key, extent, deviation, reach, shards=(), held_as=jnp.bfloat16):
    values = jax.random.normal(stream_key, extent, jnp.float32) * deviation
    if len(shards) > 0:
        values = level_of(stream_key, extent, shards, -0.22, 0.18) * values
    return jnp.clip(values, min=-reach, max=reach).astype(held_as)


def setup_inputs(seed: int = 0) -> dict:
    splits = jax.random.split(jax.random.key(seed), 16)
    tokens = gaussian(splits[0], (TOKENS, D), 1.0, 6.0, ((0, 32),))
    memory = gaussian(splits[1], (TOKENS, D), 1.0, 6.0, ((0, 32),))
    cotangent = gaussian(splits[2], (TOKENS, D), 1.0, 6.0, ((0, 32),))
    dec_segments = jax.vmap(lambda own: jnp.searchsorted(jnp.cumsum(ragged_sizes(own, SEGS, TOK_DEV, MOST, 2)), jnp.arange(TOK_DEV), side="right"))(jax.random.split(splits[3], ROWS)).reshape((ROWS, TOK_DEV)).astype(jnp.int32)
    enc_segments = jax.vmap(lambda own: jnp.searchsorted(jnp.cumsum(ragged_sizes(own, SEGS, TOK_DEV, MOST, 2)), jnp.arange(TOK_DEV), side="right"))(jax.random.split(splits[4], ROWS)).reshape((ROWS, TOK_DEV)).astype(jnp.int32)
    dec_valid = set_ends((jax.random.randint(splits[5], (ROWS, TOK_DEV), 0, 8) < 7).astype(jnp.int32), jax.random.fold_in(splits[5], 1), 0, 1)
    attn_weights = gaussian(splits[6], (8, D, D), (D // 2) ** -0.5, 0.3125, ((1, 32),))
    w_in = gaussian(splits[7], (D, FF), D ** -0.5, 0.21875, ((0, 32),))
    w_out = gaussian(splits[8], (FF, D), FF ** -0.5, 0.109375, ((0, 32),))
    norm_gains = jnp.clip(1.0 + 0.1 * jax.random.normal(splits[9], (3, D), jnp.float32), 0.5, 1.5).astype(jnp.bfloat16)
    rel_table = gaussian(splits[10], (BUCKETS, HEADS), 1.0, 4.0)
    row_main = jnp.clip(jnp.exp(math.log(1000.0) - 6.9077553 * jax.random.uniform(splits[11], (9, D), jnp.float32) ** level_of(splits[11], (9, D), ((1, 32),), -0.2, 0.2)), 1.0, 1000.0)
    row_out = jnp.clip(jnp.exp(math.log(1000.0) - 6.9077553 * jax.random.uniform(splits[12], (FF,), jnp.float32) ** level_of(splits[12], (FF,), ((0, 32),), -0.2, 0.2)), 1.0, 1000.0)
    col_main = jnp.clip(jnp.exp(jax.random.uniform(splits[13], (9, D), jnp.float32, math.log(1.0), math.log(1000.0))), 1.0, 1000.0)
    col_in = jnp.clip(jnp.exp(jax.random.uniform(splits[14], (FF,), jnp.float32, math.log(1.0), math.log(1000.0))), 1.0, 1000.0)
    return {"tokens": tokens, "memory": memory, "cotangent": cotangent, "dec_segments": dec_segments, "enc_segments": enc_segments, "dec_valid": dec_valid, "attn_weights": attn_weights, "w_in": w_in, "w_out": w_out, "norm_gains": norm_gains, "rel_table": rel_table, "row_main": row_main, "row_out": row_out, "col_main": col_main, "col_in": col_in}


EPSILON = 1e-06
DECAY = 0.8
NEGATIVE = -1e+30
HIGH = lax.Precision.HIGHEST

@jax.custom_vjp
def low(v):
    return lax.optimization_barrier(v.astype(jnp.bfloat16)).astype(jnp.float32)

@jax.custom_vjp
def low_back(v):
    return v

def low_keep(v):
    return (low(v), None)

def low_pass(kept, grad):
    return (grad,)

def back_keep(v):
    return (v, None)

def back_low(kept, grad):
    return (low(grad),)
low.defvjp(low_keep, low_pass)
low_back.defvjp(back_keep, back_low)

def both_ways(values):
    return low(low_back(values))

def thresholds():
    exact_count = BUCKETS // 2
    limits = list(range(1, exact_count + 1))
    for bucket_level in range(exact_count + 1, BUCKETS):
        limits.append(int(math.ceil(exact_count * (MAXDIST / exact_count) ** ((bucket_level - exact_count) / exact_count))))
    return limits

def bucket_table(distance, number_type):
    level_count = jnp.zeros(distance.shape, jnp.int32)
    for threshold in thresholds():
        level_count = level_count + (distance >= threshold).astype(jnp.int32)
    return (level_count[..., None] == jnp.arange(BUCKETS, dtype=jnp.int32)).astype(number_type)

def rms_norm(hidden, gain_row):
    return hidden * lax.rsqrt(lax.optimization_barrier(jnp.mean(hidden * hidden, axis=-1, keepdims=True)) + EPSILON) * gain_row

def matmul(left_side, right_side):
    return jnp.dot(left_side, right_side, precision=HIGH)

def softmax_mix(scores, allowed, value_heads):
    scores = low_back(scores)
    scores = jnp.where(allowed[None], scores, NEGATIVE)
    largest = lax.optimization_barrier(jnp.max(scores, axis=-1, keepdims=True))
    weights = jnp.exp(scores - largest)
    weights = low(weights / lax.optimization_barrier(jnp.sum(weights, axis=-1, keepdims=True)))
    return jnp.einsum('hqk,khd->qhd', weights, value_heads, precision=HIGH)

def self_block(query_block, first_row, key_heads, value_heads, table_low, segment, key_valid):
    row_index = first_row + jnp.arange(BLOCK, dtype=jnp.int32)
    col_index = jnp.arange(segment.shape[0], dtype=jnp.int32)
    distance = row_index[:, None] - col_index[None, :]
    row_segment = lax.dynamic_slice_in_dim(segment, first_row, BLOCK)
    allowed = (row_segment[:, None] == segment[None, :]) & (distance >= 0) & ((key_valid[None, :] > 0) | (distance == 0))
    scores = jnp.einsum('qhd,khd->hqk', query_block, key_heads, precision=HIGH) * HEAD ** (-0.5)
    scores = scores + jnp.einsum('qkb,bh->hqk', bucket_table(distance, jnp.float32), table_low, precision=HIGH)
    return softmax_mix(scores, allowed, value_heads)

def cross_block(query_block, first_row, key_heads, value_heads, segment, mem_segment):
    row_segment = lax.dynamic_slice_in_dim(segment, first_row, BLOCK)
    allowed = row_segment[:, None] == mem_segment[None, :]
    scores = jnp.einsum('qhd,khd->hqk', query_block, key_heads, precision=HIGH) * HEAD ** (-0.5)
    return softmax_mix(scores, allowed, value_heads)

def blocked(block_fn, query_heads, extras):
    block_count = query_heads.shape[0] // BLOCK
    pieces = query_heads.reshape(block_count, BLOCK, HEADS, HEAD)
    starts = jnp.arange(block_count, dtype=jnp.int32) * BLOCK

    def one_block(block_pair):
        return block_fn(block_pair[0], block_pair[1], *extras)
    outputs = lax.map(jax.checkpoint(one_block), (pieces, starts))
    return outputs.reshape(block_count * BLOCK, HEADS * HEAD)

def layer(attn_w, weight_in, weight_out, gain_all, bias_table, residual, mem_rows, segment, mem_segment, key_valid):
    first_low = low(rms_norm(residual, gain_all[0]))
    query_heads = both_ways(matmul(first_low, attn_w[0])).reshape(-1, HEADS, HEAD)
    key_heads = both_ways(matmul(first_low, attn_w[1])).reshape(-1, HEADS, HEAD)
    value_heads = both_ways(matmul(first_low, attn_w[2])).reshape(-1, HEADS, HEAD)
    table_low = low(bias_table)
    mixed = both_ways(blocked(self_block, query_heads, (key_heads, value_heads, table_low, segment, key_valid)))
    middle = residual + low_back(matmul(mixed, attn_w[3]))
    second_low = low(rms_norm(middle, gain_all[1]))
    cross_query = both_ways(matmul(second_low, attn_w[4])).reshape(-1, HEADS, HEAD)
    memory_keys = both_ways(matmul(mem_rows, attn_w[5])).reshape(-1, HEADS, HEAD)
    memory_values = both_ways(matmul(mem_rows, attn_w[6])).reshape(-1, HEADS, HEAD)
    crossed = both_ways(blocked(cross_block, cross_query, (memory_keys, memory_values, segment, mem_segment)))
    upper = middle + low_back(matmul(crossed, attn_w[7]))
    third_low = low(rms_norm(upper, gain_all[2]))
    inner = low_back(matmul(third_low, weight_in))
    active = low(jax.nn.gelu(inner, approximate=True))
    return upper + low_back(matmul(active, weight_out))

def reference(tokens, memory, cotangent, dec_segments, enc_segments, dec_valid, attn_weights, w_in, w_out, norm_gains, rel_table, row_main, row_out, col_main, col_in):
    row_total = dec_segments.shape[0]
    params = (attn_weights.astype(jnp.float32), w_in.astype(jnp.float32), w_out.astype(jnp.float32), norm_gains.astype(jnp.float32), rel_table.astype(jnp.float32))
    inputs_rows = (tokens.astype(jnp.float32).reshape(row_total, TOK_DEV, D), memory.astype(jnp.float32).reshape(row_total, TOK_DEV, D), cotangent.astype(jnp.float32).reshape(row_total, TOK_DEV, D), dec_segments, enc_segments, dec_valid)

    def one_row(running, row_data):
        tokens_row, memory_row, cot_row, segment, mem_segment, key_valid = row_data

        def forward(attn_w, weight_in, weight_out, gain_all, bias_table, residual, mem_rows):
            return layer(attn_w, weight_in, weight_out, gain_all, bias_table, residual, mem_rows, segment, mem_segment, key_valid)
        result, pullback = jax.vjp(forward, *params, tokens_row, memory_row)
        grads = pullback(cot_row)
        running = tuple((summed + added for summed, added in zip(running, grads[:5])))
        return (running, (result, grads[5], grads[6]))
    initial = tuple((jnp.zeros_like(param) for param in params))
    running, (result_rows, token_rows, memory_rows) = lax.scan(one_row, initial, inputs_rows)
    grad_attn, grad_in, grad_out, grad_gains, grad_table = running
    square_attn = grad_attn * grad_attn
    square_in = grad_in * grad_in
    square_out = grad_out * grad_out
    row_means = jnp.concatenate([lax.optimization_barrier(jnp.mean(square_attn, axis=2)), lax.optimization_barrier(jnp.mean(square_in, axis=1))[None]], axis=0)
    col_means = jnp.concatenate([lax.optimization_barrier(jnp.mean(square_attn, axis=1)), lax.optimization_barrier(jnp.mean(square_out, axis=0))[None]], axis=0)
    new_row_main = DECAY * row_main + (1.0 - DECAY) * row_means
    new_row_out = DECAY * row_out + (1.0 - DECAY) * lax.optimization_barrier(jnp.mean(square_out, axis=1))
    new_col_main = DECAY * col_main + (1.0 - DECAY) * col_means
    new_col_in = DECAY * col_in + (1.0 - DECAY) * lax.optimization_barrier(jnp.mean(square_in, axis=0))
    layer_out = result_rows.reshape(TOKENS, D).astype(jnp.bfloat16)
    grad_tokens = token_rows.reshape(TOKENS, D)
    grad_memory = memory_rows.reshape(TOKENS, D)
    return (layer_out, grad_tokens, grad_memory, grad_attn, grad_in, grad_out, grad_gains, grad_table, new_row_main, new_row_out, new_col_main, new_col_in)
```

```python
import math

import jax
import jax.numpy as jnp
from jax import lax
from jax.sharding import PartitionSpec as P

D = 768
HEADS = 12
HEAD = 64
FF = 3072
BUCKETS = 32
MAXDIST = 128
BLOCK = 512


EPSILON = 1e-06
DECAY = 0.8
NEGATIVE = -1e30


def thresholds():
    exact_count = BUCKETS // 2
    limits = list(range(1, exact_count + 1))
    for bucket_level in range(exact_count + 1, BUCKETS):
        limits.append(
            int(
                math.ceil(
                    exact_count
                    * (MAXDIST / exact_count) ** ((bucket_level - exact_count) / exact_count)
                )
            )
        )
    return limits


def bucket_table(distance, number_type):
    level_count = jnp.zeros(distance.shape, jnp.int32)
    for threshold in thresholds():
        level_count = level_count + (distance >= threshold).astype(jnp.int32)
    return (level_count[..., None] == jnp.arange(BUCKETS, dtype=jnp.int32)).astype(number_type)


def rms_norm(hidden, gain_row):
    return (
        hidden * lax.rsqrt(jnp.mean(hidden * hidden, axis=-1, keepdims=True) + EPSILON) * gain_row
    )


def smooth(values):
    return jax.nn.gelu(values, approximate=True)


def project(left_side, right_side):
    return jnp.dot(left_side, right_side, preferred_element_type=jnp.float32)


def project_back(gradient, right_side):
    return lax.dot_general(
        gradient, right_side, (((1,), (1,)), ((), ())), preferred_element_type=jnp.float32
    )


def weight_grad(left_side, gradient):
    return lax.dot_general(
        left_side, gradient, (((0,), (0,)), ((), ())), preferred_element_type=jnp.float32
    )


def split_heads(matrix):
    return matrix.reshape(matrix.shape[0], HEADS, HEAD)


def join_heads(tensor):
    return tensor.reshape(tensor.shape[0], HEADS * HEAD)


def self_mask(first_row, segment, key_valid):
    row_index = first_row + jnp.arange(BLOCK, dtype=jnp.int32)
    col_index = jnp.arange(segment.shape[0], dtype=jnp.int32)
    distance = row_index[:, None] - col_index[None, :]
    allowed = (
        (segment[:, None] == segment[None, :])
        & (distance >= 0)
        & ((key_valid[None, :] > 0) | (distance == 0))
    )
    return (allowed, bucket_table(distance, jnp.bfloat16))


def cross_mask(segment, mem_segment):
    return (segment[:, None] == mem_segment[None, :], None)


def block_scores(query_block, key_heads, bias_table, allowed, buckets):
    scores = jnp.einsum(
        "qhd,khd->hqk", query_block, key_heads, preferred_element_type=jnp.float32
    ) * HEAD ** (-0.5)
    if buckets is not None:
        scores = scores + jnp.einsum(
            "qkb,bh->hqk", buckets, bias_table, preferred_element_type=jnp.float32
        )
    return jnp.where(allowed[None], scores, NEGATIVE)


def attend_forward(query_heads, key_heads, value_heads, make_mask, bias_table):
    allowed, buckets = make_mask(0)
    scores = block_scores(query_heads, key_heads, bias_table, allowed, buckets)
    largest = jnp.max(scores, axis=-1, keepdims=True)
    weights = jnp.exp(scores - largest)
    totals = jnp.sum(weights, axis=-1, keepdims=True)
    weights_low = (weights / totals).astype(jnp.bfloat16)
    results = jnp.einsum(
        "hqk,khd->qhd", weights_low, value_heads, preferred_element_type=jnp.float32
    )
    log_totals = [largest + jnp.log(totals)]
    return (results, log_totals)


def attend_backward(
    query_heads, key_heads, value_heads, make_mask, bias_table, log_totals, grad_heads
):
    table_grad = jnp.zeros((BUCKETS, HEADS), jnp.float32)
    allowed, buckets = make_mask(0)
    scores = block_scores(query_heads, key_heads, bias_table, allowed, buckets)
    weights = jnp.exp(scores - log_totals[0])
    grad_weights = jnp.einsum(
        "qhd,khd->hqk", grad_heads, value_heads, preferred_element_type=jnp.float32
    )
    centre = jnp.sum(weights * grad_weights, axis=-1, keepdims=True)
    grad_scores = (weights * (grad_weights - centre)).astype(jnp.bfloat16)
    query_grads = jnp.einsum(
        "hqk,khd->qhd", grad_scores, key_heads, preferred_element_type=jnp.float32
    ) * HEAD ** (-0.5)
    key_grad = jnp.einsum(
        "hqk,qhd->khd", grad_scores, query_heads, preferred_element_type=jnp.float32
    ) * HEAD ** (-0.5)
    value_grad = jnp.einsum(
        "hqk,qhd->khd", weights.astype(jnp.bfloat16), grad_heads, preferred_element_type=jnp.float32
    )
    if buckets is not None:
        table_grad = jnp.einsum(
            "qkb,hqk->bh", buckets, grad_scores, preferred_element_type=jnp.float32
        )
    return (query_grads, key_grad, value_grad, table_grad)


AXES = ("wide", "narrow")


class Cube:
    def __init__(self):
        self.count = lax.axis_size("wide") * lax.axis_size("narrow")
        self.bits = self.count.bit_length() - 1
        self.me = lax.axis_index("wide") * lax.axis_size("narrow") + lax.axis_index("narrow")
        high = list(range(self.bits - 1, 1, -1))
        self.plan_a = high + [1]
        self.plan_b = [1] + high

    def bit(self, which):
        return (self.me >> which) & 1

    def swap(self, value, which):
        pairs = [(i, i ^ (1 << which)) for i in range(self.count)]
        return lax.ppermute(value, AXES, pairs)

    def place(self, mine, theirs, which, axis, joined):
        join = jnp.concatenate if joined else jnp.stack
        return jnp.where(
            self.bit(which) == 0, join([mine, theirs], axis), join([theirs, mine], axis)
        )

    def gather(self, value, plan):
        held = []
        for which in plan:
            axis = sum(other > which for other in held)
            value = self.place(value, self.swap(value, which), which, axis, False)
            held.append(which)
        return value.reshape((-1,) + value.shape[len(plan) :])

    def scatter(self, value, plan):
        value = value.reshape((2,) * (self.bits - 1) + value.shape[1:])
        held = sorted(plan, reverse=True)
        for which in reversed(plan):
            axis = held.index(which)
            mine = self.bit(which)
            send = lax.dynamic_index_in_dim(value, 1 - mine, axis, False).astype(jnp.bfloat16)
            keep = lax.dynamic_index_in_dim(value, mine, axis, False)
            value = keep + self.swap(send, which).astype(jnp.float32)
            held.remove(which)
        return value

    def half(self, value, whose):
        size = value.shape[-1] // 2
        return lax.dynamic_slice_in_dim(value, whose * size, size, value.ndim - 1)

    def total(self, value):
        for which in range(self.bits):
            value = value + self.swap(value, which)
        return value


def gather_weights(cube, attn, w_in, w_out, gains):
    rows = attn.shape[1]
    wide_in = w_in.shape[1] // 2
    core = cube.bit(0)

    def packed(whose):
        attn_half = cube.half(attn, whose).reshape(-1, D // 2)
        in_half = cube.half(w_in, whose).reshape(-1, D // 2)
        out_half = cube.half(w_out, whose)
        gain_rows = jnp.pad(gains, ((0, 5), (0, D // 2 - gains.shape[1])))
        return attn_half, in_half, out_half, gain_rows

    mine = packed(core)
    sizes = [part.shape[0] for part in mine]
    theirs = cube.swap(jnp.concatenate(packed(1 - core), axis=0), 0)
    starts = [sum(sizes[:k]) for k in range(5)]
    theirs = [theirs[starts[k] : starts[k + 1]] for k in range(4)]
    attn_pair = cube.place(
        mine[0].reshape(8, rows, D // 2), theirs[0].reshape(8, rows, D // 2), 0, 1, True
    )
    in_pair = cube.place(
        mine[1].reshape(rows, wide_in), theirs[1].reshape(rows, wide_in), 0, 0, True
    )
    out_pair = cube.place(mine[2], theirs[2], 0, 0, True)
    gain_pair = cube.place(mine[3], theirs[3], 0, 0, True)

    def whole(value):
        return cube.place(value, cube.swap(value, 0), 0, value.ndim - 1, True)

    def attn_chunk(first, last, plan, extra):
        chunk = attn_pair[first:last].reshape(-1, D // 2)
        chunk = chunk if extra is None else jnp.concatenate([chunk, extra], axis=0)
        gathered = cube.gather(chunk, plan)
        full = whole(gathered)
        size = (last - first) * rows * 2
        weights = full[:, :size].reshape(-1, last - first, rows * 2, D)
        return [weights[:, k].reshape(D, D) for k in range(last - first)], gathered[:, size:]

    first_two, gain_rows = attn_chunk(0, 2, cube.plan_a, gain_pair)
    next_two, _ = attn_chunk(2, 4, cube.plan_b, None)
    last_four, _ = attn_chunk(4, 8, cube.plan_a, None)
    in_full = whole(cube.gather(in_pair, cube.plan_b)).reshape(D, -1)
    out_full = whole(cube.gather(out_pair, cube.plan_a)).reshape(-1, D)
    gain_full = gain_rows.reshape(-1, 8, D // 2)[:, :3, : gains.shape[1]]
    gain_full = gain_full.transpose(1, 0, 2).reshape(3, D)
    return first_two + next_two + last_four, in_full, out_full, gain_full


def pair_grads(cube, products, plan):
    core = cube.bit(0)
    chips = cube.count // 2
    sent = [weight_grad(left, cube.half(right, 1 - core)) for left, right in products]
    kept = [weight_grad(left, cube.half(right, core)) for left, right in products]
    columns = kept[0].shape[1]

    def stacked(parts):
        return jnp.concatenate(
            [part.reshape(chips, part.shape[0] // chips, columns) for part in parts], axis=1
        )

    value = stacked(kept) + cube.swap(stacked(sent).astype(jnp.bfloat16), 0).astype(jnp.float32)
    value = cube.scatter(value, plan)
    value = value.reshape(len(products), 2, -1, columns)
    mine = lax.dynamic_index_in_dim(value, core, 1, False)
    theirs = cube.swap(lax.dynamic_index_in_dim(value, 1 - core, 1, False), 0)
    return cube.place(mine, theirs, 0, 2, True)


def on_device(
    tokens,
    memory,
    cotangent,
    dec_segments,
    enc_segments,
    dec_valid,
    attn_weights,
    w_in,
    w_out,
    norm_gains,
    rel_table,
    row_main,
    row_out,
    col_main,
    col_in,
):
    cube = Cube()
    attn_full, in_full, out_full, gain_full = gather_weights(
        cube, attn_weights, w_in, w_out, norm_gains
    )
    segment = dec_segments[0]
    mem_segment = enc_segments[0]
    key_valid = dec_valid[0]

    def self_masks(first_row):
        return self_mask(first_row, segment, key_valid)

    def cross_masks(first_row):
        return cross_mask(segment, mem_segment)

    residual = tokens.astype(jnp.float32)
    normed_first, norm_back_first = jax.vjp(rms_norm, residual, gain_full[0].astype(jnp.float32))
    first_low = normed_first.astype(jnp.bfloat16)
    query_heads = split_heads(project(first_low, attn_full[0]).astype(jnp.bfloat16))
    key_heads = split_heads(project(first_low, attn_full[1]).astype(jnp.bfloat16))
    value_heads = split_heads(project(first_low, attn_full[2]).astype(jnp.bfloat16))
    mixed, self_logs = attend_forward(query_heads, key_heads, value_heads, self_masks, rel_table)
    mixed_low = join_heads(mixed).astype(jnp.bfloat16)
    middle = residual + project(mixed_low, attn_full[3])
    normed_second, norm_back_second = jax.vjp(rms_norm, middle, gain_full[1].astype(jnp.float32))
    second_low = normed_second.astype(jnp.bfloat16)
    cross_query = split_heads(project(second_low, attn_full[4]).astype(jnp.bfloat16))
    memory_keys = split_heads(project(memory, attn_full[5]).astype(jnp.bfloat16))
    memory_values = split_heads(project(memory, attn_full[6]).astype(jnp.bfloat16))
    crossed, cross_logs = attend_forward(
        cross_query, memory_keys, memory_values, cross_masks, rel_table
    )
    crossed_low = join_heads(crossed).astype(jnp.bfloat16)
    upper = middle + project(crossed_low, attn_full[7])
    normed_third, norm_back_third = jax.vjp(rms_norm, upper, gain_full[2].astype(jnp.float32))
    third_low = normed_third.astype(jnp.bfloat16)
    inner = project(third_low, in_full)
    activated, smooth_back = jax.vjp(smooth, inner)
    active_low = activated.astype(jnp.bfloat16)
    layer_out = (upper + project(active_low, out_full)).astype(jnp.bfloat16)
    grad_upper = cotangent.astype(jnp.float32)
    grad_ffn_branch = grad_upper.astype(jnp.bfloat16)
    grad_out = pair_grads(cube, [(active_low, grad_ffn_branch)], cube.plan_a)[0]
    (grad_inner,) = smooth_back(project_back(grad_ffn_branch, out_full))
    grad_inner_low = grad_inner.astype(jnp.bfloat16)
    grad_in = pair_grads(cube, [(third_low, grad_inner_low)], cube.plan_b)[0]
    grad_from_third, grad_gain_third = norm_back_third(project_back(grad_inner_low, in_full))
    grad_upper = grad_upper + grad_from_third
    grad_cross_branch = grad_upper.astype(jnp.bfloat16)
    grad_crossed = split_heads(project_back(grad_cross_branch, attn_full[7]).astype(jnp.bfloat16))
    cross_query_grad, memory_key_grad, memory_value_grad, unused_table = attend_backward(
        cross_query, memory_keys, memory_values, cross_masks, rel_table, cross_logs, grad_crossed
    )
    cross_query_low = join_heads(cross_query_grad).astype(jnp.bfloat16)
    memory_key_low = join_heads(memory_key_grad).astype(jnp.bfloat16)
    memory_value_low = join_heads(memory_value_grad).astype(jnp.bfloat16)
    cross_grads = pair_grads(
        cube,
        [
            (second_low, cross_query_low),
            (memory, memory_key_low),
            (memory, memory_value_low),
            (crossed_low, grad_cross_branch),
        ],
        cube.plan_a,
    )
    grad_memory = project_back(memory_key_low, attn_full[5]) + project_back(
        memory_value_low, attn_full[6]
    )
    grad_from_second, grad_gain_second = norm_back_second(
        project_back(cross_query_low, attn_full[4])
    )
    grad_middle = grad_upper + grad_from_second
    grad_self_branch = grad_middle.astype(jnp.bfloat16)
    grad_mixed = split_heads(project_back(grad_self_branch, attn_full[3]).astype(jnp.bfloat16))
    query_grad, key_grad, value_grad, table_grad = attend_backward(
        query_heads, key_heads, value_heads, self_masks, rel_table, self_logs, grad_mixed
    )
    query_low = join_heads(query_grad).astype(jnp.bfloat16)
    key_low = join_heads(key_grad).astype(jnp.bfloat16)
    value_low = join_heads(value_grad).astype(jnp.bfloat16)
    late_grads = pair_grads(
        cube, [(first_low, value_low), (mixed_low, grad_self_branch)], cube.plan_b
    )
    self_grads = pair_grads(cube, [(first_low, query_low), (first_low, key_low)], cube.plan_a)
    grad_first = (
        project_back(query_low, attn_full[0])
        + project_back(key_low, attn_full[1])
        + project_back(value_low, attn_full[2])
    )
    grad_from_first, grad_gain_first = norm_back_first(grad_first)
    grad_tokens = grad_middle + grad_from_first
    gain_local = jnp.stack([grad_gain_first, grad_gain_second, grad_gain_third])
    grad_attn = jnp.concatenate([self_grads, late_grads, cross_grads], axis=0)
    square_attn = grad_attn * grad_attn
    square_in = grad_in * grad_in
    square_out = grad_out * grad_out
    row_means = jnp.concatenate(
        [jnp.mean(square_attn, axis=2), jnp.mean(square_in, axis=1)[None]], axis=0
    )
    new_row_main = DECAY * row_main + (1.0 - DECAY) * row_means
    new_row_out = DECAY * row_out + (1.0 - DECAY) * jnp.mean(square_out, axis=1)
    column_main = jnp.concatenate(
        [jnp.sum(square_attn, axis=1), jnp.sum(square_out, axis=0)[None]], axis=0
    )
    column_in = jnp.sum(square_in, axis=0)
    column_main, column_in, grad_table, gain_sums = lax.psum(
        (column_main, column_in, table_grad, gain_local), AXES
    )
    grad_gains = lax.dynamic_slice_in_dim(
        gain_sums, cube.me * norm_gains.shape[1], norm_gains.shape[1], 1
    )
    col_means = jnp.concatenate([column_main[:8] / D, column_main[8:] / FF], axis=0)
    new_col_main = DECAY * col_main + (1.0 - DECAY) * col_means
    new_col_in = DECAY * col_in + (1.0 - DECAY) * (column_in / D)
    return (
        layer_out,
        grad_tokens,
        grad_memory,
        grad_attn,
        grad_in,
        grad_out,
        grad_gains,
        grad_table,
        new_row_main,
        new_row_out,
        new_col_main,
        new_col_in,
    )


def solution(mesh):
    placed = (
        P(("wide", "narrow"), None),
        P(("wide", "narrow"), None),
        P(("wide", "narrow"), None),
        P(("wide", "narrow"), None),
        P(("wide", "narrow"), None),
        P(("wide", "narrow"), None),
        P(None, ("wide", "narrow"), None),
        P(("wide", "narrow"), None),
        P(("wide", "narrow"), None),
        P(None, ("wide", "narrow")),
        P(),
        P(None, ("wide", "narrow")),
        P(("wide", "narrow")),
        P(),
        P(),
    )
    return jax.shard_map(
        on_device,
        mesh=mesh,
        in_specs=placed,
        out_specs=(
            P(("wide", "narrow"), None),
            P(("wide", "narrow"), None),
            P(("wide", "narrow"), None),
            P(None, ("wide", "narrow"), None),
            P(("wide", "narrow"), None),
            P(("wide", "narrow"), None),
            P(None, ("wide", "narrow")),
            P(),
            P(None, ("wide", "narrow")),
            P(("wide", "narrow")),
            P(),
            P(),
        ),
        check_vma=False,
    )
```

```python
import functools
import math

import jax
import jax.numpy as jnp
from jax import lax
from jax.experimental import pallas as pl
from jax.experimental.pallas import tpu as pltpu
from jax.sharding import PartitionSpec as P

D = 768
HEADS = 12
HEAD = 64
FF = 3072
BUCKETS = 32
MAXDIST = 128


EPSILON = 1e-06
DECAY = 0.8
NEGATIVE = -1e30


def thresholds():
    exact_count = BUCKETS // 2
    limits = list(range(1, exact_count + 1))
    for bucket_level in range(exact_count + 1, BUCKETS):
        limits.append(
            int(
                math.ceil(
                    exact_count
                    * (MAXDIST / exact_count) ** ((bucket_level - exact_count) / exact_count)
                )
            )
        )
    return limits


def bucket_table(distance, number_type):
    level_count = jnp.zeros(distance.shape, jnp.int32)
    for threshold in thresholds():
        level_count = level_count + (distance >= threshold).astype(jnp.int32)
    return (level_count[..., None] == jnp.arange(BUCKETS, dtype=jnp.int32)).astype(number_type)


def rms_norm(hidden, gain_row):
    return (
        hidden * lax.rsqrt(jnp.mean(hidden * hidden, axis=-1, keepdims=True) + EPSILON) * gain_row
    )


def project(left_side, right_side):
    return jnp.dot(left_side, right_side, preferred_element_type=jnp.float32)


def project_back(gradient, right_side):
    return lax.dot_general(
        gradient, right_side, (((1,), (1,)), ((), ())), preferred_element_type=jnp.float32
    )


def weight_grad(left_side, gradient):
    return lax.dot_general(
        left_side, gradient, (((0,), (0,)), ((), ())), preferred_element_type=jnp.float32
    )


LANES = 128
GROUP = LANES // HEAD
CUT = 256
VMEM_BYTES = 56 * 1024 * 1024
COST = pl.CostEstimate(flops=1000, bytes_accessed=1000, transcendentals=0)

NT = (((1,), (1,)), ((), ()))
TN = (((0,), (0,)), ((), ()))


def dot(left, right, dims=(((1,), (0,)), ((), ()))):
    return lax.dot_general(left, right, dims, preferred_element_type=jnp.float32)


def spans(rows, causal):
    return [(at, at + CUT if causal else rows) for at in range(0, rows, CUT)]


def lane_mask(head):
    lanes = lax.broadcasted_iota(jnp.int32, (1, LANES), 1)
    return ((lanes // HEAD) == head).astype(jnp.float32)


def only_head(block, head, scale):
    return (block.astype(jnp.float32) * (lane_mask(head) * scale)).astype(jnp.bfloat16)


def near_bias(line_ref, head):
    line = jnp.broadcast_to(line_ref[0, head : head + 1], (LANES, 2 * LANES))
    return pltpu.roll(line, 0, 1, stride=1, stride_axis=0)


def add_bias(scores, bias, at):
    columns = []
    for first in range(0, CUT, LANES):
        rows = []
        for key in range(0, scores.shape[0], LANES):
            apart = at + first - key
            block = scores[key : key + LANES, first : first + LANES]
            if apart >= 2 * LANES:
                block = block + bias[:1, 2 * LANES - 1 :]
            elif apart >= 0:
                block = block + bias[:, apart : apart + LANES]
            rows.append(block)
        columns.append(jnp.concatenate(rows, axis=0))
    return jnp.concatenate(columns, axis=1)


def attend_kernel(causal, q_ref, k_ref, v_ref, mask_ref, line_ref, probs_ref, out_ref):
    rows = q_ref.shape[0]
    biases = [near_bias(line_ref, head) for head in range(GROUP)] if causal else None
    for at, depth in spans(rows, causal):
        keys, values = k_ref[:depth], v_ref[:depth]
        total = jnp.zeros((CUT, LANES), jnp.float32)
        for head in range(GROUP):
            query = only_head(q_ref[at : at + CUT], head, HEAD**-0.5)
            scores = dot(keys, query, NT)
            if causal:
                scores = add_bias(scores, biases[head], at)
            scores = scores + mask_ref[:depth, at : at + CUT]
            weights = jnp.exp(scores - jnp.max(scores, axis=0, keepdims=True))
            weights = weights * (1.0 / jnp.sum(weights, axis=0, keepdims=True))
            low = weights.astype(jnp.bfloat16)
            probs_ref[head, :depth, at : at + CUT] = low
            total = total + dot(low, values, TN) * lane_mask(head)
        out_ref[at : at + CUT] = total.astype(jnp.bfloat16)


def diagonal_sums(block):
    width = block.shape[1]
    slabs = [block[at : at + 8] for at in range(0, block.shape[0], 8)]
    total = slabs[0]
    for at, slab in enumerate(slabs[1:], 1):
        total = total + pltpu.roll(slab, width - 8 * at, 1)
    row = lax.broadcasted_iota(jnp.int32, total.shape, 0)
    for step in (1, 2, 4):
        total = jnp.where((row & step) != 0, pltpu.roll(total, width - step, 1), total)
    return jnp.sum(total, axis=0, keepdims=True)


def attend_back_kernel(causal, q_ref, k_ref, v_ref, g_ref, probs_ref, *rest):
    if causal:
        dq_ref, dk_ref, dv_ref, sums_ref, dk_sum, dv_sum = rest
    else:
        dq_ref, dk_ref, dv_ref, dk_sum, dv_sum = rest
    rows = q_ref.shape[0]
    dk_sum[...] = jnp.zeros_like(dk_sum)
    dv_sum[...] = jnp.zeros_like(dv_sum)
    near = [[], []]
    far = [[], []]
    for at, depth in spans(rows, causal):
        dq = jnp.zeros((CUT, LANES), jnp.float32)
        for head in range(GROUP):
            grad = only_head(g_ref[at : at + CUT], head, 1.0)
            query = only_head(q_ref[at : at + CUT], head, HEAD**-0.5)
            keys = only_head(k_ref[:depth], head, HEAD**-0.5)
            low = probs_ref[head, :depth, at : at + CUT]
            probs = low.astype(jnp.float32)
            scaled = probs * dot(v_ref[:depth], grad, NT)
            centre = jnp.sum(scaled, axis=0, keepdims=True)
            grad_scores = (scaled - probs * centre).astype(jnp.bfloat16)
            dv_sum[:depth] += dot(low, grad)
            dk_sum[:depth] += dot(grad_scores, query)
            dq = dq + dot(grad_scores, keys, TN)
            if causal:
                parts = grad_scores.astype(jnp.float32)
                for first in range(0, CUT, LANES):
                    own = at + first
                    column = parts[:, first : first + LANES]
                    if own:
                        before = column[own - LANES : own]
                    else:
                        before = jnp.zeros((LANES, LANES), jnp.float32)
                    near[head].append((column[own : own + LANES], before))
                    if own > LANES:
                        far[head].append(jnp.sum(column[: own - LANES], axis=0, keepdims=True))
        dq_ref[at : at + CUT] = dq.astype(jnp.bfloat16)
    dk_ref[...] = dk_sum[...].astype(jnp.bfloat16)
    dv_ref[...] = dv_sum[...].astype(jnp.bfloat16)
    if causal:
        lines = []
        for head in range(GROUP):
            own = sum(pair[0] for pair in near[head][1:]) + near[head][0][0]
            before = sum(pair[1] for pair in near[head][1:]) + near[head][0][1]
            lines.append(diagonal_sums(jnp.concatenate([own, before], axis=1)))
        for head in range(GROUP):
            line = sum(far[head][1:]) + far[head][0]
            lines.append(jnp.concatenate([line, jnp.zeros_like(line)], axis=1))
        lines.append(jnp.zeros((8 - len(lines), 2 * LANES), jnp.float32))
        sums_ref[0] = jnp.concatenate(lines, axis=0)


def head_spec(rows):
    return pl.BlockSpec((rows, LANES), lambda pair: (0, pair))


def probs_spec(rows):
    return pl.BlockSpec((GROUP, rows, rows), lambda pair: (pair, 0, 0))


def attend_forward(query, keys, values, mask, lines, causal):
    rows = query.shape[0]
    return pl.pallas_call(
        functools.partial(attend_kernel, causal),
        grid=(HEADS // GROUP,),
        in_specs=[head_spec(rows)] * 3
        + [
            pl.BlockSpec((rows, rows), lambda pair: (0, 0)),
            pl.BlockSpec((1, 8, 2 * LANES), lambda pair: (pair, 0, 0)),
        ],
        out_specs=[probs_spec(rows), head_spec(rows)],
        out_shape=[
            jax.ShapeDtypeStruct((HEADS, rows, rows), jnp.bfloat16),
            jax.ShapeDtypeStruct(query.shape, jnp.bfloat16),
        ],
        compiler_params=pltpu.CompilerParams(vmem_limit_bytes=VMEM_BYTES),
        cost_estimate=COST,
        name="attend",
    )(query, keys, values, mask, lines)


def attend_backward(query, keys, values, grad, probs, causal):
    rows = query.shape[0]
    out_specs = [head_spec(rows)] * 3
    out_shape = [jax.ShapeDtypeStruct(query.shape, jnp.bfloat16)] * 3
    if causal:
        out_specs.append(pl.BlockSpec((1, 8, 2 * LANES), lambda pair: (pair, 0, 0)))
        out_shape.append(jax.ShapeDtypeStruct((HEADS // GROUP, 8, 2 * LANES), jnp.float32))
    return pl.pallas_call(
        functools.partial(attend_back_kernel, causal),
        grid=(HEADS // GROUP,),
        in_specs=[head_spec(rows)] * 4 + [probs_spec(rows)],
        out_specs=out_specs,
        out_shape=out_shape,
        scratch_shapes=[pltpu.VMEM((rows, LANES), jnp.float32)] * 2,
        compiler_params=pltpu.CompilerParams(vmem_limit_bytes=VMEM_BYTES),
        cost_estimate=COST,
        name="attend_back",
    )(query, keys, values, grad, probs)


def self_mask(segment, key_valid):
    rows = segment.shape[0]
    index = jnp.arange(rows, dtype=jnp.int32)
    distance = index[None, :] - index[:, None]
    allowed = (
        (segment[:, None] == segment[None, :])
        & (distance >= 0)
        & ((key_valid[:, None] > 0) | (distance == 0))
    )
    return jnp.where(allowed, 0.0, NEGATIVE).astype(jnp.float32)


def cross_mask(segment, mem_segment):
    allowed = mem_segment[:, None] == segment[None, :]
    return jnp.where(allowed, 0.0, NEGATIVE).astype(jnp.float32)


def bias_lines(table):
    places = bucket_table(jnp.arange(2 * LANES, dtype=jnp.int32), jnp.float32)
    lines = jnp.einsum(
        "nb,bh->hn", places, table.astype(jnp.float32), precision=lax.Precision.HIGHEST
    )
    lines = lines.reshape(HEADS // GROUP, GROUP, 2 * LANES)
    return jnp.pad(lines, ((0, 0), (0, 8 - GROUP), (0, 0)))


def table_sums(sums):
    near = sums[:, :GROUP].reshape(HEADS, 2 * LANES)
    far = jnp.sum(sums[:, GROUP : 2 * GROUP], axis=-1).reshape(HEADS)
    places = bucket_table(jnp.arange(2 * LANES, dtype=jnp.int32), jnp.float32)
    grad = jnp.einsum("nb,hn->bh", places, near, precision=lax.Precision.HIGHEST)
    return grad.at[BUCKETS - 1].add(far)


GELU_SCALE = math.sqrt(2.0 / math.pi)
GELU_CUBE = 0.044715
BLOCK = 768
CUTS = FF // (2 * BLOCK)


def ffn_kernel(
    core_ref, third_ref, upper_ref, cot_ref, in_ref, other_in_ref, out_ref, other_out_ref,
    layer_ref, gthird_ref, gin_ref, other_gin_ref, gout_ref, other_gout_ref,
    total, third_turned, out_block, gout_block,
):
    step = pl.program_id(0)
    half = D // 2
    mine = pl.ds(pl.multiple_of(core_ref[0] * half, half), half)
    other = pl.ds(pl.multiple_of((1 - core_ref[0]) * half, half), half)

    @pl.when(step == 0)
    def _():
        total[...] = upper_ref[...]
        gthird_ref[...] = jnp.zeros_like(gthird_ref)
        third_turned[...] = third_ref[...].T

    out_block[:, mine] = out_ref[...]
    out_block[:, other] = other_out_ref[...]

    def block(weight_ref, grad_ref):
        inner = dot(third_ref[...], weight_ref[...])
        square = inner * inner
        slope = jnp.tanh(inner * (GELU_SCALE + (GELU_SCALE * GELU_CUBE) * square))
        half_up = 0.5 + 0.5 * slope
        active = (inner * half_up).astype(jnp.bfloat16)
        total[...] += dot(active, out_block[...])
        grad_active = dot(cot_ref[...], out_block[...], NT)
        bend = (0.5 * inner) * (1.0 - slope * slope)
        bend = bend * (GELU_SCALE + (3.0 * GELU_SCALE * GELU_CUBE) * square)
        grad_inner = (grad_active * (half_up + bend)).astype(jnp.bfloat16)
        gthird_ref[...] += dot(grad_inner, weight_ref[...], NT)
        grad_ref[...] = dot(third_turned[...], grad_inner).astype(jnp.bfloat16)
        gout_block[...] = dot(active, cot_ref[...], TN).astype(jnp.bfloat16)

    @pl.when(step < CUTS)
    def _():
        block(other_in_ref, other_gin_ref)

    @pl.when(step >= CUTS)
    def _():
        block(in_ref, gin_ref)

    gout_ref[...] = gout_block[:, mine]
    other_gout_ref[...] = gout_block[:, other]

    @pl.when(step == 2 * CUTS - 1)
    def _():
        layer_ref[...] = total[...].astype(jnp.bfloat16)


def ffn(core, third, upper, cotangent, w_in, other_in, w_out, other_out):
    rows = third.shape[0]
    half = D // 2

    def place(step, core_ref):
        return ((1 - core_ref[0]) * CUTS + step) % (2 * CUTS)

    whole = pl.BlockSpec((rows, D), lambda step, core_ref: (0, 0))
    late = pl.BlockSpec((D, BLOCK), lambda step, core_ref: (0, jnp.maximum(step - CUTS, 0)))
    early = pl.BlockSpec((D, BLOCK), lambda step, core_ref: (0, jnp.minimum(step, CUTS - 1)))
    lines = pl.BlockSpec((BLOCK, half), lambda step, core_ref: (place(step, core_ref), 0))
    return pl.pallas_call(
        ffn_kernel,
        grid_spec=pltpu.PrefetchScalarGridSpec(
            num_scalar_prefetch=1,
            grid=(2 * CUTS,),
            in_specs=[whole, whole, whole, late, early, lines, lines],
            out_specs=[whole, whole, late, early, lines, lines],
            scratch_shapes=[
                pltpu.VMEM((rows, D), jnp.float32),
                pltpu.VMEM((D, rows), jnp.bfloat16),
                pltpu.VMEM((BLOCK, D), jnp.bfloat16),
                pltpu.VMEM((BLOCK, D), jnp.bfloat16),
            ],
        ),
        out_shape=[
            jax.ShapeDtypeStruct((rows, D), jnp.bfloat16),
            jax.ShapeDtypeStruct((rows, D), jnp.float32),
            jax.ShapeDtypeStruct((D, FF // 2), jnp.bfloat16),
            jax.ShapeDtypeStruct((D, FF // 2), jnp.bfloat16),
            jax.ShapeDtypeStruct((FF, half), jnp.bfloat16),
            jax.ShapeDtypeStruct((FF, half), jnp.bfloat16),
        ],
        compiler_params=pltpu.CompilerParams(vmem_limit_bytes=VMEM_BYTES),
        cost_estimate=COST,
        name="ffn",
    )(core[None], third, upper, cotangent, w_in, other_in, w_out, other_out)


AXES = ("wide", "narrow")


def after(value, *others):
    return lax.optimization_barrier((value,) + others)[0]


class Cube:
    def __init__(self):
        self.count = lax.axis_size("wide") * lax.axis_size("narrow")
        self.bits = self.count.bit_length() - 1
        self.me = lax.axis_index("wide") * lax.axis_size("narrow") + lax.axis_index("narrow")
        high = list(range(self.bits - 1, 1, -1))
        self.plan_a = high + [1]
        self.plan_b = [1] + high

    def bit(self, which):
        return (self.me >> which) & 1

    def swap(self, value, flip):
        return lax.ppermute(value, AXES, [(i, i ^ flip) for i in range(self.count)])

    def place(self, mine, theirs, which, axis, joined):
        join = jnp.concatenate if joined else jnp.stack
        return jnp.where(
            self.bit(which) == 0, join([mine, theirs], axis), join([theirs, mine], axis)
        )

    def send_step(self, value, plan, step):
        return self.swap(value, 1 << plan[step])

    def place_step(self, value, theirs, plan, step):
        axis = sum(other > plan[step] for other in plan[:step])
        return self.place(value, theirs, plan[step], axis, False)

    def half(self, value, whose):
        size = value.shape[-1] // 2
        return lax.dynamic_slice_in_dim(value, whose * size, size, value.ndim - 1)

    def total(self, value):
        for low in [0] + list(range(1, self.bits, 2)):
            top = 1 if low == 0 else min(2, self.bits - low)
            flips = [flip << low for flip in range(1, 1 << top)]
            value = value + sum(self.swap(value, flip) for flip in flips)
        return value


class Gather:
    def __init__(self, cube, value, plan):
        self.cube, self.value, self.plan, self.steps = cube, value, plan, 0

    def send(self, *behind):
        self.value = after(self.value, *behind)
        self.theirs = self.cube.send_step(self.value, self.plan, self.steps)

    def take(self, *behind):
        value = after(self.value, *behind) if behind else self.value
        self.value = self.cube.place_step(value, self.theirs, self.plan, self.steps)
        self.steps += 1
        return self.value


def pair_weights(cube, w_in, w_out):
    rows = w_in.shape[0]
    core = cube.bit(0)
    count = FF // D
    in_rows = jnp.stack([w_in[:, k * D // 2 : (k + 1) * D // 2] for k in range(2 * count)])

    def packed(whose):
        in_half = lax.dynamic_slice_in_dim(in_rows, whose * count, count, 0)
        return [in_half, cube.half(w_out, whose)]

    mine = packed(core)
    sent = [part.reshape(-1, D // 2) for part in packed(1 - core)]
    other = cube.swap(jnp.concatenate(sent, axis=0), 1)
    size = count * rows
    theirs = [other[:size].reshape(mine[0].shape), other[size:]]
    in_pair, out_pair = [
        cube.place(ours, others, 0, ours.ndim - 2, True) for ours, others in zip(mine, theirs)
    ]
    return jnp.concatenate([in_pair[k] for k in range(count)], axis=1), out_pair


def both_halves(cube, value):
    value = value.reshape((-1,) + value.shape[-2:])
    return value, cube.swap(value, 1)


def whole_weights(cube, parts, first, count):
    rows = D // cube.count
    full = cube.place(parts[0], parts[1], 0, 1, False)
    return [
        full[:, :, first + k * rows : first + (k + 1) * rows].reshape(D, D) for k in range(count)
    ]


class Sums:
    def __init__(self, cube, plan, sent, kept):
        self.cube, self.plan, self.steps = cube, plan, 0
        self.kept, self.theirs = kept, cube.swap(sent, 1)

    def take(self, *behind):
        kept = after(self.kept, *behind) if behind else self.kept
        value = kept.astype(jnp.float32) + self.theirs.astype(jnp.float32)
        if self.steps == 0:
            shape = (value.shape[0],) + (2,) * len(self.plan) + (-1, value.shape[-1])
            value = value.reshape(shape)
        self.value = value

    def send(self, *behind):
        which = self.plan[-1 - self.steps]
        axis = 1 + sum(other > which for other in self.plan[: len(self.plan) - self.steps])
        mine = self.cube.bit(which)
        sent = lax.dynamic_index_in_dim(self.value, 1 - mine, axis, False).astype(jnp.bfloat16)
        sent = after(sent, *behind)
        self.kept = lax.dynamic_index_in_dim(self.value, mine, axis, False)
        self.theirs = self.cube.swap(sent, 1 << which)
        self.steps += 1
        return sent

    def going(self):
        return self.steps < len(self.plan)


def product_sums(cube, plan, pairs):
    grads = jnp.stack([weight_grad(left, right).astype(jnp.bfloat16) for left, right in pairs])
    grads = grads.reshape(len(pairs), cube.count // 2, 2, -1, D)
    core = cube.bit(0)
    sent = lax.dynamic_index_in_dim(grads, 1 - core, 2, False)
    kept = lax.dynamic_index_in_dim(grads, core, 2, False)
    return Sums(cube, plan, sent, kept)


def half_swap(cube, value):
    value = value.reshape(2, -1, value.shape[-1])
    core = cube.bit(0)
    mine = lax.dynamic_index_in_dim(value, core, 0, False)
    return mine, cube.swap(lax.dynamic_index_in_dim(value, 1 - core, 0, False), 1)


def on_device(
    tokens,
    memory,
    cotangent,
    dec_segments,
    enc_segments,
    dec_valid,
    attn_weights,
    w_in,
    w_out,
    norm_gains,
    rel_table,
    row_main,
    row_out,
    col_main,
    col_in,
):
    cube = Cube()
    core = cube.bit(0)
    rows = attn_weights.shape[1]
    gain_rows = jnp.pad(norm_gains, ((0, 5), (0, D - norm_gains.shape[1])))
    one = Gather(
        cube,
        jnp.concatenate([attn_weights[:2].reshape(-1, D), gain_rows], axis=0),
        cube.plan_a,
    )
    two = Gather(cube, attn_weights[2:4].reshape(-1, D), cube.plan_b)
    one.send()
    two.send()
    in_pair, out_pair = pair_weights(cube, w_in, w_out)
    three = Gather(cube, attn_weights[4:].reshape(-1, D), cube.plan_a)
    inner_half = Gather(cube, in_pair, cube.plan_b)
    outer_half = Gather(cube, out_pair, cube.plan_a)
    last = len(cube.plan_a) - 1
    for step in range(last):
        one.take()
        two.take()
        one.send()
        two.send()
        if step > 0:
            three.take()
        three.send(one.value, two.value)
        if step > 1:
            inner_half.take()
            outer_half.take()
        if step > 0:
            inner_half.send(three.value)
            outer_half.send(three.value)
    one.take()
    two.take()
    first_halves = both_halves(cube, one.value)
    second_halves = both_halves(cube, two.value)
    three.take()
    three.send(one.value, two.value)
    inner_half.take()
    outer_half.take()
    inner_half.send(three.value)
    outer_half.send(three.value)
    attn_full = whole_weights(cube, first_halves, 0, 2)
    attn_full = attn_full + whole_weights(cube, second_halves, 0, 2)
    gain_full = cube.place(
        first_halves[0][:, 2 * rows :], first_halves[1][:, 2 * rows :], 0, 1, False
    )[:, :, :3, : norm_gains.shape[1]]
    gain_full = gain_full.transpose(2, 0, 1, 3).reshape(3, D)
    segment = dec_segments[0]
    see_self = self_mask(segment, dec_valid[0])
    see_cross = cross_mask(segment, enc_segments[0])
    lines = bias_lines(rel_table)

    residual = tokens.astype(jnp.float32)
    normed_first, norm_back_first = jax.vjp(rms_norm, residual, gain_full[0].astype(jnp.float32))
    first_low = normed_first.astype(jnp.bfloat16)
    query = project(first_low, attn_full[0]).astype(jnp.bfloat16)
    keys = project(first_low, attn_full[1]).astype(jnp.bfloat16)
    values = project(first_low, attn_full[2]).astype(jnp.bfloat16)
    inner_half.take(query, keys, values)
    outer_half.take(query, keys, values)
    query = after(query, inner_half.value, outer_half.value)
    inner_half.send()
    outer_half.send()
    self_probs, mixed_low = attend_forward(query, keys, values, see_self, lines, True)
    three.take(mixed_low)
    attn_full = attn_full + whole_weights(cube, both_halves(cube, three.value), 0, 4)
    middle = residual + project(mixed_low, attn_full[3])
    normed_second, norm_back_second = jax.vjp(rms_norm, middle, gain_full[1].astype(jnp.float32))
    second_low = normed_second.astype(jnp.bfloat16)
    cross_query = project(second_low, attn_full[4]).astype(jnp.bfloat16)
    memory_keys = project(memory, attn_full[5]).astype(jnp.bfloat16)
    memory_values = project(memory, attn_full[6]).astype(jnp.bfloat16)
    inner_half.take(cross_query)
    outer_half.take(cross_query)
    cross_query = after(cross_query, inner_half.value, outer_half.value)
    own_in, other_in = both_halves(cube, inner_half.value)
    own_out, other_out = both_halves(cube, outer_half.value)
    cross_probs, crossed_low = attend_forward(
        cross_query, memory_keys, memory_values, see_cross, lines, False
    )
    upper = middle + project(crossed_low, attn_full[7])
    normed_third, norm_back_third = jax.vjp(rms_norm, upper, gain_full[2].astype(jnp.float32))
    third_low = normed_third.astype(jnp.bfloat16)
    layer_out, grad_third, grad_in, other_grad_in, grad_out, other_grad_out = ffn(
        core,
        third_low,
        upper,
        cotangent,
        own_in.reshape(D, -1),
        other_in.reshape(D, -1),
        own_out.reshape(FF, -1),
        other_out.reshape(FF, -1),
    )
    in_sums = Sums(cube, cube.plan_b, other_grad_in[None], grad_in[None])
    out_sums = Sums(cube, cube.plan_a, other_grad_out[None], grad_out[None])
    grad_from_third, grad_gain_third = norm_back_third(grad_third)
    grad_upper = cotangent.astype(jnp.float32) + grad_from_third
    grad_cross_branch = grad_upper.astype(jnp.bfloat16)
    grad_crossed = project_back(grad_cross_branch, attn_full[7]).astype(jnp.bfloat16)
    in_sums.take(grad_crossed)
    out_sums.take(grad_crossed)
    grad_crossed = after(grad_crossed, in_sums.send(), out_sums.send())
    cross_query_low, memory_key_low, memory_value_low = attend_backward(
        cross_query, memory_keys, memory_values, grad_crossed, cross_probs, False
    )
    cross_sums = product_sums(
        cube,
        cube.plan_a,
        [
            (second_low, cross_query_low),
            (memory, memory_key_low),
            (memory, memory_value_low),
            (crossed_low, grad_cross_branch),
        ],
    )
    grad_from_second, grad_gain_second = norm_back_second(
        project_back(cross_query_low, attn_full[4])
    )
    grad_middle = grad_upper + grad_from_second
    grad_self_branch = grad_middle.astype(jnp.bfloat16)
    grad_mixed = project_back(grad_self_branch, attn_full[3]).astype(jnp.bfloat16)
    sums = [cross_sums, in_sums, out_sums]
    for each in sums:
        each.take(grad_mixed)
    grad_mixed = after(grad_mixed, *[each.send() for each in sums])
    query_low, key_low, value_low, score_sums = attend_backward(
        query, keys, values, grad_mixed, self_probs, True
    )
    for each in sums[1:]:
        each.take(query_low)
    query_low, key_low, value_low = lax.optimization_barrier(
        (query_low, key_low, value_low) + tuple(each.send() for each in sums[1:])
    )[:3]
    late_sums = product_sums(
        cube, cube.plan_b, [(first_low, value_low), (mixed_low, grad_self_branch)]
    )
    early_sums = product_sums(cube, cube.plan_a, [(first_low, query_low), (first_low, key_low)])
    memory_key_low, memory_value_low = lax.optimization_barrier(
        (memory_key_low, memory_value_low, late_sums.kept, early_sums.kept)
    )[:2]
    grad_memory = project_back(memory_key_low, attn_full[5]) + project_back(
        memory_value_low, attn_full[6]
    )
    sums = [late_sums, early_sums, cross_sums, in_sums, out_sums]
    for each in sums:
        each.take(grad_memory)
    started = [each.send() for each in sums if each.going()]
    query_low, key_low, value_low = lax.optimization_barrier(
        (query_low, key_low, value_low, *started)
    )[:3]
    grad_first = (
        project_back(query_low, attn_full[0])
        + project_back(key_low, attn_full[1])
        + project_back(value_low, attn_full[2])
    )
    grad_from_first, grad_gain_first = norm_back_first(grad_first)
    grad_tokens = grad_middle + grad_from_first
    table_grad = table_sums(score_sums)
    gain_local = jnp.stack([grad_gain_first, grad_gain_second, grad_gain_third])
    behind = (grad_tokens,)
    while any(each.going() for each in sums):
        moving = [each for each in sums if each.going()]
        for each in moving:
            each.take(*behind)
            each.send()
        behind = ()
    for each in sums:
        each.take(*behind)
    grad_in, grad_out = [
        cube.place(*half_swap(cube, each.value), 0, 1, True) for each in sums[3:]
    ]
    grad_attn = jnp.concatenate(
        [each.value.reshape(-1, rows, D) for each in (early_sums, late_sums, cross_sums)], axis=0
    )
    square_attn = grad_attn * grad_attn
    square_in = grad_in * grad_in
    square_out = grad_out * grad_out
    row_means = jnp.concatenate(
        [jnp.mean(square_attn, axis=2), jnp.mean(square_in, axis=1)[None]], axis=0
    )
    new_row_main = DECAY * row_main + (1.0 - DECAY) * row_means
    new_row_out = DECAY * row_out + (1.0 - DECAY) * jnp.mean(square_out, axis=1)
    column_main = jnp.concatenate(
        [jnp.sum(square_attn, axis=1), jnp.sum(square_out, axis=0)[None]], axis=0
    )
    column_in = jnp.sum(square_in, axis=0)
    parts = [column_main, column_in, table_grad, gain_local]
    sizes = [part.size for part in parts]
    width = D // 2
    lines = -(-sum(sizes) // (8 * width)) * 8
    flat = jnp.concatenate([part.reshape(-1, width) for part in parts], axis=0)
    flat = cube.total(jnp.pad(flat, ((0, lines - flat.shape[0]), (0, 0))))
    sums, at = [], 0
    for part, size in zip(parts, sizes):
        sums.append(flat[at : at + size // width].reshape(part.shape))
        at += size // width
    column_main, column_in, grad_table, gain_sums = sums
    grad_gains = lax.dynamic_slice_in_dim(
        gain_sums, cube.me * norm_gains.shape[1], norm_gains.shape[1], 1
    )
    col_means = jnp.concatenate([column_main[:8] / D, column_main[8:] / FF], axis=0)
    new_col_main = DECAY * col_main + (1.0 - DECAY) * col_means
    new_col_in = DECAY * col_in + (1.0 - DECAY) * (column_in / D)
    return (
        layer_out,
        grad_tokens,
        grad_memory,
        grad_attn,
        grad_in,
        grad_out,
        grad_gains,
        grad_table,
        new_row_main,
        new_row_out,
        new_col_main,
        new_col_in,
    )


def solution(mesh):
    placed = (
        P(("wide", "narrow"), None),
        P(("wide", "narrow"), None),
        P(("wide", "narrow"), None),
        P(("wide", "narrow"), None),
        P(("wide", "narrow"), None),
        P(("wide", "narrow"), None),
        P(None, ("wide", "narrow"), None),
        P(("wide", "narrow"), None),
        P(("wide", "narrow"), None),
        P(None, ("wide", "narrow")),
        P(),
        P(None, ("wide", "narrow")),
        P(("wide", "narrow")),
        P(),
        P(),
    )
    return jax.shard_map(
        on_device,
        mesh=mesh,
        in_specs=placed,
        out_specs=(
            P(("wide", "narrow"), None),
            P(("wide", "narrow"), None),
            P(("wide", "narrow"), None),
            P(None, ("wide", "narrow"), None),
            P(("wide", "narrow"), None),
            P(("wide", "narrow"), None),
            P(None, ("wide", "narrow")),
            P(),
            P(None, ("wide", "narrow")),
            P(("wide", "narrow")),
            P(),
            P(),
        ),
        check_vma=False,
    )
```

```python
import functools
import math

import jax
import jax.numpy as jnp
from jax import lax
from jax.experimental import pallas as pl
from jax.experimental.pallas import tpu as pltpu
from jax.sharding import PartitionSpec as P

D = 768
HEADS = 12
HEAD = 64
FF = 3072
BUCKETS = 32
MAXDIST = 128


EPSILON = 1e-06
DECAY = 0.8
NEGATIVE = -1e30


def thresholds():
    exact_count = BUCKETS // 2
    limits = list(range(1, exact_count + 1))
    for bucket_level in range(exact_count + 1, BUCKETS):
        limits.append(
            int(
                math.ceil(
                    exact_count
                    * (MAXDIST / exact_count) ** ((bucket_level - exact_count) / exact_count)
                )
            )
        )
    return limits


def bucket_table(distance, number_type):
    level_count = jnp.zeros(distance.shape, jnp.int32)
    for threshold in thresholds():
        level_count = level_count + (distance >= threshold).astype(jnp.int32)
    return (level_count[..., None] == jnp.arange(BUCKETS, dtype=jnp.int32)).astype(number_type)


def weight_grad(left_side, gradient):
    return lax.dot_general(
        left_side, gradient, (((0,), (0,)), ((), ())), preferred_element_type=jnp.float32
    )


LANES = 128
GROUP = LANES // HEAD
CUT = 256
VMEM_BYTES = 56 * 1024 * 1024

NT = (((1,), (1,)), ((), ()))
TN = (((0,), (0,)), ((), ()))


def dot(left, right, dims=(((1,), (0,)), ((), ()))):
    return lax.dot_general(left, right, dims, preferred_element_type=jnp.float32)


def spans(rows, causal):
    return [(at, at + CUT if causal else rows) for at in range(0, rows, CUT)]


def lane_mask(head):
    lanes = lax.broadcasted_iota(jnp.int32, (1, LANES), 1)
    return ((lanes // HEAD) == head).astype(jnp.float32)


def only_head(block, head, scale):
    return (block.astype(jnp.float32) * (lane_mask(head) * scale)).astype(jnp.bfloat16)


def near_bias(line_ref, head):
    line = jnp.broadcast_to(line_ref[0, head : head + 1], (LANES, 2 * LANES))
    return pltpu.roll(line, 0, 1, stride=1, stride_axis=0)


def add_bias(scores, bias, at):
    columns = []
    for first in range(0, CUT, LANES):
        rows = []
        for key in range(0, scores.shape[0], LANES):
            apart = at + first - key
            block = scores[key : key + LANES, first : first + LANES]
            if apart >= 2 * LANES:
                block = block + bias[:1, 2 * LANES - 1 :]
            elif apart >= 0:
                block = block + bias[:, apart : apart + LANES]
            rows.append(block)
        columns.append(jnp.concatenate(rows, axis=0))
    return jnp.concatenate(columns, axis=1)


def attend_pair(causal, pair, q_ref, k_ref, v_ref, mask_ref, line_ref, probs_ref, out_ref):
    rows = q_ref.shape[0]
    lanes = pl.ds(pl.multiple_of(pair * LANES, LANES), LANES)
    biases = [near_bias(line_ref, head) for head in range(GROUP)] if causal else None
    for at, depth in spans(rows, causal):
        keys, values = k_ref[:depth, lanes], v_ref[:depth, lanes]
        total = jnp.zeros((CUT, LANES), jnp.float32)
        for head in range(GROUP):
            query = only_head(q_ref[at : at + CUT, lanes], head, HEAD**-0.5)
            scores = dot(keys, query, NT)
            if causal:
                scores = add_bias(scores, biases[head], at)
            scores = scores + mask_ref[:depth, at : at + CUT]
            weights = jnp.exp(scores - jnp.max(scores, axis=0, keepdims=True))
            weights = weights * (1.0 / jnp.sum(weights, axis=0, keepdims=True))
            low = weights.astype(jnp.bfloat16)
            probs_ref[head, :depth, at : at + CUT] = low
            total = total + dot(low, values, TN) * lane_mask(head)
        out_ref[at : at + CUT, lanes] = total.astype(jnp.bfloat16)


def diagonal_sums(block):
    width = block.shape[1]
    slabs = [block[at : at + 8] for at in range(0, block.shape[0], 8)]
    total = slabs[0]
    for at, slab in enumerate(slabs[1:], 1):
        total = total + pltpu.roll(slab, width - 8 * at, 1)
    row = lax.broadcasted_iota(jnp.int32, total.shape, 0)
    for step in (1, 2, 4):
        total = jnp.where((row & step) != 0, pltpu.roll(total, width - step, 1), total)
    return jnp.sum(total, axis=0, keepdims=True)


def attend_back_pair(
    causal, pair, q_ref, k_ref, v_ref, g_ref, probs_ref, dq_ref, dk_ref, dv_ref, sums_ref,
    dk_sum, dv_sum,
):
    rows = q_ref.shape[0]
    lanes = pl.ds(pl.multiple_of(pair * LANES, LANES), LANES)
    dk_sum[...] = jnp.zeros_like(dk_sum)
    dv_sum[...] = jnp.zeros_like(dv_sum)
    near = [[], []]
    far = [[], []]
    for at, depth in spans(rows, causal):
        dq = jnp.zeros((CUT, LANES), jnp.float32)
        for head in range(GROUP):
            grad = only_head(g_ref[at : at + CUT, lanes], head, 1.0)
            query = only_head(q_ref[at : at + CUT, lanes], head, HEAD**-0.5)
            keys = only_head(k_ref[:depth, lanes], head, HEAD**-0.5)
            low = probs_ref[head, :depth, at : at + CUT]
            probs = low.astype(jnp.float32)
            scaled = probs * dot(v_ref[:depth, lanes], grad, NT)
            centre = jnp.sum(scaled, axis=0, keepdims=True)
            grad_scores = (scaled - probs * centre).astype(jnp.bfloat16)
            dv_sum[:depth] += dot(low, grad)
            dk_sum[:depth] += dot(grad_scores, query)
            dq = dq + dot(grad_scores, keys, TN)
            if causal:
                parts = grad_scores.astype(jnp.float32)
                for first in range(0, CUT, LANES):
                    own = at + first
                    column = parts[:, first : first + LANES]
                    if own:
                        before = column[own - LANES : own]
                    else:
                        before = jnp.zeros((LANES, LANES), jnp.float32)
                    near[head].append((column[own : own + LANES], before))
                    if own > LANES:
                        far[head].append(jnp.sum(column[: own - LANES], axis=0, keepdims=True))
        dq_ref[at : at + CUT, lanes] = dq.astype(jnp.bfloat16)
    dk_ref[:, lanes] = dk_sum[...].astype(jnp.bfloat16)
    dv_ref[:, lanes] = dv_sum[...].astype(jnp.bfloat16)
    if causal:
        lines = []
        for head in range(GROUP):
            own = sum(pair[0] for pair in near[head][1:]) + near[head][0][0]
            before = sum(pair[1] for pair in near[head][1:]) + near[head][0][1]
            lines.append(diagonal_sums(jnp.concatenate([own, before], axis=1)))
        for head in range(GROUP):
            line = sum(far[head][1:]) + far[head][0]
            lines.append(jnp.concatenate([line, jnp.zeros_like(line)], axis=1))
        lines.append(jnp.zeros((8 - len(lines), 2 * LANES), jnp.float32))
        sums_ref[0] = jnp.concatenate(lines, axis=0)


def self_mask(segment, key_valid):
    rows = segment.shape[0]
    index = jnp.arange(rows, dtype=jnp.int32)
    distance = index[None, :] - index[:, None]
    allowed = (
        (segment[:, None] == segment[None, :])
        & (distance >= 0)
        & ((key_valid[:, None] > 0) | (distance == 0))
    )
    return jnp.where(allowed, 0.0, NEGATIVE).astype(jnp.float32)


def cross_mask(segment, mem_segment):
    allowed = mem_segment[:, None] == segment[None, :]
    return jnp.where(allowed, 0.0, NEGATIVE).astype(jnp.float32)


def bias_lines(table):
    places = bucket_table(jnp.arange(2 * LANES, dtype=jnp.int32), jnp.float32)
    lines = jnp.einsum(
        "nb,bh->hn", places, table.astype(jnp.float32), precision=lax.Precision.HIGHEST
    )
    lines = lines.reshape(HEADS // GROUP, GROUP, 2 * LANES)
    return jnp.pad(lines, ((0, 0), (0, 8 - GROUP), (0, 0)))


def table_sums(sums):
    near = sums[:, :GROUP].reshape(HEADS, 2 * LANES)
    far = jnp.sum(sums[:, GROUP : 2 * GROUP], axis=-1).reshape(HEADS)
    places = bucket_table(jnp.arange(2 * LANES, dtype=jnp.int32), jnp.float32)
    grad = jnp.einsum("nb,hn->bh", places, near, precision=lax.Precision.HIGHEST)
    return grad.at[BUCKETS - 1].add(far)


GELU_SCALE = math.sqrt(2.0 / math.pi)
GELU_CUBE = 0.044715
BLOCK = 768
CUTS = FF // (2 * BLOCK)


def ffn_kernel(
    core_ref, third_ref, upper_ref, cot_ref, in_ref, other_in_ref, out_ref, other_out_ref,
    layer_ref, gthird_ref, gin_ref, other_gin_ref, gout_ref, other_gout_ref,
    total, third_turned, out_block, gout_block,
):
    step = pl.program_id(0)
    half = D // 2
    mine = pl.ds(pl.multiple_of(core_ref[0] * half, half), half)
    other = pl.ds(pl.multiple_of((1 - core_ref[0]) * half, half), half)

    @pl.when(step == 0)
    def _():
        total[...] = upper_ref[...]
        gthird_ref[...] = jnp.zeros_like(gthird_ref)
        third_turned[...] = third_ref[...].T

    out_block[:, mine] = out_ref[...]
    out_block[:, other] = other_out_ref[...]

    def block(weight_ref, grad_ref):
        inner = dot(third_ref[...], weight_ref[...])
        square = inner * inner
        slope = jnp.tanh(inner * (GELU_SCALE + (GELU_SCALE * GELU_CUBE) * square))
        half_up = 0.5 + 0.5 * slope
        active = (inner * half_up).astype(jnp.bfloat16)
        total[...] += dot(active, out_block[...])
        grad_active = dot(cot_ref[...], out_block[...], NT)
        bend = (0.5 * inner) * (1.0 - slope * slope)
        bend = bend * (GELU_SCALE + (3.0 * GELU_SCALE * GELU_CUBE) * square)
        grad_inner = (grad_active * (half_up + bend)).astype(jnp.bfloat16)
        gthird_ref[...] += dot(grad_inner, weight_ref[...], NT)
        grad_ref[...] = dot(third_turned[...], grad_inner).astype(jnp.bfloat16)
        gout_block[...] = dot(active, cot_ref[...], TN).astype(jnp.bfloat16)

    @pl.when(step < CUTS)
    def _():
        block(other_in_ref, other_gin_ref)

    @pl.when(step >= CUTS)
    def _():
        block(in_ref, gin_ref)

    gout_ref[...] = gout_block[:, mine]
    other_gout_ref[...] = gout_block[:, other]

    @pl.when(step == 2 * CUTS - 1)
    def _():
        layer_ref[...] = total[...].astype(jnp.bfloat16)


def ffn(core, third, upper, cotangent, w_in, other_in, w_out, other_out):
    rows = third.shape[0]
    half = D // 2

    def place(step, core_ref):
        return ((1 - core_ref[0]) * CUTS + step) % (2 * CUTS)

    whole = pl.BlockSpec((rows, D), lambda step, core_ref: (0, 0))
    late = pl.BlockSpec((D, BLOCK), lambda step, core_ref: (0, jnp.maximum(step - CUTS, 0)))
    early = pl.BlockSpec((D, BLOCK), lambda step, core_ref: (0, jnp.minimum(step, CUTS - 1)))
    lines = pl.BlockSpec((BLOCK, half), lambda step, core_ref: (place(step, core_ref), 0))
    return pl.pallas_call(
        ffn_kernel,
        grid_spec=pltpu.PrefetchScalarGridSpec(
            num_scalar_prefetch=1,
            grid=(2 * CUTS,),
            in_specs=[whole, whole, whole, late, early, lines, lines],
            out_specs=[whole, whole, late, early, lines, lines],
            scratch_shapes=[
                pltpu.VMEM((rows, D), jnp.float32),
                pltpu.VMEM((D, rows), jnp.bfloat16),
                pltpu.VMEM((BLOCK, D), jnp.bfloat16),
                pltpu.VMEM((BLOCK, D), jnp.bfloat16),
            ],
        ),
        out_shape=[
            jax.ShapeDtypeStruct((rows, D), jnp.bfloat16),
            jax.ShapeDtypeStruct((rows, D), jnp.float32),
            jax.ShapeDtypeStruct((D, FF // 2), jnp.bfloat16),
            jax.ShapeDtypeStruct((D, FF // 2), jnp.bfloat16),
            jax.ShapeDtypeStruct((FF, half), jnp.bfloat16),
            jax.ShapeDtypeStruct((FF, half), jnp.bfloat16),
        ],
        compiler_params=pltpu.CompilerParams(vmem_limit_bytes=VMEM_BYTES),

        name="ffn",
    )(core[None], third, upper, cotangent, w_in, other_in, w_out, other_out)


def scale_of(hidden):
    return lax.rsqrt(jnp.mean(hidden * hidden, axis=-1, keepdims=True) + EPSILON)


def norm_back(hidden, gain, grad):
    scale = scale_of(hidden)
    grown = grad * gain
    inner = jnp.mean(grown * hidden, axis=-1, keepdims=True)
    gain_grad = jnp.sum(grad * (hidden * scale), axis=0, keepdims=True)
    return scale * grown - hidden * (scale * scale * scale * inner), gain_grad


def fused(kernel, outs, *args):
    space = pl.BlockSpec(memory_space=pltpu.VMEM)
    return pl.pallas_call(
        kernel,
        in_specs=[space] * len(args),
        out_specs=[space] * len(outs),
        out_shape=[jax.ShapeDtypeStruct(shape, held_as) for shape, held_as in outs],
        compiler_params=pltpu.CompilerParams(vmem_limit_bytes=VMEM_BYTES),

        name=kernel.__name__,
    )(*args)


PAIRS = HEADS // GROUP


def whole_spec(array, space=None):
    rank = len(array.shape)
    return pl.BlockSpec(array.shape, lambda pair: (0,) * rank, pipeline_mode=space)


def by_pair(kernel, args, outs, scratch, by_step, name):
    held = [jax.ShapeDtypeStruct(shape, held_as) for shape, held_as in outs]

    def spec(array, once):
        if len(array.shape) == 3 and array.shape in by_step:
            block = (array.shape[0] // PAIRS,) + array.shape[1:]
            return pl.BlockSpec(block, lambda pair: (pair, 0, 0))
        if array.shape == (1,):
            return pl.BlockSpec(memory_space=pltpu.SMEM)
        return whole_spec(array, pl.Buffered(1) if once else None)

    return pl.pallas_call(
        kernel,
        grid=(PAIRS,),
        in_specs=[spec(array, True) for array in args],
        out_specs=[spec(array, False) for array in held],
        out_shape=held,
        scratch_shapes=scratch,
        compiler_params=pltpu.CompilerParams(vmem_limit_bytes=VMEM_BYTES),
        name=name,
    )(*args)


def self_part(
    tokens_ref, gain_ref, wq_ref, wk_ref, wv_ref, mask_ref, line_ref,
    first_ref, q_ref, k_ref, v_ref, probs_ref, mixed_ref,
):
    pair = pl.program_id(0)

    @pl.when(pair == 0)
    def _():
        hidden = tokens_ref[...].astype(jnp.float32)
        first = (hidden * scale_of(hidden) * gain_ref[...]).astype(jnp.bfloat16)
        first_ref[...] = first
        for weight, result in ((wq_ref, q_ref), (wk_ref, k_ref), (wv_ref, v_ref)):
            result[...] = dot(first, weight[...]).astype(jnp.bfloat16)

    attend_pair(True, pair, q_ref, k_ref, v_ref, mask_ref, line_ref, probs_ref, mixed_ref)


def cross_part(
    tokens_ref, mixed_ref, memory_ref, gain_ref, wso_ref, wq_ref, wk_ref, wv_ref, wo_ref,
    next_gain_ref, mask_ref,
    middle_ref, second_ref, q_ref, k_ref, v_ref, probs_ref, crossed_ref, upper_ref, third_ref,
):
    pair = pl.program_id(0)

    @pl.when(pair == 0)
    def _():
        middle = tokens_ref[...].astype(jnp.float32) + dot(mixed_ref[...], wso_ref[...])
        middle_ref[...] = middle
        second = (middle * scale_of(middle) * gain_ref[...]).astype(jnp.bfloat16)
        second_ref[...] = second
        q_ref[...] = dot(second, wq_ref[...]).astype(jnp.bfloat16)
        k_ref[...] = dot(memory_ref[...], wk_ref[...]).astype(jnp.bfloat16)
        v_ref[...] = dot(memory_ref[...], wv_ref[...]).astype(jnp.bfloat16)

    attend_pair(False, pair, q_ref, k_ref, v_ref, mask_ref, None, probs_ref, crossed_ref)

    @pl.when(pair == PAIRS - 1)
    def _():
        upper = middle_ref[...] + dot(crossed_ref[...], wo_ref[...])
        upper_ref[...] = upper
        third = upper * scale_of(upper) * next_gain_ref[...]
        third_ref[...] = third.astype(jnp.bfloat16)


def third_back(
    gthird_ref, upper_ref, cot_ref, gain_ref, wo_ref, gupper_ref, branch_ref, gmix_ref, ggain_ref
):
    grad, ggain_ref[...] = norm_back(upper_ref[...], gain_ref[...], gthird_ref[...])
    grad = cot_ref[...].astype(jnp.float32) + grad
    gupper_ref[...] = grad
    low = grad.astype(jnp.bfloat16)
    branch_ref[...] = low
    gmix_ref[...] = dot(low, wo_ref[...], NT).astype(jnp.bfloat16)


def last_back(
    gq_ref, gk_ref, gv_ref, gmk_ref, gmv_ref, tokens_ref, gmiddle_ref, gain_ref,
    wq_ref, wk_ref, wv_ref, wmk_ref, wmv_ref,
    gtokens_ref, gmemory_ref, ggain_ref,
):
    gmemory_ref[...] = dot(gmk_ref[...], wmk_ref[...], NT) + dot(gmv_ref[...], wmv_ref[...], NT)
    gfirst = dot(gq_ref[...], wq_ref[...], NT) + dot(gk_ref[...], wk_ref[...], NT)
    gfirst = gfirst + dot(gv_ref[...], wv_ref[...], NT)
    hidden = tokens_ref[...].astype(jnp.float32)
    grad, ggain_ref[...] = norm_back(hidden, gain_ref[...], gfirst)
    gtokens_ref[...] = gmiddle_ref[...] + grad


def put_products(core_ref, rows, pairs, sent_ref, kept_ref):
    for k, (left, right) in enumerate(pairs):
        grads = dot(left[...], right[...], TN)
        if kept_ref is None:
            sent_ref[k] = grads.astype(jnp.bfloat16)
        else:
            grads = grads.reshape(-1, 2, rows, D)
            even, odd = grads[:, 0].reshape(-1, D), grads[:, 1].reshape(-1, D)
            first = core_ref[0] == 0
            sent_ref[k] = jnp.where(first, odd, even).astype(jnp.bfloat16)
            kept_ref[k] = jnp.where(first, even, odd).astype(jnp.bfloat16)


def cross_back(
    rows, core_ref, q_ref, k_ref, v_ref, gcrossed_ref, probs_ref,
    second_ref, memory_ref, crossed_ref, gcross_ref, middle_ref, gupper_ref, gain_ref,
    wq_ref, wso_ref,
    gk_ref, gv_ref, gmiddle_ref, branch_ref, gmix_ref, ggain_ref, sent_ref, *rest,
):
    kept_ref, (gq_ref, dk_sum, dv_sum) = rest[0] if len(rest) == 4 else None, rest[-3:]
    pair = pl.program_id(0)
    attend_back_pair(
        False, pair, q_ref, k_ref, v_ref, gcrossed_ref, probs_ref, gq_ref, gk_ref, gv_ref, None,
        dk_sum, dv_sum,
    )

    @pl.when(pair == PAIRS - 1)
    def _():
        pairs = [
            (second_ref, gq_ref),
            (memory_ref, gk_ref),
            (memory_ref, gv_ref),
            (crossed_ref, gcross_ref),
        ]
        put_products(core_ref, rows, pairs, sent_ref, kept_ref)
        gsecond = dot(gq_ref[...], wq_ref[...], NT)
        grad, ggain_ref[...] = norm_back(middle_ref[...], gain_ref[...], gsecond)
        grad = gupper_ref[...] + grad
        gmiddle_ref[...] = grad
        low = grad.astype(jnp.bfloat16)
        branch_ref[...] = low
        gmix_ref[...] = dot(low, wso_ref[...], NT).astype(jnp.bfloat16)


def self_back(
    rows, core_ref, q_ref, k_ref, v_ref, gmixed_ref, probs_ref, first_ref, mixed_ref, gself_ref,
    gq_ref, gk_ref, gv_ref, sums_ref, late_sent_ref, early_sent_ref, *rest,
):
    kept, (dk_sum, dv_sum) = rest[:2] if len(rest) == 4 else (None, None), rest[-2:]
    pair = pl.program_id(0)
    attend_back_pair(
        True, pair, q_ref, k_ref, v_ref, gmixed_ref, probs_ref, gq_ref, gk_ref, gv_ref, sums_ref,
        dk_sum, dv_sum,
    )

    @pl.when(pair == PAIRS - 1)
    def _():
        late = [(first_ref, gv_ref), (mixed_ref, gself_ref)]
        early = [(first_ref, gq_ref), (first_ref, gk_ref)]
        put_products(core_ref, rows, late, late_sent_ref, kept[0])
        put_products(core_ref, rows, early, early_sent_ref, kept[1])


AXES = ("wide", "narrow")


def after(value, *others):
    return lax.optimization_barrier((value,) + others)[0]


class Cube:
    def __init__(self):
        self.count = lax.axis_size("wide") * lax.axis_size("narrow")
        self.bits = self.count.bit_length() - 1
        self.me = lax.axis_index("wide") * lax.axis_size("narrow") + lax.axis_index("narrow")
        high = list(range(self.bits - 1, 1, -1))
        self.plan_a = high + [1]
        self.plan_b = [1] + high

    def bit(self, which):
        return (self.me >> which) & 1

    def swap(self, value, flip):
        return lax.ppermute(value, AXES, [(i, i ^ flip) for i in range(self.count)])

    def place(self, mine, theirs, which, axis, joined):
        join = jnp.concatenate if joined else jnp.stack
        return jnp.where(
            self.bit(which) == 0, join([mine, theirs], axis), join([theirs, mine], axis)
        )

    def send_step(self, value, plan, step):
        return self.swap(value, 1 << plan[step])

    def place_step(self, value, theirs, plan, step):
        axis = sum(other > plan[step] for other in plan[:step])
        return self.place(value, theirs, plan[step], axis, False)

    def half(self, value, whose):
        size = value.shape[-1] // 2
        return lax.dynamic_slice_in_dim(value, whose * size, size, value.ndim - 1)

    def total(self, value):
        for low in [0] + list(range(1, self.bits, 2)):
            top = 1 if low == 0 else min(2, self.bits - low)
            flips = [flip << low for flip in range(1, 1 << top)]
            value = value + sum(self.swap(value, flip) for flip in flips)
        return value


class Gather:
    def __init__(self, cube, value, plan):
        self.cube, self.value, self.plan, self.steps = cube, value, plan, 0

    def send(self, *behind):
        sent = after(self.value, *behind) if behind else self.value
        self.theirs = self.cube.send_step(sent, self.plan, self.steps)
        return sent

    def take(self, *behind):
        theirs = after(self.theirs, *behind) if behind else self.theirs
        self.value = self.cube.place_step(self.value, theirs, self.plan, self.steps)
        self.steps += 1
        return self.value


def pair_weights(cube, w_in, w_out):
    core = cube.bit(0)
    return [
        cube.place(
            cube.half(part, core), cube.swap(cube.half(part, 1 - core), 1), 0, 0, True
        )
        for part in (w_in, w_out)
    ]


def both_halves(cube, value):
    value = value.reshape((-1,) + value.shape[-2:])
    return value, cube.swap(value, 1)


def whole_weights(cube, parts, first, count):
    rows = D // cube.count
    full = cube.place(parts[0], parts[1], 0, 1, False)
    return [
        full[:, :, first + k * rows : first + (k + 1) * rows].reshape(D, D) for k in range(count)
    ]


class Sums:
    def __init__(self, cube, plan, sent, kept):
        self.cube, self.plan, self.steps = cube, plan, 0
        self.shape = (kept.shape[0],) + (2,) * len(plan) + (-1, kept.shape[-1])
        self.terms, self.theirs = [kept.reshape(self.shape)], cube.swap(sent, 1)

    def take(self, *behind):
        theirs = after(self.theirs, *behind) if behind else self.theirs
        if self.steps == 0:
            theirs = theirs.reshape(self.shape)
        self.terms.append(theirs)

    def value(self):
        return sum(term.astype(jnp.float32) for term in self.terms)

    def send(self, *behind):
        which = self.plan[-1 - self.steps]
        axis = 1 + sum(other > which for other in self.plan[: len(self.plan) - self.steps])
        mine = self.cube.bit(which)
        whole = self.terms
        self.terms = [lax.dynamic_index_in_dim(term, 1 - mine, axis, False) for term in whole]
        sent = self.value().astype(jnp.bfloat16)
        sent = after(sent, *behind) if behind else sent
        self.terms = [lax.dynamic_index_in_dim(term, mine, axis, False) for term in whole]
        self.theirs = self.cube.swap(sent, 1 << which)
        self.steps += 1
        return sent

    def going(self):
        return self.steps < len(self.plan)


def whole_tiles(cube):
    return (D // cube.count) % 8 == 0


def product_outs(cube, count):
    if whole_tiles(cube):
        return [((count, D // 2, D), jnp.bfloat16)] * 2
    return [((count, D, D), jnp.bfloat16)]


def product_sums(cube, plan, parts, *behind):
    chips, rows = cube.count // 2, D // cube.count
    if len(parts) == 1:
        grads = parts[0].reshape(-1, chips, 2, rows, D)
        core = cube.bit(0)
        parts = [lax.dynamic_index_in_dim(grads, core ^ k, 2, False) for k in (1, 0)]
    sent, kept = [part.reshape(-1, chips, rows, D) for part in parts]
    return Sums(cube, plan, after(sent, *behind) if behind else sent, kept)


def half_swap(cube, value):
    value = value.reshape(2, -1, value.shape[-1])
    core = cube.bit(0)
    mine = lax.dynamic_index_in_dim(value, core, 0, False)
    return mine, cube.swap(lax.dynamic_index_in_dim(value, 1 - core, 0, False), 1)


def on_device(
    tokens,
    memory,
    cotangent,
    dec_segments,
    enc_segments,
    dec_valid,
    attn_weights,
    w_in,
    w_out,
    norm_gains,
    rel_table,
    row_main,
    row_out,
    col_main,
    col_in,
):
    cube = Cube()
    core = cube.bit(0)
    rows = attn_weights.shape[1]
    gain_rows = jnp.pad(norm_gains, ((0, 5), (0, D - norm_gains.shape[1])))
    one = Gather(
        cube,
        jnp.concatenate([attn_weights[:2].reshape(-1, D), gain_rows], axis=0),
        cube.plan_a,
    )
    two = Gather(cube, attn_weights[2:4].reshape(-1, D), cube.plan_b)
    one.send()
    two.send()
    in_pair, out_pair = pair_weights(cube, w_in, w_out)
    three = Gather(cube, attn_weights[4:].reshape(-1, D), cube.plan_a)
    inner_half = Gather(cube, in_pair, cube.plan_b)
    outer_half = Gather(cube, out_pair, cube.plan_a)
    last = len(cube.plan_a) - 1
    for step in range(last):
        one.take()
        two.take()
        ahead = one.send(), two.send()
        if step > 0:
            three.take(*ahead)
        ahead = ahead + (three.send(*ahead),)
        if step > 1:
            inner_half.take(*ahead)
            outer_half.take(*ahead)
        if step > 0:
            inner_half.send(*ahead)
            outer_half.send(*ahead)
    one.take()
    two.take()
    first_halves = both_halves(cube, one.value)
    second_halves = both_halves(cube, two.value)
    ahead = first_halves[0], second_halves[0]
    three.take(*ahead)
    ahead = ahead + (three.send(*ahead),)
    inner_half.take(*ahead)
    outer_half.take(*ahead)
    inner_half.send(*ahead)
    outer_half.send(*ahead)
    attn_full = whole_weights(cube, first_halves, 0, 2)
    attn_full = attn_full + whole_weights(cube, second_halves, 0, 2)
    gain_full = cube.place(
        first_halves[0][:, 2 * rows :], first_halves[1][:, 2 * rows :], 0, 1, False
    )[:, :, :3, : norm_gains.shape[1]]
    gain_full = gain_full.transpose(2, 0, 1, 3).reshape(3, D)
    segment = dec_segments[0]
    see_self = self_mask(segment, dec_valid[0])
    see_cross = cross_mask(segment, enc_segments[0])
    lines = bias_lines(rel_table)

    tile, low, full = tokens.shape, jnp.bfloat16, jnp.float32
    gain_one, gain_two, gain_three = [gain_full[k : k + 1].astype(full) for k in range(3)]
    probs = (HEADS, segment.shape[0], segment.shape[0])
    first_low, query, keys, values, self_probs, mixed_low = by_pair(
        self_part,
        [tokens, gain_one, *attn_full[:3], see_self, lines],
        [(tile, low)] * 4 + [(probs, low), (tile, low)],
        [],
        (probs, lines.shape),
        "self_part",
    )
    three.take(mixed_low)
    cross_halves = both_halves(cube, three.value)
    inner_half.take(mixed_low)
    outer_half.take(mixed_low)
    inner_half.send()
    outer_half.send()
    attn_full = attn_full + whole_weights(cube, cross_halves, 0, 4)
    (
        middle, second_low, cross_query, memory_keys, memory_values, cross_probs, crossed_low,
        upper, third_low,
    ) = by_pair(
        cross_part,
        [tokens, mixed_low, memory, gain_two, *attn_full[3:], gain_three, see_cross],
        [(tile, full)] + [(tile, low)] * 4 + [(probs, low), (tile, low), (tile, full), (tile, low)],
        [],
        (probs,),
        "cross_part",
    )
    inner_half.take(third_low)
    outer_half.take(third_low)
    own_in, other_in = both_halves(cube, inner_half.value)
    own_out, other_out = both_halves(cube, outer_half.value)
    layer_out, grad_third, grad_in, other_grad_in, grad_out, other_grad_out = ffn(
        core,
        third_low,
        upper,
        cotangent,
        own_in.reshape(D, -1),
        other_in.reshape(D, -1),
        own_out.reshape(FF, -1),
        other_out.reshape(FF, -1),
    )
    in_sums = Sums(cube, cube.plan_b, other_grad_in[None], grad_in[None])
    out_sums = Sums(cube, cube.plan_a, other_grad_out[None], grad_out[None])
    grad_upper, grad_cross_branch, grad_crossed, grad_gain_third = fused(
        third_back,
        [(tile, full), (tile, low), (tile, low), ((1, D), full)],
        grad_third,
        upper,
        cotangent,
        gain_three,
        attn_full[7],
    )
    in_sums.take(grad_crossed)
    out_sums.take(grad_crossed)
    grad_crossed = after(grad_crossed, in_sums.send(), out_sums.send())
    sums_scratch = [pltpu.VMEM((tile[0], LANES), full)] * 2
    memory_key_low, memory_value_low, grad_middle, grad_self_branch, grad_mixed, *rest = by_pair(
        functools.partial(cross_back, rows),
        [
            core[None],
            cross_query,
            memory_keys,
            memory_values,
            grad_crossed,
            cross_probs,
            second_low,
            memory,
            crossed_low,
            grad_cross_branch,
            middle,
            grad_upper,
            gain_two,
            attn_full[4],
            attn_full[3],
        ],
        [(tile, low)] * 2
        + [(tile, full), (tile, low), (tile, low), ((1, D), full)]
        + product_outs(cube, 4),
        [pltpu.VMEM(tile, low)] + sums_scratch,
        (probs,),
        "cross_back",
    )
    grad_gain_second = rest[0]
    for each in (in_sums, out_sums):
        each.take(grad_mixed)
    cross_sums = product_sums(
        cube, cube.plan_a, rest[1:], in_sums.terms[-1], out_sums.terms[-1]
    )
    started = [in_sums.send(), out_sums.send()]
    cross_sums.take(*started)
    grad_mixed = after(grad_mixed, *started, cross_sums.send())
    lots = (PAIRS, 8, 2 * LANES)
    outs = product_outs(cube, 2)
    query_low, key_low, value_low, score_sums, *rest = by_pair(
        functools.partial(self_back, rows),
        [
            core[None],
            query,
            keys,
            values,
            grad_mixed,
            self_probs,
            first_low,
            mixed_low,
            grad_self_branch,
        ],
        [(tile, low)] * 3 + [(lots, full)] + outs[:1] * 2 + outs[1:] * 2,
        sums_scratch,
        (probs, lots),
        "self_back",
    )
    for each in (in_sums, out_sums):
        each.take(query_low)
    arrived = in_sums.terms[-1], out_sums.terms[-1]
    late_sums = product_sums(cube, cube.plan_b, rest[::2], *arrived)
    early_sums = product_sums(cube, cube.plan_a, rest[1::2], *arrived)
    started = [in_sums.send(), out_sums.send()]
    cross_sums.take(*started)
    started.append(cross_sums.send())
    late_sums.take(*started)
    early_sums.take(*started)
    started.extend([late_sums.send(), early_sums.send()])
    sums = [late_sums, early_sums, cross_sums, in_sums, out_sums]
    query_low = after(query_low, *started)
    grad_tokens, grad_memory, grad_gain_first = fused(
        last_back,
        [(tile, full), (tile, full), ((1, D), full)],
        query_low,
        key_low,
        value_low,
        memory_key_low,
        memory_value_low,
        tokens,
        grad_middle,
        gain_one,
        *attn_full[:3],
        *attn_full[5:7],
    )
    table_grad = table_sums(score_sums)
    gain_local = jnp.concatenate([grad_gain_first, grad_gain_second, grad_gain_third], axis=0)
    behind = (grad_tokens,)
    while any(each.going() for each in sums):
        moving = [each for each in sums if each.going()]
        for each in moving:
            each.take(*behind)
            behind = behind + (each.send(),)
        behind = ()
    for each in sums:
        each.take(*behind)
    grad_in, grad_out = [
        cube.place(*half_swap(cube, each.value()), 0, 1, True) for each in sums[3:]
    ]
    grad_attn = jnp.concatenate(
        [each.value().reshape(-1, rows, D) for each in (early_sums, late_sums, cross_sums)], axis=0
    )
    square_attn = grad_attn * grad_attn
    square_in = grad_in * grad_in
    square_out = grad_out * grad_out
    row_means = jnp.concatenate(
        [jnp.mean(square_attn, axis=2), jnp.mean(square_in, axis=1)[None]], axis=0
    )
    new_row_main = DECAY * row_main + (1.0 - DECAY) * row_means
    new_row_out = DECAY * row_out + (1.0 - DECAY) * jnp.mean(square_out, axis=1)
    column_main = jnp.concatenate(
        [jnp.sum(square_attn, axis=1), jnp.sum(square_out, axis=0)[None]], axis=0
    )
    column_in = jnp.sum(square_in, axis=0)
    parts = [column_main, column_in, table_grad, gain_local]
    sizes = [part.size for part in parts]
    width = D // 2
    lines = -(-sum(sizes) // (8 * width)) * 8
    flat = jnp.concatenate([part.reshape(-1, width) for part in parts], axis=0)
    flat = cube.total(jnp.pad(flat, ((0, lines - flat.shape[0]), (0, 0))))
    sums, at = [], 0
    for part, size in zip(parts, sizes):
        sums.append(flat[at : at + size // width].reshape(part.shape))
        at += size // width
    column_main, column_in, grad_table, gain_sums = sums
    grad_gains = lax.dynamic_slice_in_dim(
        gain_sums, cube.me * norm_gains.shape[1], norm_gains.shape[1], 1
    )
    col_means = jnp.concatenate([column_main[:8] / D, column_main[8:] / FF], axis=0)
    new_col_main = DECAY * col_main + (1.0 - DECAY) * col_means
    new_col_in = DECAY * col_in + (1.0 - DECAY) * (column_in / D)
    return (
        layer_out,
        grad_tokens,
        grad_memory,
        grad_attn,
        grad_in,
        grad_out,
        grad_gains,
        grad_table,
        new_row_main,
        new_row_out,
        new_col_main,
        new_col_in,
    )


def solution(mesh):
    placed = (
        P(("wide", "narrow"), None),
        P(("wide", "narrow"), None),
        P(("wide", "narrow"), None),
        P(("wide", "narrow"), None),
        P(("wide", "narrow"), None),
        P(("wide", "narrow"), None),
        P(None, ("wide", "narrow"), None),
        P(("wide", "narrow"), None),
        P(("wide", "narrow"), None),
        P(None, ("wide", "narrow")),
        P(),
        P(None, ("wide", "narrow")),
        P(("wide", "narrow")),
        P(),
        P(),
    )
    return jax.shard_map(
        on_device,
        mesh=mesh,
        in_specs=placed,
        out_specs=(
            P(("wide", "narrow"), None),
            P(("wide", "narrow"), None),
            P(("wide", "narrow"), None),
            P(None, ("wide", "narrow"), None),
            P(("wide", "narrow"), None),
            P(("wide", "narrow"), None),
            P(None, ("wide", "narrow")),
            P(),
            P(None, ("wide", "narrow")),
            P(("wide", "narrow")),
            P(),
            P(),
        ),
        check_vma=False,
    )
```

```python
import functools
import math

import jax
import jax.numpy as jnp
from jax import lax
from jax.experimental import pallas as pl
from jax.experimental.pallas import tpu as pltpu
from jax.sharding import PartitionSpec as P

D = 768
HEADS = 12
HEAD = 64
FF = 3072
BUCKETS = 32
MAXDIST = 128


EPSILON = 1e-06
DECAY = 0.8
NEGATIVE = -1e30


def thresholds():
    exact_count = BUCKETS // 2
    limits = list(range(1, exact_count + 1))
    for bucket_level in range(exact_count + 1, BUCKETS):
        limits.append(
            int(
                math.ceil(
                    exact_count
                    * (MAXDIST / exact_count) ** ((bucket_level - exact_count) / exact_count)
                )
            )
        )
    return limits


def bucket_table(distance, number_type):
    level_count = jnp.zeros(distance.shape, jnp.int32)
    for threshold in thresholds():
        level_count = level_count + (distance >= threshold).astype(jnp.int32)
    return (level_count[..., None] == jnp.arange(BUCKETS, dtype=jnp.int32)).astype(number_type)


def weight_grad(left_side, gradient):
    return lax.dot_general(
        left_side, gradient, (((0,), (0,)), ((), ())), preferred_element_type=jnp.float32
    )


LANES = 128
GROUP = LANES // HEAD
CUT = 256
VMEM_BYTES = 56 * 1024 * 1024

NT = (((1,), (1,)), ((), ()))
TN = (((0,), (0,)), ((), ()))


def dot(left, right, dims=(((1,), (0,)), ((), ()))):
    return lax.dot_general(left, right, dims, preferred_element_type=jnp.float32)


def spans(rows, causal):
    return [(at, at + CUT if causal else rows) for at in range(0, rows, CUT)]


def lane_mask(head):
    lanes = lax.broadcasted_iota(jnp.int32, (1, LANES), 1)
    return ((lanes // HEAD) == head).astype(jnp.float32)


def only_head(block, head, scale):
    return (block.astype(jnp.float32) * (lane_mask(head) * scale)).astype(jnp.bfloat16)


def near_bias(line_ref, head):
    line = jnp.broadcast_to(line_ref[0, head : head + 1], (LANES, 2 * LANES))
    return pltpu.roll(line, 0, 1, stride=1, stride_axis=0)


def add_bias(scores, bias, at):
    columns = []
    for first in range(0, CUT, LANES):
        rows = []
        for key in range(0, scores.shape[0], LANES):
            apart = at + first - key
            block = scores[key : key + LANES, first : first + LANES]
            if apart >= 2 * LANES:
                block = block + bias[:1, 2 * LANES - 1 :]
            elif apart >= 0:
                block = block + bias[:, apart : apart + LANES]
            rows.append(block)
        columns.append(jnp.concatenate(rows, axis=0))
    return jnp.concatenate(columns, axis=1)


def attend_pair(causal, pair, q_ref, k_ref, v_ref, mask_ref, line_ref, probs_ref, out_ref):
    rows = q_ref.shape[0]
    lanes = pl.ds(pl.multiple_of(pair * LANES, LANES), LANES)
    biases = [near_bias(line_ref, head) for head in range(GROUP)] if causal else None
    for at, depth in spans(rows, causal):
        keys, values = k_ref[:depth, lanes], v_ref[:depth, lanes]
        total = jnp.zeros((CUT, LANES), jnp.float32)
        for head in range(GROUP):
            query = only_head(q_ref[at : at + CUT, lanes], head, HEAD**-0.5)
            scores = dot(keys, query, NT)
            if causal:
                scores = add_bias(scores, biases[head], at)
            scores = scores + mask_ref[:depth, at : at + CUT]
            weights = jnp.exp(scores - jnp.max(scores, axis=0, keepdims=True))
            weights = weights * (1.0 / jnp.sum(weights, axis=0, keepdims=True))
            low = weights.astype(jnp.bfloat16)
            probs_ref[head, :depth, at : at + CUT] = low
            total = total + dot(low, values, TN) * lane_mask(head)
        out_ref[at : at + CUT, lanes] = total.astype(jnp.bfloat16)


def diagonal_sums(block):
    width = block.shape[1]
    slabs = [block[at : at + 8] for at in range(0, block.shape[0], 8)]
    total = slabs[0]
    for at, slab in enumerate(slabs[1:], 1):
        total = total + pltpu.roll(slab, width - 8 * at, 1)
    row = lax.broadcasted_iota(jnp.int32, total.shape, 0)
    for step in (1, 2, 4):
        total = jnp.where((row & step) != 0, pltpu.roll(total, width - step, 1), total)
    return jnp.sum(total, axis=0, keepdims=True)


def attend_back_pair(
    causal, pair, q_ref, k_ref, v_ref, g_ref, probs_ref, dq_ref, dk_ref, dv_ref, sums_ref,
    dk_sum, dv_sum,
):
    rows = q_ref.shape[0]
    lanes = pl.ds(pl.multiple_of(pair * LANES, LANES), LANES)
    dk_sum[...] = jnp.zeros_like(dk_sum)
    dv_sum[...] = jnp.zeros_like(dv_sum)
    near = [[], []]
    far = [[], []]
    for at, depth in spans(rows, causal):
        dq = jnp.zeros((CUT, LANES), jnp.float32)
        for head in range(GROUP):
            grad = only_head(g_ref[at : at + CUT, lanes], head, 1.0)
            query = only_head(q_ref[at : at + CUT, lanes], head, HEAD**-0.5)
            keys = only_head(k_ref[:depth, lanes], head, HEAD**-0.5)
            low = probs_ref[head, :depth, at : at + CUT]
            probs = low.astype(jnp.float32)
            scaled = probs * dot(v_ref[:depth, lanes], grad, NT)
            centre = jnp.sum(scaled, axis=0, keepdims=True)
            grad_scores = (scaled - probs * centre).astype(jnp.bfloat16)
            dv_sum[:depth] += dot(low, grad)
            dk_sum[:depth] += dot(grad_scores, query)
            dq = dq + dot(grad_scores, keys, TN)
            if causal:
                parts = grad_scores.astype(jnp.float32)
                for first in range(0, CUT, LANES):
                    own = at + first
                    column = parts[:, first : first + LANES]
                    if own:
                        before = column[own - LANES : own]
                    else:
                        before = jnp.zeros((LANES, LANES), jnp.float32)
                    near[head].append((column[own : own + LANES], before))
                    if own > LANES:
                        far[head].append(jnp.sum(column[: own - LANES], axis=0, keepdims=True))
        dq_ref[at : at + CUT, lanes] = dq.astype(jnp.bfloat16)
    dk_ref[:, lanes] = dk_sum[...].astype(jnp.bfloat16)
    dv_ref[:, lanes] = dv_sum[...].astype(jnp.bfloat16)
    if causal:
        lines = []
        for head in range(GROUP):
            own = sum(pair[0] for pair in near[head][1:]) + near[head][0][0]
            before = sum(pair[1] for pair in near[head][1:]) + near[head][0][1]
            lines.append(diagonal_sums(jnp.concatenate([own, before], axis=1)))
        for head in range(GROUP):
            line = sum(far[head][1:]) + far[head][0]
            lines.append(jnp.concatenate([line, jnp.zeros_like(line)], axis=1))
        lines.append(jnp.zeros((8 - len(lines), 2 * LANES), jnp.float32))
        sums_ref[0] = jnp.concatenate(lines, axis=0)


def self_mask(segment, key_valid):
    rows = segment.shape[0]
    index = jnp.arange(rows, dtype=jnp.int32)
    distance = index[None, :] - index[:, None]
    allowed = (
        (segment[:, None] == segment[None, :])
        & (distance >= 0)
        & ((key_valid[:, None] > 0) | (distance == 0))
    )
    return jnp.where(allowed, 0.0, NEGATIVE).astype(jnp.float32)


def cross_mask(segment, mem_segment):
    allowed = mem_segment[:, None] == segment[None, :]
    return jnp.where(allowed, 0.0, NEGATIVE).astype(jnp.float32)


def bias_lines(table):
    places = bucket_table(jnp.arange(2 * LANES, dtype=jnp.int32), jnp.float32)
    lines = jnp.einsum(
        "nb,bh->hn", places, table.astype(jnp.float32), precision=lax.Precision.HIGHEST
    )
    lines = lines.reshape(HEADS // GROUP, GROUP, 2 * LANES)
    return jnp.pad(lines, ((0, 0), (0, 8 - GROUP), (0, 0)))


def table_sums(sums):
    near = sums[:, :GROUP].reshape(HEADS, 2 * LANES)
    far = jnp.sum(sums[:, GROUP : 2 * GROUP], axis=-1).reshape(HEADS)
    places = bucket_table(jnp.arange(2 * LANES, dtype=jnp.int32), jnp.float32)
    grad = jnp.einsum("nb,hn->bh", places, near, precision=lax.Precision.HIGHEST)
    return grad.at[BUCKETS - 1].add(far)


GELU_SCALE = math.sqrt(2.0 / math.pi)
GELU_CUBE = 0.044715
BLOCK = 768
CUTS = FF // (2 * BLOCK)


def chip_of(chip, place, plan):
    bits = [which for group in plan for which in group]
    flip = sum(((place >> k) & 1) << (which - 1) for k, which in enumerate(bits))
    return chip ^ flip


def halves_of(core):
    half = D // 2
    mine = pl.ds(pl.multiple_of(core * half, half), half)
    return mine, pl.ds(pl.multiple_of((1 - core) * half, half), half)


def fill_weight(weight_ref, parts, at, spot_ref, plan):
    if len(parts) == 1:
        weight_ref[...] = parts[0][at]
        return
    blocks, rows = parts[0].shape[0], D // (2 * parts[0].shape[0])
    mine, other = halves_of(spot_ref[1])
    for place in range(2 * blocks):
        chip = chip_of(spot_ref[0], place, plan)
        lines = pl.ds(pl.multiple_of(chip * rows, rows), rows)
        which, block = divmod(place, blocks)
        weight_ref[lines, mine] = parts[which][block, at * rows : (at + 1) * rows]
        weight_ref[lines, other] = parts[2 + which][block, at * rows : (at + 1) * rows]


def put_divided(grads, rows, core, sent_ref, kept_ref):
    columns = grads.shape[1]
    grads = grads.reshape(-1, 2, rows, columns)
    even, odd = grads[:, 0].reshape(-1, columns), grads[:, 1].reshape(-1, columns)
    sent_ref[...] = jnp.where(core == 0, odd, even).astype(jnp.bfloat16)
    kept_ref[...] = jnp.where(core == 0, even, odd).astype(jnp.bfloat16)


def ffn_kernel(tiled, plan, spot_ref, third_ref, upper_ref, cot_ref, *refs):
    step = pl.program_id(0)
    if tiled:
        own_in, other_in, out_parts, refs = refs[:2], refs[2:4], refs[4:8], refs[8:]
        layer_ref, gthird_ref, gin_ref, kept_gin_ref, gout_ref, kept_gout_ref = refs[:6]
        total, third_turned, in_block, out_block = refs[6:]
    else:
        in_block, out_block, layer_ref, gthird_ref, gin_ref, gout_ref = refs[:6]
        total, third_turned = refs[6:]

    @pl.when(step == 0)
    def _():
        total[...] = upper_ref[...]
        gthird_ref[...] = jnp.zeros_like(gthird_ref)
        third_turned[...] = third_ref[...].T

    def fill_in(parts):
        blocks, rows, _ = parts[0].shape
        for place in range(2 * blocks):
            chip = chip_of(spot_ref[0], place, plan)
            lines = pl.ds(pl.multiple_of(chip * rows, rows), rows)
            in_block[lines, :] = parts[place // blocks][place % blocks]

    if tiled:
        pl.when(step < CUTS)(lambda: fill_in(other_in))
        pl.when(step >= CUTS)(lambda: fill_in(own_in))
        mine, other = halves_of(spot_ref[1])
        rows = out_parts[0].shape[2]
        for place in range(4):
            chip = (spot_ref[0] & 3) ^ place
            lines = pl.ds(pl.multiple_of(chip * rows, rows), rows)
            out_block[lines, mine] = out_parts[place % 2][place // 2, 0]
            out_block[lines, other] = out_parts[2 + place % 2][place // 2, 0]

    inner = dot(third_ref[...], in_block[...])
    square = inner * inner
    slope = jnp.tanh(inner * (GELU_SCALE + (GELU_SCALE * GELU_CUBE) * square))
    half_up = 0.5 + 0.5 * slope
    active = (inner * half_up).astype(jnp.bfloat16)
    total[...] += dot(active, out_block[...])
    grad_active = dot(cot_ref[...], out_block[...], NT)
    bend = (0.5 * inner) * (1.0 - slope * slope)
    bend = bend * (GELU_SCALE + (3.0 * GELU_SCALE * GELU_CUBE) * square)
    grad_inner = (grad_active * (half_up + bend)).astype(jnp.bfloat16)
    gthird_ref[...] += dot(grad_inner, in_block[...], NT)
    grad_in = dot(third_turned[...], grad_inner)
    grad_out = dot(active, cot_ref[...], TN)
    if tiled:
        chips = 2 * own_in[0].shape[0]
        put_divided(grad_in, D // (2 * chips), spot_ref[1], gin_ref, kept_gin_ref)
        put_divided(grad_out, FF // (2 * chips), spot_ref[1], gout_ref, kept_gout_ref)
    else:
        gin_ref[...] = grad_in.astype(jnp.bfloat16)
        gout_ref[...] = grad_out.astype(jnp.bfloat16)

    @pl.when(step == 2 * CUTS - 1)
    def _():
        layer_ref[...] = total[...].astype(jnp.bfloat16)


def ffn(spot, plan, third, upper, cotangent, in_parts, out_parts):
    rows = third.shape[0]
    tiled = len(in_parts) > 1

    def block(step, spot_ref):
        return ((1 - spot_ref[1]) * CUTS + step) % (2 * CUTS)

    def line(step, spot_ref):
        flips = block(step, spot_ref) ^ (spot_ref[0] >> 2)
        return (0, (flips >> 1) + 2 * (flips & 1), 0, 0)

    whole = pl.BlockSpec((rows, D), lambda step, spot_ref: (0, 0))
    across = lambda step, spot_ref: (0, block(step, spot_ref))
    down = lambda step, spot_ref: (block(step, spot_ref), 0)
    scratch = [pltpu.VMEM((rows, D), jnp.float32), pltpu.VMEM((D, rows), jnp.bfloat16)]
    if tiled:
        chips, lines, _ = in_parts[0].shape
        late = lambda step, spot_ref: (0, 0, jnp.maximum(step - CUTS, 0))
        early = lambda step, spot_ref: (0, 0, jnp.minimum(step, CUTS - 1))
        in_specs = [pl.BlockSpec((chips, lines, BLOCK), late)] * 2
        in_specs += [pl.BlockSpec((chips, lines, BLOCK), early)] * 2
        out_parts = [part.reshape(2, 4, -1, D // 2) for part in out_parts]
        in_specs += [pl.BlockSpec((2, 1) + out_parts[0].shape[2:], line)] * 4
        out_specs = [pl.BlockSpec((D // 2, BLOCK), across)] * 2
        out_specs += [pl.BlockSpec((BLOCK // 2, D), down)] * 2
        shapes = [(D // 2, FF)] * 2 + [(FF // 2, D)] * 2
        scratch += [pltpu.VMEM((D, BLOCK), jnp.bfloat16), pltpu.VMEM((BLOCK, D), jnp.bfloat16)]
    else:
        in_specs = [pl.BlockSpec((D, BLOCK), across), pl.BlockSpec((BLOCK, D), down)]
        out_specs, shapes = in_specs, [(D, FF), (FF, D)]
    return pl.pallas_call(
        functools.partial(ffn_kernel, tiled, plan),
        grid_spec=pltpu.PrefetchScalarGridSpec(
            num_scalar_prefetch=1,
            grid=(2 * CUTS,),
            in_specs=[whole, whole, whole] + in_specs,
            out_specs=[whole, whole] + out_specs,
            scratch_shapes=scratch,
        ),
        out_shape=[
            jax.ShapeDtypeStruct((rows, D), jnp.bfloat16),
            jax.ShapeDtypeStruct((rows, D), jnp.float32),
        ]
        + [jax.ShapeDtypeStruct(shape, jnp.bfloat16) for shape in shapes],
        compiler_params=pltpu.CompilerParams(vmem_limit_bytes=VMEM_BYTES),
        name="ffn",
    )(spot, third, upper, cotangent, *in_parts, *out_parts)


def scale_of(hidden):
    return lax.rsqrt(jnp.mean(hidden * hidden, axis=-1, keepdims=True) + EPSILON)


def norm_back(hidden, gain, grad):
    scale = scale_of(hidden)
    grown = grad * gain
    inner = jnp.mean(grown * hidden, axis=-1, keepdims=True)
    gain_grad = jnp.sum(grad * (hidden * scale), axis=0, keepdims=True)
    return scale * grown - hidden * (scale * scale * scale * inner), gain_grad


def fused(kernel, outs, *args):
    space = pl.BlockSpec(memory_space=pltpu.VMEM)
    return pl.pallas_call(
        kernel,
        in_specs=[space] * len(args),
        out_specs=[space] * len(outs),
        out_shape=[jax.ShapeDtypeStruct(shape, held_as) for shape, held_as in outs],
        compiler_params=pltpu.CompilerParams(vmem_limit_bytes=VMEM_BYTES),

        name=kernel.__name__,
    )(*args)


PAIRS = HEADS // GROUP


def whole_spec(array, space=None):
    rank = len(array.shape)
    return pl.BlockSpec(array.shape, lambda pair: (0,) * rank, pipeline_mode=space)


def by_pair(kernel, args, outs, scratch, by_step, name):
    held = [jax.ShapeDtypeStruct(shape, held_as) for shape, held_as in outs]

    def spec(array, once):
        if len(array.shape) == 3 and array.shape in by_step:
            block = (array.shape[0] // PAIRS,) + array.shape[1:]
            return pl.BlockSpec(block, lambda pair: (pair, 0, 0))
        if len(array.shape) == 1:
            return pl.BlockSpec(memory_space=pltpu.SMEM)
        return whole_spec(array, pl.Buffered(1) if once else None)

    return pl.pallas_call(
        kernel,
        grid=(PAIRS,),
        in_specs=[spec(array, True) for array in args],
        out_specs=[spec(array, False) for array in held],
        out_shape=held,
        scratch_shapes=scratch,
        compiler_params=pltpu.CompilerParams(vmem_limit_bytes=VMEM_BYTES),
        name=name,
    )(*args)


def self_part(plans, spot_ref, tokens_ref, gain_ref, mask_ref, line_ref, *refs):
    count = (len(refs) - 10) // 2
    one, two, refs = refs[:count], refs[count : 2 * count], refs[2 * count :]
    first_ref, q_ref, k_ref, v_ref, probs_ref, mixed_ref, wq_ref, wk_ref, wv_ref, wo_ref = refs
    pair = pl.program_id(0)

    @pl.when(pair == 0)
    def _():
        hidden = tokens_ref[...].astype(jnp.float32)
        first = (hidden * scale_of(hidden) * gain_ref[...]).astype(jnp.bfloat16)
        first_ref[...] = first
        weights = [(wq_ref, one, 0, q_ref), (wk_ref, one, 1, k_ref), (wv_ref, two, 0, v_ref)]
        for weight_ref, parts, at, result in weights:
            fill_weight(weight_ref, parts, at, spot_ref, plans[parts is two])
            result[...] = dot(first, weight_ref[...]).astype(jnp.bfloat16)
        fill_weight(wo_ref, two, 1, spot_ref, plans[1])

    attend_pair(True, pair, q_ref, k_ref, v_ref, mask_ref, line_ref, probs_ref, mixed_ref)


def cross_part(
    plan, spot_ref, tokens_ref, mixed_ref, memory_ref, gain_ref, wso_ref, next_gain_ref, mask_ref,
    *refs,
):
    parts, refs = refs[:-13], refs[-13:]
    middle_ref, second_ref, q_ref, k_ref, v_ref, probs_ref, crossed_ref = refs[:7]
    upper_ref, third_ref, wq_ref, wk_ref, wv_ref, wo_ref = refs[7:]
    pair = pl.program_id(0)

    @pl.when(pair == 0)
    def _():
        for at, weight_ref in enumerate((wq_ref, wk_ref, wv_ref, wo_ref)):
            fill_weight(weight_ref, parts, at, spot_ref, plan)
        middle = tokens_ref[...].astype(jnp.float32) + dot(mixed_ref[...], wso_ref[...])
        middle_ref[...] = middle
        second = (middle * scale_of(middle) * gain_ref[...]).astype(jnp.bfloat16)
        second_ref[...] = second
        q_ref[...] = dot(second, wq_ref[...]).astype(jnp.bfloat16)
        k_ref[...] = dot(memory_ref[...], wk_ref[...]).astype(jnp.bfloat16)
        v_ref[...] = dot(memory_ref[...], wv_ref[...]).astype(jnp.bfloat16)

    attend_pair(False, pair, q_ref, k_ref, v_ref, mask_ref, None, probs_ref, crossed_ref)

    @pl.when(pair == PAIRS - 1)
    def _():
        upper = middle_ref[...] + dot(crossed_ref[...], wo_ref[...])
        upper_ref[...] = upper
        third = upper * scale_of(upper) * next_gain_ref[...]
        third_ref[...] = third.astype(jnp.bfloat16)


def third_back(
    gthird_ref, upper_ref, cot_ref, gain_ref, wo_ref, gupper_ref, branch_ref, gmix_ref, ggain_ref
):
    grad, ggain_ref[...] = norm_back(upper_ref[...], gain_ref[...], gthird_ref[...])
    grad = cot_ref[...].astype(jnp.float32) + grad
    gupper_ref[...] = grad
    low = grad.astype(jnp.bfloat16)
    branch_ref[...] = low
    gmix_ref[...] = dot(low, wo_ref[...], NT).astype(jnp.bfloat16)


def last_back(
    gq_ref, gk_ref, gv_ref, gmk_ref, gmv_ref, tokens_ref, gmiddle_ref, gain_ref,
    wq_ref, wk_ref, wv_ref, wmk_ref, wmv_ref,
    gtokens_ref, gmemory_ref, ggain_ref,
):
    gmemory_ref[...] = dot(gmk_ref[...], wmk_ref[...], NT) + dot(gmv_ref[...], wmv_ref[...], NT)
    gfirst = dot(gq_ref[...], wq_ref[...], NT) + dot(gk_ref[...], wk_ref[...], NT)
    gfirst = gfirst + dot(gv_ref[...], wv_ref[...], NT)
    hidden = tokens_ref[...].astype(jnp.float32)
    grad, ggain_ref[...] = norm_back(hidden, gain_ref[...], gfirst)
    gtokens_ref[...] = gmiddle_ref[...] + grad


def put_products(core_ref, rows, pairs, sent_ref, kept_ref):
    for k, (left, right) in enumerate(pairs):
        grads = dot(left[...], right[...], TN)
        if kept_ref is None:
            sent_ref[k] = grads.astype(jnp.bfloat16)
        else:
            put_divided(grads, rows, core_ref[0], sent_ref.at[k], kept_ref.at[k])


def cross_back(
    rows, core_ref, q_ref, k_ref, v_ref, gcrossed_ref, probs_ref,
    second_ref, memory_ref, crossed_ref, gcross_ref, middle_ref, gupper_ref, gain_ref,
    wq_ref, wso_ref,
    gk_ref, gv_ref, gmiddle_ref, branch_ref, gmix_ref, ggain_ref, sent_ref, *rest,
):
    kept_ref, (gq_ref, dk_sum, dv_sum) = rest[0] if len(rest) == 4 else None, rest[-3:]
    pair = pl.program_id(0)
    attend_back_pair(
        False, pair, q_ref, k_ref, v_ref, gcrossed_ref, probs_ref, gq_ref, gk_ref, gv_ref, None,
        dk_sum, dv_sum,
    )

    @pl.when(pair == PAIRS - 1)
    def _():
        pairs = [
            (second_ref, gq_ref),
            (memory_ref, gk_ref),
            (memory_ref, gv_ref),
            (crossed_ref, gcross_ref),
        ]
        put_products(core_ref, rows, pairs, sent_ref, kept_ref)
        gsecond = dot(gq_ref[...], wq_ref[...], NT)
        grad, ggain_ref[...] = norm_back(middle_ref[...], gain_ref[...], gsecond)
        grad = gupper_ref[...] + grad
        gmiddle_ref[...] = grad
        low = grad.astype(jnp.bfloat16)
        branch_ref[...] = low
        gmix_ref[...] = dot(low, wso_ref[...], NT).astype(jnp.bfloat16)


def self_back(
    rows, core_ref, q_ref, k_ref, v_ref, gmixed_ref, probs_ref, first_ref, mixed_ref, gself_ref,
    gq_ref, gk_ref, gv_ref, sums_ref, late_sent_ref, early_sent_ref, *rest,
):
    kept, (dk_sum, dv_sum) = rest[:2] if len(rest) == 4 else (None, None), rest[-2:]
    pair = pl.program_id(0)
    attend_back_pair(
        True, pair, q_ref, k_ref, v_ref, gmixed_ref, probs_ref, gq_ref, gk_ref, gv_ref, sums_ref,
        dk_sum, dv_sum,
    )

    @pl.when(pair == PAIRS - 1)
    def _():
        late = [(first_ref, gv_ref), (mixed_ref, gself_ref)]
        early = [(first_ref, gq_ref), (first_ref, gk_ref)]
        put_products(core_ref, rows, late, late_sent_ref, kept[0])
        put_products(core_ref, rows, early, early_sent_ref, kept[1])


AXES = ("wide", "narrow")


def after(value, *others):
    return lax.optimization_barrier((value,) + others)[0]


class Cube:
    def __init__(self):
        self.count = lax.axis_size("wide") * lax.axis_size("narrow")
        self.bits = self.count.bit_length() - 1
        self.me = lax.axis_index("wide") * lax.axis_size("narrow") + lax.axis_index("narrow")
        high = [[which] for which in range(self.bits - 1, 1, -1)]
        self.plan_a = high + [[1]]
        self.plan_b = [[1]] + high

    def bit(self, which):
        return (self.me >> which) & 1

    def swap(self, value, flip):
        return lax.ppermute(value, AXES, [(i, i ^ flip) for i in range(self.count)])

    def place(self, mine, theirs, axis):
        first = self.bit(0) == 0
        return jnp.where(
            first, jnp.concatenate([mine, theirs], axis), jnp.concatenate([theirs, mine], axis)
        )

    def half(self, value, whose):
        size = value.shape[-1] // 2
        return lax.dynamic_slice_in_dim(value, whose * size, size, value.ndim - 1)

    def total(self, value):
        for low in [0] + list(range(1, self.bits, 2)):
            top = 1 if low == 0 else min(2, self.bits - low)
            flips = [flip << low for flip in range(1, 1 << top)]
            value = value + sum(self.swap(value, flip) for flip in flips)
        return value


def flips_of(group):
    picks = range(1, 1 << len(group))
    return [sum(((pick >> k) & 1) << which for k, which in enumerate(group)) for pick in picks]


class Gather:
    def __init__(self, cube, value, plan):
        self.cube, self.plan, self.steps = cube, plan, 0
        self.held, self.parts = value[None], []

    def send(self, *behind):
        sent = after(self.held, *behind) if behind else self.held
        self.theirs = [self.cube.swap(sent, flip) for flip in flips_of(self.plan[self.steps])]
        self.steps += 1
        if self.steps == len(self.plan):
            self.parts = [self.held, self.cube.swap(sent, 1)]
        return sent

    def take(self, *behind):
        theirs = [after(their, *behind) if behind else their for their in self.theirs]
        if self.parts:
            self.parts = [self.parts[0], *theirs, self.parts[1], self.cube.swap(theirs[0], 1)]
        else:
            self.held = jnp.concatenate([self.held, *theirs], axis=0)


def pair_columns(cube, value, *behind):
    core = cube.bit(0)
    sent = cube.half(value, 1 - core)
    theirs = cube.swap(after(sent, *behind) if behind else sent, 1)
    return cube.half(value, core), theirs


class Sums:
    def __init__(self, cube, plan, sent, kept):
        self.cube, self.plan, self.steps = cube, plan, 0
        self.bits = sorted(which for group in plan for which in group)
        self.shape = (kept.shape[0],) + (2,) * len(self.bits) + (-1, kept.shape[-1])
        self.terms, self.theirs = [kept.reshape(self.shape)], [cube.swap(sent, 1)]

    def take(self, *behind):
        for their in self.theirs:
            their = after(their, *behind) if behind else their
            self.terms.append(their.reshape(self.shape) if self.steps == 0 else their)

    def value(self):
        return sum(term.astype(jnp.float32) for term in self.terms)

    def pick(self, group, flip):
        terms = self.terms
        for which in sorted(group):
            axis = 1 + sum(other > which for other in self.bits)
            index = self.cube.bit(which) ^ ((flip >> which) & 1)
            terms = [lax.dynamic_index_in_dim(term, index, axis, False) for term in terms]
        return terms

    def send(self, *behind):
        group = self.plan[-1 - self.steps]
        everything, sent = self.terms, []
        for flip in flips_of(group):
            self.terms = self.pick(group, flip)
            part = self.value().astype(jnp.bfloat16)
            sent.append(after(part, *behind) if behind else part)
            self.terms = everything
        self.terms = self.pick(group, 0)
        self.bits = [which for which in self.bits if which not in group]
        self.theirs = [self.cube.swap(part, flip) for part, flip in zip(sent, flips_of(group))]
        self.steps += 1
        return tuple(sent)

    def going(self):
        return self.steps < len(self.plan)


def whole_tiles(cube):
    return cube.bits == 5


def product_outs(cube, count):
    if whole_tiles(cube):
        return [((count, D // 2, D), jnp.bfloat16)] * 2
    return [((count, D, D), jnp.bfloat16)]


def product_sums(cube, plan, parts, *behind):
    chips, count, columns = cube.count // 2, parts[0].shape[0], parts[0].shape[2]
    if len(parts) == 1:
        grads = parts[0].reshape(count, chips, 2, -1, columns)
        core = cube.bit(0)
        parts = [lax.dynamic_index_in_dim(grads, core ^ k, 2, False) for k in (1, 0)]
    sent, kept = [part.reshape(count, chips, -1, columns) for part in parts]
    return Sums(cube, plan, after(sent, *behind) if behind else sent, kept)


def chip_order(cube, parts, plan):
    places = jnp.concatenate(parts, axis=0)
    chips = chip_of(cube.me >> 1, jnp.arange(places.shape[0], dtype=jnp.int32), plan)
    moves = jnp.arange(places.shape[0], dtype=jnp.int32)[:, None] == chips[None, :]
    moved = jnp.dot(moves.astype(places.dtype), places.reshape(places.shape[0], -1))
    return moved.reshape(places.shape)


def on_device(
    tokens,
    memory,
    cotangent,
    dec_segments,
    enc_segments,
    dec_valid,
    attn_weights,
    w_in,
    w_out,
    norm_gains,
    rel_table,
    row_main,
    row_out,
    col_main,
    col_in,
):
    cube = Cube()
    core = cube.bit(0)
    spot = jnp.stack([cube.me >> 1, core])
    rows = attn_weights.shape[1]
    tiled = whole_tiles(cube)
    plans = cube.plan_a, cube.plan_b
    segment = dec_segments[0]
    see_self = self_mask(segment, dec_valid[0])
    see_cross = cross_mask(segment, enc_segments[0])
    lines = bias_lines(rel_table)
    tile, low, full = tokens.shape, jnp.bfloat16, jnp.float32
    square = ((D, D), low)
    probs = (HEADS, segment.shape[0], segment.shape[0])
    if tiled:
        attn_rows = attn_weights[:4].reshape(-1, D)
        gain_rows = jnp.pad(norm_gains, ((0, 5), (0, D // 2 - rows)))
        sent = jnp.concatenate([cube.half(attn_rows, 1 - core), gain_rows], axis=0)
        theirs = cube.swap(sent, 1)
        pairs = cube.place(
            cube.half(attn_rows, core).reshape(4, rows, -1),
            theirs[: 4 * rows].reshape(4, rows, -1),
            1,
        ).reshape(4 * 2 * rows, -1)
        gain_pair = cube.place(gain_rows, theirs[4 * rows :], 0)
        one = Gather(cube, jnp.concatenate([pairs[: 4 * rows], gain_pair], axis=0), cube.plan_a)
        two = Gather(cube, pairs[4 * rows :], cube.plan_b)
        ahead = one.send(), two.send()
        cross = pair_columns(cube, attn_weights[4:], *ahead)
        inner = pair_columns(cube, w_in, *ahead)
        outer = pair_columns(cube, w_out, *ahead)
        three = Gather(cube, cube.place(*cross, 1).reshape(8 * rows, -1), cube.plan_a)
        inner = Gather(cube, cube.place(*inner, 0), cube.plan_b)
        outer = Gather(cube, cube.place(*outer, 0), cube.plan_a)
        last = len(cube.plan_a) - 1
        for step in range(last):
            one.take()
            two.take()
            ahead = one.send(), two.send()
            if step > 0:
                three.take(*ahead)
            ahead = ahead + (three.send(*ahead),)
            if step > 1:
                inner.take(*ahead)
                outer.take(*ahead)
            if step > 0:
                inner.send(*ahead)
                outer.send(*ahead)
        one.take()
        two.take()
        ahead = one.parts[2], two.parts[2]
        three.take(*ahead)
        ahead = ahead + (three.send(*ahead),)
        inner.take(*ahead)
        outer.take(*ahead)
        ahead = ahead + (inner.send(*ahead), outer.send(*ahead))
        gain_full = chip_order(cube, [part[:, 4 * rows :, :rows] for part in one.parts[:2]], plans[0])
        gain_full = gain_full.reshape(-1, 2, 8, rows)[:, :, :3].transpose(2, 0, 1, 3)
        gain_full = gain_full.reshape(3, D)
        first_chunk, second_chunk = one.parts, two.parts
        gain_full = after(gain_full, *ahead)
    else:
        attn_full = lax.all_gather(attn_weights, AXES, axis=1, tiled=True)
        gain_full = lax.all_gather(norm_gains, AXES, axis=1, tiled=True)
        first_chunk, second_chunk = [attn_full[:2]], [attn_full[2:4]]
    gain_one, gain_two, gain_three = [gain_full[k : k + 1].astype(full) for k in range(3)]
    first_low, query, keys, values, self_probs, mixed_low, *weights = by_pair(
        functools.partial(self_part, plans),
        [spot, tokens, gain_one, see_self, lines, *first_chunk, *second_chunk],
        [(tile, low)] * 4 + [(probs, low), (tile, low)] + [square] * 4,
        [],
        (probs, lines.shape),
        "self_part",
    )
    if tiled:
        three.take(mixed_low)
        cross_chunk = three.parts
        inner.take(mixed_low)
        outer.take(mixed_low)
        weights[3] = after(weights[3], inner.send(), outer.send())
    else:
        cross_chunk = [attn_full[4:]]
    (
        middle, second_low, cross_query, memory_keys, memory_values, cross_probs, crossed_low,
        upper, third_low, *cross_weights,
    ) = by_pair(
        functools.partial(cross_part, plans[0]),
        [
            spot, tokens, mixed_low, memory, gain_two, weights[3], gain_three, see_cross,
            *cross_chunk,
        ],
        [(tile, full)] + [(tile, low)] * 4 + [(probs, low), (tile, low), (tile, full), (tile, low)]
        + [square] * 4,
        [],
        (probs,),
        "cross_part",
    )
    attn_full = weights + cross_weights
    if tiled:
        inner.take(third_low)
        outer.take(third_low)
        in_parts, out_parts = inner.parts, outer.parts
    else:
        in_parts = [lax.all_gather(w_in, AXES, axis=0, tiled=True)]
        out_parts = [lax.all_gather(w_out, AXES, axis=0, tiled=True)]
    layer_out, grad_third, *rest = ffn(
        spot, plans[1], third_low, upper, cotangent, in_parts, out_parts
    )
    half = len(rest) // 2
    in_sums = product_sums(cube, cube.plan_b, [part[None] for part in rest[:half]])
    out_sums = product_sums(cube, cube.plan_a, [part[None] for part in rest[half:]])
    grad_upper, grad_cross_branch, grad_crossed, grad_gain_third = fused(
        third_back,
        [(tile, full), (tile, low), (tile, low), ((1, D), full)],
        grad_third,
        upper,
        cotangent,
        gain_three,
        attn_full[7],
    )
    in_sums.take(grad_crossed)
    out_sums.take(grad_crossed)
    grad_crossed = after(grad_crossed, *in_sums.send(), *out_sums.send())
    sums_scratch = [pltpu.VMEM((tile[0], LANES), full)] * 2
    memory_key_low, memory_value_low, grad_middle, grad_self_branch, grad_mixed, *rest = by_pair(
        functools.partial(cross_back, rows),
        [
            core[None],
            cross_query,
            memory_keys,
            memory_values,
            grad_crossed,
            cross_probs,
            second_low,
            memory,
            crossed_low,
            grad_cross_branch,
            middle,
            grad_upper,
            gain_two,
            attn_full[4],
            attn_full[3],
        ],
        [(tile, low)] * 2
        + [(tile, full), (tile, low), (tile, low), ((1, D), full)]
        + product_outs(cube, 4),
        [pltpu.VMEM(tile, low)] + sums_scratch,
        (probs,),
        "cross_back",
    )
    grad_gain_second = rest[0]
    for each in (in_sums, out_sums):
        each.take(grad_mixed)
    arrived = in_sums.terms[-1], out_sums.terms[-1]
    cross_sums = product_sums(cube, cube.plan_a, rest[1:], *arrived)
    started = in_sums.send() + out_sums.send()
    cross_sums.take(*started)
    grad_mixed = after(grad_mixed, *started, *cross_sums.send())
    lots = (PAIRS, 8, 2 * LANES)
    outs = product_outs(cube, 2)
    query_low, key_low, value_low, score_sums, *rest = by_pair(
        functools.partial(self_back, rows),
        [
            core[None],
            query,
            keys,
            values,
            grad_mixed,
            self_probs,
            first_low,
            mixed_low,
            grad_self_branch,
        ],
        [(tile, low)] * 3 + [(lots, full)] + outs[:1] * 2 + outs[1:] * 2,
        sums_scratch,
        (probs, lots),
        "self_back",
    )
    for each in (in_sums, out_sums):
        each.take(query_low)
    arrived = in_sums.terms[-1], out_sums.terms[-1]
    late_sums = product_sums(cube, cube.plan_b, rest[::2], *arrived)
    early_sums = product_sums(cube, cube.plan_a, rest[1::2], *arrived)
    late_sums.take()
    early_sums.take()
    started = early_sums.send() + late_sums.send()
    started = started + out_sums.send(*started) + in_sums.send(*started)
    cross_sums.take(*started)
    started = started + cross_sums.send(*started)
    sums = [early_sums, late_sums, out_sums, in_sums, cross_sums]
    query_low = after(query_low, *started)
    grad_tokens, grad_memory, grad_gain_first = fused(
        last_back,
        [(tile, full), (tile, full), ((1, D), full)],
        query_low,
        key_low,
        value_low,
        memory_key_low,
        memory_value_low,
        tokens,
        grad_middle,
        gain_one,
        *attn_full[:3],
        *attn_full[5:7],
    )
    table_grad = table_sums(score_sums)
    gain_local = jnp.concatenate([grad_gain_first, grad_gain_second, grad_gain_third], axis=0)
    ahead = (grad_tokens,)
    while sums:
        moving, ending = [], []
        for each in sums:
            (moving if each.going() else ending).append(each)
        for each in moving:
            each.take(*ahead)
            ahead = ahead + each.send()
        for each in ending:
            each.take(*ahead)
        sums, ahead = moving, ()
    grad_in, grad_out = in_sums.value()[0], out_sums.value()[0]
    attn_sums = [each.value().reshape(-1, rows, D) for each in (early_sums, late_sums, cross_sums)]
    grad_attn = jnp.concatenate(attn_sums, axis=0)
    attn_squares = [value * value for value in attn_sums]
    square_in = grad_in * grad_in
    square_out = grad_out * grad_out
    row_means = jnp.concatenate(
        [jnp.mean(value, axis=2) for value in attn_squares] + [jnp.mean(square_in, axis=1)[None]], axis=0
    )
    new_row_main = DECAY * row_main + (1.0 - DECAY) * row_means
    new_row_out = DECAY * row_out + (1.0 - DECAY) * jnp.mean(square_out, axis=1)
    column_main = jnp.concatenate(
        [jnp.sum(value, axis=1) for value in attn_squares] + [jnp.sum(square_out, axis=0)[None]], axis=0
    )
    column_in = jnp.sum(square_in, axis=0)
    parts = [column_main, column_in, table_grad, gain_local]
    sizes = [part.size for part in parts]
    width = D // 2
    lines = -(-sum(sizes) // (8 * width)) * 8
    flat = jnp.concatenate([part.reshape(-1, width) for part in parts], axis=0)
    flat = cube.total(jnp.pad(flat, ((0, lines - flat.shape[0]), (0, 0))))
    sums, at = [], 0
    for part, size in zip(parts, sizes):
        sums.append(flat[at : at + size // width].reshape(part.shape))
        at += size // width
    column_main, column_in, grad_table, gain_sums = sums
    grad_gains = lax.dynamic_slice_in_dim(
        gain_sums, cube.me * norm_gains.shape[1], norm_gains.shape[1], 1
    )
    col_means = jnp.concatenate([column_main[:8] / D, column_main[8:] / FF], axis=0)
    new_col_main = DECAY * col_main + (1.0 - DECAY) * col_means
    new_col_in = DECAY * col_in + (1.0 - DECAY) * (column_in / D)
    return (
        layer_out,
        grad_tokens,
        grad_memory,
        grad_attn,
        grad_in,
        grad_out,
        grad_gains,
        grad_table,
        new_row_main,
        new_row_out,
        new_col_main,
        new_col_in,
    )


def solution(mesh):
    placed = (
        P(("wide", "narrow"), None),
        P(("wide", "narrow"), None),
        P(("wide", "narrow"), None),
        P(("wide", "narrow"), None),
        P(("wide", "narrow"), None),
        P(("wide", "narrow"), None),
        P(None, ("wide", "narrow"), None),
        P(("wide", "narrow"), None),
        P(("wide", "narrow"), None),
        P(None, ("wide", "narrow")),
        P(),
        P(None, ("wide", "narrow")),
        P(("wide", "narrow")),
        P(),
        P(),
    )
    return jax.shard_map(
        on_device,
        mesh=mesh,
        in_specs=placed,
        out_specs=(
            P(("wide", "narrow"), None),
            P(("wide", "narrow"), None),
            P(("wide", "narrow"), None),
            P(None, ("wide", "narrow"), None),
            P(("wide", "narrow"), None),
            P(("wide", "narrow"), None),
            P(None, ("wide", "narrow")),
            P(),
            P(None, ("wide", "narrow")),
            P(("wide", "narrow")),
            P(),
            P(),
        ),
        check_vma=False,
    )
```

```python
import functools
import math

import jax
import jax.numpy as jnp
import numpy as np
from jax import lax
from jax.experimental import pallas as pl
from jax.experimental.pallas import tpu as pltpu
from jax.sharding import PartitionSpec as P

D = 768
HEADS = 12
HEAD = 64
FF = 3072
BUCKETS = 32
MAXDIST = 128


EPSILON = 1e-06
DECAY = 0.8
NEGATIVE = -1e30


def thresholds():
    exact_count = BUCKETS // 2
    limits = list(range(1, exact_count + 1))
    for bucket_level in range(exact_count + 1, BUCKETS):
        limits.append(
            int(
                math.ceil(
                    exact_count
                    * (MAXDIST / exact_count) ** ((bucket_level - exact_count) / exact_count)
                )
            )
        )
    return limits


def bucket_table(distance, number_type):
    level_count = jnp.zeros(distance.shape, jnp.int32)
    for threshold in thresholds():
        level_count = level_count + (distance >= threshold).astype(jnp.int32)
    return (level_count[..., None] == jnp.arange(BUCKETS, dtype=jnp.int32)).astype(number_type)


def weight_grad(left_side, gradient):
    return lax.dot_general(
        left_side, gradient, (((0,), (0,)), ((), ())), preferred_element_type=jnp.float32
    )


LANES = 128
GROUP = LANES // HEAD
CUT = 256
VMEM_BYTES = 56 * 1024 * 1024

NT = (((1,), (1,)), ((), ()))
TN = (((0,), (0,)), ((), ()))


def dot(left, right, dims=(((1,), (0,)), ((), ()))):
    return lax.dot_general(left, right, dims, preferred_element_type=jnp.float32)


def spans(rows, causal):
    return [(at, at + CUT if causal else rows) for at in range(0, rows, CUT)]


def lane_mask(head):
    lanes = lax.broadcasted_iota(jnp.int32, (1, LANES), 1)
    return ((lanes // HEAD) == head).astype(jnp.float32)


def only_head(block, head, scale):
    return (block.astype(jnp.float32) * (lane_mask(head) * scale)).astype(jnp.bfloat16)


def near_bias(line_ref, head):
    line = jnp.broadcast_to(line_ref[0, head : head + 1], (LANES, 2 * LANES))
    return pltpu.roll(line, 0, 1, stride=1, stride_axis=0)


def add_bias(scores, bias, at):
    columns = []
    for first in range(0, CUT, LANES):
        rows = []
        for key in range(0, scores.shape[0], LANES):
            apart = at + first - key
            block = scores[key : key + LANES, first : first + LANES]
            if apart >= 2 * LANES:
                block = block + bias[:1, 2 * LANES - 1 :]
            elif apart >= 0:
                block = block + bias[:, apart : apart + LANES]
            rows.append(block)
        columns.append(jnp.concatenate(rows, axis=0))
    return jnp.concatenate(columns, axis=1)


def attend_pair(causal, pair, q_ref, k_ref, v_ref, mask_ref, line_ref, probs_ref, out_ref):
    rows = q_ref.shape[0]
    lanes = pl.ds(pl.multiple_of(pair * LANES, LANES), LANES)
    biases = [near_bias(line_ref, head) for head in range(GROUP)] if causal else None
    for at, depth in spans(rows, causal):
        keys, values = k_ref[:depth, lanes], v_ref[:depth, lanes]
        total = jnp.zeros((CUT, LANES), jnp.float32)
        for head in range(GROUP):
            query = only_head(q_ref[at : at + CUT, lanes], head, HEAD**-0.5)
            scores = dot(keys, query, NT)
            if causal:
                scores = add_bias(scores, biases[head], at)
            scores = scores + mask_ref[:depth, at : at + CUT]
            weights = jnp.exp(scores - jnp.max(scores, axis=0, keepdims=True))
            weights = weights * (1.0 / jnp.sum(weights, axis=0, keepdims=True))
            low = weights.astype(jnp.bfloat16)
            probs_ref[head, :depth, at : at + CUT] = low
            total = total + dot(low, values, TN) * lane_mask(head)
        out_ref[at : at + CUT, lanes] = total.astype(jnp.bfloat16)


def diagonal_sums(block):
    width = block.shape[1]
    slabs = [block[at : at + 8] for at in range(0, block.shape[0], 8)]
    total = slabs[0]
    for at, slab in enumerate(slabs[1:], 1):
        total = total + pltpu.roll(slab, width - 8 * at, 1)
    row = lax.broadcasted_iota(jnp.int32, total.shape, 0)
    for step in (1, 2, 4):
        total = jnp.where((row & step) != 0, pltpu.roll(total, width - step, 1), total)
    return jnp.sum(total, axis=0, keepdims=True)


def attend_back_pair(
    causal, pair, q_ref, k_ref, v_ref, g_ref, probs_ref, dq_ref, dk_ref, dv_ref, sums_ref,
    dk_sum, dv_sum,
):
    rows = q_ref.shape[0]
    lanes = pl.ds(pl.multiple_of(pair * LANES, LANES), LANES)
    dk_sum[...] = jnp.zeros_like(dk_sum)
    dv_sum[...] = jnp.zeros_like(dv_sum)
    near = [[], []]
    far = [[], []]
    for at, depth in spans(rows, causal):
        dq = jnp.zeros((CUT, LANES), jnp.float32)
        for head in range(GROUP):
            grad = only_head(g_ref[at : at + CUT, lanes], head, 1.0)
            query = only_head(q_ref[at : at + CUT, lanes], head, HEAD**-0.5)
            keys = only_head(k_ref[:depth, lanes], head, HEAD**-0.5)
            low = probs_ref[head, :depth, at : at + CUT]
            probs = low.astype(jnp.float32)
            scaled = probs * dot(v_ref[:depth, lanes], grad, NT)
            centre = jnp.sum(scaled, axis=0, keepdims=True)
            grad_scores = (scaled - probs * centre).astype(jnp.bfloat16)
            dv_sum[:depth] += dot(low, grad)
            dk_sum[:depth] += dot(grad_scores, query)
            dq = dq + dot(grad_scores, keys, TN)
            if causal:
                parts = grad_scores.astype(jnp.float32)
                for first in range(0, CUT, LANES):
                    own = at + first
                    column = parts[:, first : first + LANES]
                    if own:
                        before = column[own - LANES : own]
                    else:
                        before = jnp.zeros((LANES, LANES), jnp.float32)
                    near[head].append((column[own : own + LANES], before))
                    if own > LANES:
                        far[head].append(jnp.sum(column[: own - LANES], axis=0, keepdims=True))
        dq_ref[at : at + CUT, lanes] = dq.astype(jnp.bfloat16)
    dk_ref[:, lanes] = dk_sum[...].astype(jnp.bfloat16)
    dv_ref[:, lanes] = dv_sum[...].astype(jnp.bfloat16)
    if causal:
        lines = []
        for head in range(GROUP):
            own = sum(pair[0] for pair in near[head][1:]) + near[head][0][0]
            before = sum(pair[1] for pair in near[head][1:]) + near[head][0][1]
            lines.append(diagonal_sums(jnp.concatenate([own, before], axis=1)))
        for head in range(GROUP):
            line = sum(far[head][1:]) + far[head][0]
            lines.append(jnp.concatenate([line, jnp.zeros_like(line)], axis=1))
        lines.append(jnp.zeros((8 - len(lines), 2 * LANES), jnp.float32))
        sums_ref[0] = jnp.concatenate(lines, axis=0)


def self_mask(segment, key_valid):
    rows = segment.shape[0]
    index = jnp.arange(rows, dtype=jnp.int32)
    distance = index[None, :] - index[:, None]
    allowed = (
        (segment[:, None] == segment[None, :])
        & (distance >= 0)
        & ((key_valid[:, None] > 0) | (distance == 0))
    )
    return jnp.where(allowed, 0.0, NEGATIVE).astype(jnp.float32)


def cross_mask(segment, mem_segment):
    allowed = mem_segment[:, None] == segment[None, :]
    return jnp.where(allowed, 0.0, NEGATIVE).astype(jnp.float32)


def bias_lines(table):
    places = bucket_table(jnp.arange(2 * LANES, dtype=jnp.int32), jnp.float32)
    lines = jnp.einsum(
        "nb,bh->hn", places, table.astype(jnp.float32), precision=lax.Precision.HIGHEST
    )
    lines = lines.reshape(HEADS // GROUP, GROUP, 2 * LANES)
    return jnp.pad(lines, ((0, 0), (0, 8 - GROUP), (0, 0)))


GELU_SCALE = math.sqrt(2.0 / math.pi)
GELU_CUBE = 0.044715
BLOCK = 768
CUTS = FF // (2 * BLOCK)


def chip_of(chip, place, plan):
    bits = [which for group in plan for which in group]
    flip = sum(((place >> k) & 1) << (which - 1) for k, which in enumerate(bits))
    return chip ^ flip


def halves_of(core):
    half = D // 2
    mine = pl.ds(pl.multiple_of(core * half, half), half)
    return mine, pl.ds(pl.multiple_of((1 - core) * half, half), half)


def fill_weight(weight_ref, parts, at, spot_ref, plan):
    if len(parts) == 1:
        weight_ref[...] = parts[0][at]
        return
    blocks, rows = parts[0].shape[0], D // (2 * parts[0].shape[0])
    mine, other = halves_of(spot_ref[1])
    for place in range(2 * blocks):
        chip = chip_of(spot_ref[0], place, plan)
        lines = pl.ds(pl.multiple_of(chip * rows, rows), rows)
        which, block = divmod(place, blocks)
        weight_ref[lines, mine] = parts[which][block, at * rows : (at + 1) * rows]
        weight_ref[lines, other] = parts[2 + which][block, at * rows : (at + 1) * rows]


def sums_order(plan):
    bits = [which for group in plan for which in group]
    count = 1 << len(bits)
    return [sum(((k >> at) & 1) << (which - 1) for at, which in enumerate(bits)) for k in range(count)]


def divided(grads, rows, core):
    grads = grads.reshape(-1, 2, rows, grads.shape[1])
    even, odd = grads[:, 0], grads[:, 1]
    return jnp.where(core == 0, odd, even), jnp.where(core == 0, even, odd)


def ffn_kernel(tiled, plans, spot_ref, third_ref, upper_ref, cot_ref, *refs):
    step = pl.program_id(0)
    if tiled:
        own_in, other_in, out_parts, refs = refs[:2], refs[2:4], refs[4:8], refs[8:]
        layer_ref, gthird_ref, gin_ref, kept_gin_ref, gout_ref, kept_gout_ref = refs[:6]
        total, third_turned, in_block, out_block = refs[6:]
    else:
        in_block, out_block, layer_ref, gthird_ref, gin_ref, gout_ref = refs[:6]
        total, third_turned = refs[6:]

    @pl.when(step == 0)
    def _():
        total[...] = upper_ref[...]
        gthird_ref[...] = jnp.zeros_like(gthird_ref)
        third_turned[...] = third_ref[...].T

    def fill_in(parts):
        blocks, rows, _ = parts[0].shape
        for place in range(2 * blocks):
            chip = chip_of(spot_ref[0], place, plans[1])
            lines = pl.ds(pl.multiple_of(chip * rows, rows), rows)
            in_block[lines, :] = parts[place // blocks][place % blocks]

    if tiled:
        pl.when(step < CUTS)(lambda: fill_in(other_in))
        pl.when(step >= CUTS)(lambda: fill_in(own_in))
        mine, other = halves_of(spot_ref[1])
        rows = out_parts[0].shape[2]
        for place in range(4):
            chip = (spot_ref[0] & 3) ^ place
            lines = pl.ds(pl.multiple_of(chip * rows, rows), rows)
            out_block[lines, mine] = out_parts[place % 2][place // 2, 0]
            out_block[lines, other] = out_parts[2 + place % 2][place // 2, 0]

    inner = dot(third_ref[...], in_block[...])
    square = inner * inner
    slope = jnp.tanh(inner * (GELU_SCALE + (GELU_SCALE * GELU_CUBE) * square))
    half_up = 0.5 + 0.5 * slope
    active = (inner * half_up).astype(jnp.bfloat16)
    total[...] += dot(active, out_block[...])
    grad_active = dot(cot_ref[...], out_block[...], NT)
    bend = (0.5 * inner) * (1.0 - slope * slope)
    bend = bend * (GELU_SCALE + (3.0 * GELU_SCALE * GELU_CUBE) * square)
    grad_inner = (grad_active * (half_up + bend)).astype(jnp.bfloat16)
    gthird_ref[...] += dot(grad_inner, in_block[...], NT)
    grad_in = dot(third_turned[...], grad_inner)
    grad_out = dot(active, cot_ref[...], TN)
    if tiled:
        chips = 2 * own_in[0].shape[0]
        order = sums_order(plans[1])
        parts = divided(grad_in, D // (2 * chips), spot_ref[1])
        for part, result in zip(parts, (gin_ref, kept_gin_ref)):
            part = jnp.concatenate([part[chip] for chip in order], axis=0)
            result[...] = part.astype(jnp.bfloat16)
        parts = divided(grad_out, FF // (2 * chips), spot_ref[1])
        for part, result in zip(parts, (gout_ref, kept_gout_ref)):
            for place in range(4):
                chip = (place >> 1) | ((place & 1) << 1)
                result[place, 0] = part[chip].astype(jnp.bfloat16)
    else:
        gin_ref[...] = grad_in.astype(jnp.bfloat16)
        gout_ref[...] = grad_out.astype(jnp.bfloat16)

    @pl.when(step == 2 * CUTS - 1)
    def _():
        layer_ref[...] = total[...].astype(jnp.bfloat16)


def ffn(spot, plans, third, upper, cotangent, in_parts, out_parts):
    rows = third.shape[0]
    tiled = len(in_parts) > 1

    def block(step, spot_ref):
        return ((1 - spot_ref[1]) * CUTS + step) % (2 * CUTS)

    def line(step, spot_ref):
        flips = block(step, spot_ref) ^ (spot_ref[0] >> 2)
        return (0, (flips >> 1) + 2 * (flips & 1), 0, 0)

    whole = pl.BlockSpec((rows, D), lambda step, spot_ref: (0, 0))
    across = lambda step, spot_ref: (0, block(step, spot_ref))
    down = lambda step, spot_ref: (block(step, spot_ref), 0)
    scratch = [pltpu.VMEM((rows, D), jnp.float32), pltpu.VMEM((D, rows), jnp.bfloat16)]
    if tiled:
        chips, lines, _ = in_parts[0].shape
        late = lambda step, spot_ref: (0, 0, jnp.maximum(step - CUTS, 0))
        early = lambda step, spot_ref: (0, 0, jnp.minimum(step, CUTS - 1))
        in_specs = [pl.BlockSpec((chips, lines, BLOCK), late)] * 2
        in_specs += [pl.BlockSpec((chips, lines, BLOCK), early)] * 2
        out_parts = [part.reshape(2, 4, -1, D // 2) for part in out_parts]
        in_specs += [pl.BlockSpec((2, 1) + out_parts[0].shape[2:], line)] * 4
        out_specs = [pl.BlockSpec((D // 2, BLOCK), across)] * 2
        own = lambda step, spot_ref: (0, (b := block(step, spot_ref)) // 2 + 2 * (b % 2), 0, 0)
        out_specs += [pl.BlockSpec((4, 1, FF // (4 * chips), D), own)] * 2
        shapes = [(D // 2, FF)] * 2 + [(4, 4, FF // (4 * chips), D)] * 2
        scratch += [pltpu.VMEM((D, BLOCK), jnp.bfloat16), pltpu.VMEM((BLOCK, D), jnp.bfloat16)]
    else:
        in_specs = [pl.BlockSpec((D, BLOCK), across), pl.BlockSpec((BLOCK, D), down)]
        out_specs, shapes = in_specs, [(D, FF), (FF, D)]
    return pl.pallas_call(
        functools.partial(ffn_kernel, tiled, plans),
        grid_spec=pltpu.PrefetchScalarGridSpec(
            num_scalar_prefetch=1,
            grid=(2 * CUTS,),
            in_specs=[whole, whole, whole] + in_specs,
            out_specs=[whole, whole] + out_specs,
            scratch_shapes=scratch,
        ),
        out_shape=[
            jax.ShapeDtypeStruct((rows, D), jnp.bfloat16),
            jax.ShapeDtypeStruct((rows, D), jnp.float32),
        ]
        + [jax.ShapeDtypeStruct(shape, jnp.bfloat16) for shape in shapes],
        compiler_params=pltpu.CompilerParams(vmem_limit_bytes=VMEM_BYTES),
        name="ffn",
    )(spot, third, upper, cotangent, *in_parts, *out_parts)


def scale_of(hidden):
    return lax.rsqrt(jnp.mean(hidden * hidden, axis=-1, keepdims=True) + EPSILON)


def norm_back(hidden, gain, grad):
    scale = scale_of(hidden)
    grown = grad * gain
    inner = jnp.mean(grown * hidden, axis=-1, keepdims=True)
    gain_grad = jnp.sum(grad * (hidden * scale), axis=0, keepdims=True)
    return scale * grown - hidden * (scale * scale * scale * inner), gain_grad


def fused(kernel, outs, *args):
    space = pl.BlockSpec(memory_space=pltpu.VMEM)
    return pl.pallas_call(
        kernel,
        in_specs=[space] * len(args),
        out_specs=[space] * len(outs),
        out_shape=[jax.ShapeDtypeStruct(shape, held_as) for shape, held_as in outs],
        compiler_params=pltpu.CompilerParams(vmem_limit_bytes=VMEM_BYTES),

        name=kernel.__name__,
    )(*args)


PAIRS = HEADS // GROUP


def whole_spec(array, space=None):
    rank = len(array.shape)
    return pl.BlockSpec(array.shape, lambda pair: (0,) * rank, pipeline_mode=space)


def by_pair(kernel, args, outs, scratch, by_step, name):
    held = [jax.ShapeDtypeStruct(shape, held_as) for shape, held_as in outs]

    def spec(array, once):
        if len(array.shape) == 3 and array.shape in by_step:
            block = (array.shape[0] // PAIRS,) + array.shape[1:]
            return pl.BlockSpec(block, lambda pair: (pair, 0, 0))
        if len(array.shape) == 1:
            return pl.BlockSpec(memory_space=pltpu.SMEM)
        return whole_spec(array, pl.Buffered(1) if once else None)

    return pl.pallas_call(
        kernel,
        grid=(PAIRS,),
        in_specs=[spec(array, True) for array in args],
        out_specs=[spec(array, False) for array in held],
        out_shape=held,
        scratch_shapes=scratch,
        compiler_params=pltpu.CompilerParams(vmem_limit_bytes=VMEM_BYTES),
        name=name,
    )(*args)


def self_part(plans, spot_ref, tokens_ref, gain_ref, mask_ref, line_ref, *refs):
    count = (len(refs) - 10) // 2
    one, two, refs = refs[:count], refs[count : 2 * count], refs[2 * count :]
    first_ref, q_ref, k_ref, v_ref, probs_ref, mixed_ref, wq_ref, wk_ref, wv_ref, wo_ref = refs
    pair = pl.program_id(0)

    @pl.when(pair == 0)
    def _():
        hidden = tokens_ref[...].astype(jnp.float32)
        first = (hidden * scale_of(hidden) * gain_ref[...]).astype(jnp.bfloat16)
        first_ref[...] = first
        weights = [(wq_ref, one, 0, q_ref), (wk_ref, one, 1, k_ref), (wv_ref, two, 0, v_ref)]
        for weight_ref, parts, at, result in weights:
            fill_weight(weight_ref, parts, at, spot_ref, plans[parts is two])
            result[...] = dot(first, weight_ref[...]).astype(jnp.bfloat16)
        fill_weight(wo_ref, two, 1, spot_ref, plans[1])

    attend_pair(True, pair, q_ref, k_ref, v_ref, mask_ref, line_ref, probs_ref, mixed_ref)


def cross_part(
    plan, spot_ref, tokens_ref, mixed_ref, memory_ref, gain_ref, wso_ref, next_gain_ref, mask_ref,
    *refs,
):
    parts, refs = refs[:-13], refs[-13:]
    middle_ref, second_ref, q_ref, k_ref, v_ref, probs_ref, crossed_ref = refs[:7]
    upper_ref, third_ref, wq_ref, wk_ref, wv_ref, wo_ref = refs[7:]
    pair = pl.program_id(0)

    @pl.when(pair == 0)
    def _():
        for at, weight_ref in enumerate((wq_ref, wk_ref, wv_ref, wo_ref)):
            fill_weight(weight_ref, parts, at, spot_ref, plan)
        middle = tokens_ref[...].astype(jnp.float32) + dot(mixed_ref[...], wso_ref[...])
        middle_ref[...] = middle
        second = (middle * scale_of(middle) * gain_ref[...]).astype(jnp.bfloat16)
        second_ref[...] = second
        q_ref[...] = dot(second, wq_ref[...]).astype(jnp.bfloat16)
        k_ref[...] = dot(memory_ref[...], wk_ref[...]).astype(jnp.bfloat16)
        v_ref[...] = dot(memory_ref[...], wv_ref[...]).astype(jnp.bfloat16)

    attend_pair(False, pair, q_ref, k_ref, v_ref, mask_ref, None, probs_ref, crossed_ref)

    @pl.when(pair == PAIRS - 1)
    def _():
        upper = middle_ref[...] + dot(crossed_ref[...], wo_ref[...])
        upper_ref[...] = upper
        third = upper * scale_of(upper) * next_gain_ref[...]
        third_ref[...] = third.astype(jnp.bfloat16)


def third_back(
    gthird_ref, upper_ref, cot_ref, gain_ref, wo_ref, gupper_ref, branch_ref, gmix_ref, ggain_ref
):
    grad, ggain_ref[...] = norm_back(upper_ref[...], gain_ref[...], gthird_ref[...])
    grad = cot_ref[...].astype(jnp.float32) + grad
    gupper_ref[...] = grad
    low = grad.astype(jnp.bfloat16)
    branch_ref[...] = low
    gmix_ref[...] = dot(low, wo_ref[...], NT).astype(jnp.bfloat16)


def last_back(
    gq_ref, gk_ref, gv_ref, gmk_ref, gmv_ref, tokens_ref, gmiddle_ref, gain_ref,
    wq_ref, wk_ref, wv_ref, wmk_ref, wmv_ref,
    sums_ref, places_ref, ggain_two_ref, ggain_three_ref, gtokens_ref, gmemory_ref, extra_ref,
):
    near = sums_ref[:, :GROUP].reshape(HEADS, 2 * LANES)
    far = jnp.sum(sums_ref[:, GROUP : 2 * GROUP].reshape(HEADS, 2 * LANES), axis=1, keepdims=True)
    high = near.astype(jnp.bfloat16)
    left = near - high.astype(jnp.float32)
    middle = left.astype(jnp.bfloat16)
    least = (left - middle.astype(jnp.float32)).astype(jnp.bfloat16)
    places = places_ref[...]
    lane = lax.broadcasted_iota(jnp.int32, (HEADS, BUCKETS * HEADS), 1)
    head = lax.broadcasted_iota(jnp.int32, (HEADS, BUCKETS * HEADS), 0)
    table = dot(high, places) + dot(middle, places) + dot(least, places)
    table = table + jnp.where(lane // HEADS == BUCKETS - 1, far, 0.0)
    table = jnp.sum(jnp.where(lane % HEADS == head, table, 0.0), axis=0, keepdims=True)
    table = jnp.concatenate([table, jnp.zeros((1, D - table.shape[1]), jnp.float32)], axis=1)
    gmemory_ref[...] = dot(gmk_ref[...], wmk_ref[...], NT) + dot(gmv_ref[...], wmv_ref[...], NT)
    gfirst = dot(gq_ref[...], wq_ref[...], NT) + dot(gk_ref[...], wk_ref[...], NT)
    gfirst = gfirst + dot(gv_ref[...], wv_ref[...], NT)
    hidden = tokens_ref[...].astype(jnp.float32)
    grad, ggain = norm_back(hidden, gain_ref[...], gfirst)
    gtokens_ref[...] = gmiddle_ref[...] + grad
    lines = [ggain, ggain_two_ref[...], ggain_three_ref[...], table] + zero_rows(4)
    extra_ref[...] = jnp.concatenate(lines, axis=0)


def put_products(core_ref, rows, plan, pairs, sent_ref, kept_ref):
    if kept_ref is None:
        for k, (left, right) in enumerate(pairs):
            sent_ref[k] = dot(left[...], right[...], TN).astype(jnp.bfloat16)
        return
    parts = [divided(dot(left[...], right[...], TN), rows, core_ref[0]) for left, right in pairs]
    for which, result in enumerate((sent_ref, kept_ref)):
        for place, chip in enumerate(sums_order(plan)):
            lines = jnp.concatenate([part[which][chip] for part in parts], axis=0)
            result[place] = lines.astype(jnp.bfloat16)


def cross_back(
    rows, plans, core_ref, q_ref, k_ref, v_ref, gcrossed_ref, probs_ref,
    second_ref, memory_ref, crossed_ref, gcross_ref, middle_ref, gupper_ref, gain_ref,
    wq_ref, wso_ref,
    gk_ref, gv_ref, gmiddle_ref, branch_ref, gmix_ref, ggain_ref, sent_ref, *rest,
):
    kept_ref, (gq_ref, dk_sum, dv_sum) = rest[0] if len(rest) == 4 else None, rest[-3:]
    pair = pl.program_id(0)
    attend_back_pair(
        False, pair, q_ref, k_ref, v_ref, gcrossed_ref, probs_ref, gq_ref, gk_ref, gv_ref, None,
        dk_sum, dv_sum,
    )

    @pl.when(pair == PAIRS - 1)
    def _():
        pairs = [
            (second_ref, gq_ref),
            (memory_ref, gk_ref),
            (memory_ref, gv_ref),
            (crossed_ref, gcross_ref),
        ]
        put_products(core_ref, rows, plans[0], pairs, sent_ref, kept_ref)
        gsecond = dot(gq_ref[...], wq_ref[...], NT)
        grad, ggain_ref[...] = norm_back(middle_ref[...], gain_ref[...], gsecond)
        grad = gupper_ref[...] + grad
        gmiddle_ref[...] = grad
        low = grad.astype(jnp.bfloat16)
        branch_ref[...] = low
        gmix_ref[...] = dot(low, wso_ref[...], NT).astype(jnp.bfloat16)


def self_back(
    rows, plans, core_ref, q_ref, k_ref, v_ref, gmixed_ref, probs_ref, first_ref, mixed_ref, gself_ref,
    gq_ref, gk_ref, gv_ref, sums_ref, late_sent_ref, early_sent_ref, *rest,
):
    kept, (dk_sum, dv_sum) = rest[:2] if len(rest) == 4 else (None, None), rest[-2:]
    pair = pl.program_id(0)
    attend_back_pair(
        True, pair, q_ref, k_ref, v_ref, gmixed_ref, probs_ref, gq_ref, gk_ref, gv_ref, sums_ref,
        dk_sum, dv_sum,
    )

    @pl.when(pair == PAIRS - 1)
    def _():
        late = [(first_ref, gv_ref), (mixed_ref, gself_ref)]
        early = [(first_ref, gq_ref), (first_ref, gk_ref)]
        put_products(core_ref, rows, plans[1], late, late_sent_ref, kept[0])
        put_products(core_ref, rows, plans[0], early, early_sent_ref, kept[1])


def term_specs(chains):
    specs = []
    for terms in chains:
        for term, at in terms:

            def place(step, spot_ref, at=at):
                bits = [((spot_ref[0] >> (which - 1)) & 1) * weight for which, _, weight in at]
                return (sum(bits, step), 0, 0)

            specs.append(pl.BlockSpec((1,) + term.shape[1:], place))
    return specs


def row_sums(squares):
    ones = jnp.ones((8, squares.shape[1]), jnp.bfloat16)
    high = squares.astype(jnp.bfloat16)
    left = (squares - high.astype(jnp.float32)).astype(jnp.bfloat16)
    return (dot(ones, high, NT) + dot(ones, left, NT))[:1]


def finish(terms, value_ref, rows_ref):
    count, rows, columns = value_ref.shape
    value = sum(term[0].astype(jnp.float32) for term in terms).reshape(count, rows, columns)
    value_ref[...] = value
    lines = []
    for k in range(count):
        squares = value[k] * value[k]
        rows_ref[k : k + 1] = row_sums(squares) * (1.0 / columns)
        lines.append(jnp.sum(squares, axis=0, keepdims=True))
    return lines


def zero_rows(count):
    return [jnp.zeros((1, D), jnp.float32)] * count


def ffn_last(counts, spot_ref, *refs):
    ins, outs, refs = refs[: counts[0]], refs[counts[0] : sum(counts)], refs[sum(counts) :]
    in_ref, in_rows_ref, out_ref, out_rows_ref, columns_ref = refs
    (wide,) = finish(ins, in_ref, in_rows_ref)
    lines = finish(outs, out_ref, out_rows_ref)
    lines = lines + [wide[:, at : at + D] for at in range(0, FF, D)]
    columns_ref[...] = jnp.concatenate(lines + zero_rows(8 - len(lines)), axis=0)


def cross_last(counts, spot_ref, *refs):
    value_ref, rows_ref, columns_ref = refs[counts[0] :]
    lines = finish(refs[: counts[0]], value_ref, rows_ref)
    columns_ref[...] = jnp.concatenate(lines + zero_rows(8 - len(lines)), axis=0)


def self_last(counts, spot_ref, *refs):
    one, two, refs = refs[: counts[0]], refs[counts[0] : sum(counts)], refs[sum(counts) :]
    cross_ref, ffn_ref, extra_ref, early_ref, early_rows_ref, late_ref, late_rows_ref, all_ref = refs
    lines = finish(one, early_ref, early_rows_ref) + finish(two, late_ref, late_rows_ref)
    all_ref[:8] = jnp.concatenate(lines + [cross_ref[:4]], axis=0)
    all_ref[8:16] = ffn_ref[...]
    all_ref[16:] = extra_ref[...]


def last_terms(kernel, spot, chains, shapes, extras, lines):
    asked = [chain.terms for chain in chains]
    outs = []
    for shape in shapes:
        outs += [shape, shape[:2]]
    outs.append((lines, D))
    whole = lambda shape: pl.BlockSpec(shape, lambda step, _: (0,) * len(shape))
    return pl.pallas_call(
        functools.partial(kernel, [len(terms) for terms in asked]),
        grid_spec=pltpu.PrefetchScalarGridSpec(
            num_scalar_prefetch=1,
            grid=(1,),
            in_specs=term_specs(asked) + [whole(extra.shape) for extra in extras],
            out_specs=[whole(shape) for shape in outs],
        ),
        out_shape=[jax.ShapeDtypeStruct(shape, jnp.float32) for shape in outs],
        compiler_params=pltpu.CompilerParams(vmem_limit_bytes=VMEM_BYTES),
        name=kernel.__name__,
    )(spot, *[term for terms in asked for term, _ in terms], *extras)


AXES = ("wide", "narrow")


def after(value, *others):
    return lax.optimization_barrier((value,) + others)[0]


class Cube:
    def __init__(self):
        self.count = lax.axis_size("wide") * lax.axis_size("narrow")
        self.bits = self.count.bit_length() - 1
        self.me = lax.axis_index("wide") * lax.axis_size("narrow") + lax.axis_index("narrow")
        high = [[which] for which in range(self.bits - 1, 1, -1)]
        self.plan_a = high + [[1]]
        self.plan_b = [[1]] + high

    def bit(self, which):
        return (self.me >> which) & 1

    def swap(self, value, flip):
        return lax.ppermute(value, AXES, [(i, i ^ flip) for i in range(self.count)])

    def place(self, mine, theirs, axis):
        first = self.bit(0) == 0
        return jnp.where(
            first, jnp.concatenate([mine, theirs], axis), jnp.concatenate([theirs, mine], axis)
        )

    def half(self, value, whose):
        size = value.shape[-1] // 2
        return lax.dynamic_slice_in_dim(value, whose * size, size, value.ndim - 1)

    def total(self, value):
        for low in [0] + list(range(1, self.bits, 2)):
            top = 1 if low == 0 else min(2, self.bits - low)
            flips = [flip << low for flip in range(1, 1 << top)]
            value = value + sum(self.swap(value, flip) for flip in flips)
        return value


def flips_of(group):
    picks = range(1, 1 << len(group))
    return [sum(((pick >> k) & 1) << which for k, which in enumerate(group)) for pick in picks]


class Gather:
    def __init__(self, cube, value, plan):
        self.cube, self.plan, self.steps = cube, plan, 0
        self.held, self.parts = value[None], []

    def send(self, *behind):
        sent = after(self.held, *behind) if behind else self.held
        self.theirs = [self.cube.swap(sent, flip) for flip in flips_of(self.plan[self.steps])]
        self.steps += 1
        if self.steps == len(self.plan):
            self.parts = [self.held, self.cube.swap(sent, 1)]
        return sent

    def take(self, *behind):
        theirs = [after(their, *behind) if behind else their for their in self.theirs]
        if self.parts:
            self.parts = [self.parts[0], *theirs, self.parts[1], self.cube.swap(theirs[0], 1)]
        else:
            self.held = jnp.concatenate([self.held, *theirs], axis=0)


def pair_columns(cube, value, *behind):
    core = cube.bit(0)
    sent = cube.half(value, 1 - core)
    theirs = cube.swap(after(sent, *behind) if behind else sent, 1)
    return cube.half(value, core), theirs


class Sums:
    def __init__(self, cube, plan, sent, kept):
        self.cube, self.bits = cube, [which for group in reversed(plan) for which in group]
        self.blocks, self.theirs = cube.count // 2, cube.swap(sent, 1)
        self.terms = [(kept, [])]

    def take(self, *behind):
        self.terms.append((after(self.theirs, *behind) if behind else self.theirs, []))

    def begin(self, at):
        bits = [(self.cube.bit(which) ^ flip) * weight for which, flip, weight in at]
        return sum(bits, jnp.int32(0))

    def send(self):
        which = self.bits.pop(0)
        self.blocks //= 2
        parts = [
            lax.dynamic_slice_in_dim(
                term, self.begin(at + [(which, 1, self.blocks)]), self.blocks, 0
            ).astype(jnp.float32)
            for term, at in self.terms
        ]
        sent = sum(parts).astype(jnp.bfloat16)
        self.terms = [(term, at + [(which, 0, self.blocks)]) for term, at in self.terms]
        self.theirs = self.cube.swap(sent, 1 << which)
        return sent

    def going(self):
        return len(self.bits) > 0


def send_all(chains):
    return tuple([chain.send() for chain in chains])


def whole_tiles(cube):
    return cube.bits == 5


def product_outs(cube, count):
    if whole_tiles(cube):
        return [((cube.count // 2, count * (D // cube.count), D), jnp.bfloat16)] * 2
    return [((count, D, D), jnp.bfloat16)]


def product_sums(cube, plan, parts, *behind):
    chips = cube.count // 2
    if len(parts) == 1:
        count, _, columns = parts[0].shape
        grads = parts[0].reshape(count, chips, 2, -1, columns).transpose(2, 1, 0, 3, 4)
        grads = grads.reshape(2, chips, -1, columns)
        grads = jnp.take(grads, np.array(sums_order(plan)), axis=1)
        core = cube.bit(0)
        parts = [lax.dynamic_index_in_dim(grads, core ^ k, 0, False) for k in (1, 0)]
    sent, kept = [part.reshape(chips, -1, part.shape[-1]) for part in parts]
    return Sums(cube, plan, after(sent, *behind) if behind else sent, kept)


def chip_order(cube, parts, plan):
    places = jnp.concatenate(parts, axis=0)
    chips = chip_of(cube.me >> 1, jnp.arange(places.shape[0], dtype=jnp.int32), plan)
    moves = jnp.arange(places.shape[0], dtype=jnp.int32)[:, None] == chips[None, :]
    moved = jnp.dot(moves.astype(places.dtype), places.reshape(places.shape[0], -1))
    return moved.reshape(places.shape)


def on_device(
    tokens,
    memory,
    cotangent,
    dec_segments,
    enc_segments,
    dec_valid,
    attn_weights,
    w_in,
    w_out,
    norm_gains,
    rel_table,
    row_main,
    row_out,
    col_main,
    col_in,
):
    cube = Cube()
    core = cube.bit(0)
    spot = jnp.stack([cube.me >> 1, core])
    rows = attn_weights.shape[1]
    tiled = whole_tiles(cube)
    plans = cube.plan_a, cube.plan_b
    segment = dec_segments[0]
    see_self = self_mask(segment, dec_valid[0])
    see_cross = cross_mask(segment, enc_segments[0])
    lines = bias_lines(rel_table)
    distances = np.arange(2 * LANES)[:, None]
    places = (distances >= np.array(thresholds())[None, :]).sum(axis=1, keepdims=True)
    places = np.repeat(places == np.arange(BUCKETS)[None, :], HEADS, axis=1)
    places = jnp.asarray(places.astype(np.float32), jnp.bfloat16)
    tile, low, full = tokens.shape, jnp.bfloat16, jnp.float32
    square = ((D, D), low)
    probs = (HEADS, segment.shape[0], segment.shape[0])
    if tiled:
        attn_rows = attn_weights[:4].reshape(-1, D)
        gain_rows = jnp.pad(norm_gains, ((0, 5), (0, D // 2 - rows)))
        sent = jnp.concatenate([cube.half(attn_rows, 1 - core), gain_rows], axis=0)
        theirs = cube.swap(sent, 1)
        pairs = cube.place(
            cube.half(attn_rows, core).reshape(4, rows, -1),
            theirs[: 4 * rows].reshape(4, rows, -1),
            1,
        ).reshape(4 * 2 * rows, -1)
        gain_pair = cube.place(gain_rows, theirs[4 * rows :], 0)
        one = Gather(cube, jnp.concatenate([pairs[: 4 * rows], gain_pair], axis=0), cube.plan_a)
        two = Gather(cube, pairs[4 * rows :], cube.plan_b)
        ahead = one.send(), two.send()
        cross = pair_columns(cube, attn_weights[4:], *ahead)
        inner = pair_columns(cube, w_in, *ahead)
        outer = pair_columns(cube, w_out, *ahead)
        three = Gather(cube, cube.place(*cross, 1).reshape(8 * rows, -1), cube.plan_a)
        inner = Gather(cube, cube.place(*inner, 0), cube.plan_b)
        outer = Gather(cube, cube.place(*outer, 0), cube.plan_a)
        last = len(cube.plan_a) - 1
        for step in range(last):
            one.take()
            two.take()
            ahead = one.send(), two.send()
            if step > 0:
                three.take(*ahead)
            ahead = ahead + (three.send(*ahead),)
            if step > 1:
                inner.take(*ahead)
                outer.take(*ahead)
            if step > 0:
                inner.send(*ahead)
                outer.send(*ahead)
        one.take()
        two.take()
        ahead = one.parts[2], two.parts[2]
        three.take(*ahead)
        ahead = ahead + (three.send(*ahead),)
        inner.take(*ahead)
        outer.take(*ahead)
        ahead = ahead + (inner.send(*ahead), outer.send(*ahead))
        gain_full = chip_order(cube, [part[:, 4 * rows :, :rows] for part in one.parts[:2]], plans[0])
        gain_full = gain_full.reshape(-1, 2, 8, rows)[:, :, :3].transpose(2, 0, 1, 3)
        gain_full = gain_full.reshape(3, D)
        first_chunk, second_chunk = one.parts, two.parts
        gain_full = after(gain_full, *ahead)
    else:
        attn_full = lax.all_gather(attn_weights, AXES, axis=1, tiled=True)
        gain_full = lax.all_gather(norm_gains, AXES, axis=1, tiled=True)
        first_chunk, second_chunk = [attn_full[:2]], [attn_full[2:4]]
    gain_one, gain_two, gain_three = [gain_full[k : k + 1].astype(full) for k in range(3)]
    first_low, query, keys, values, self_probs, mixed_low, *weights = by_pair(
        functools.partial(self_part, plans),
        [spot, tokens, gain_one, see_self, lines, *first_chunk, *second_chunk],
        [(tile, low)] * 4 + [(probs, low), (tile, low)] + [square] * 4,
        [],
        (probs, lines.shape),
        "self_part",
    )
    if tiled:
        three.take(mixed_low)
        cross_chunk = three.parts
        inner.take(mixed_low)
        outer.take(mixed_low)
        weights[3] = after(weights[3], inner.send(), outer.send())
    else:
        cross_chunk = [attn_full[4:]]
    (
        middle, second_low, cross_query, memory_keys, memory_values, cross_probs, crossed_low,
        upper, third_low, *cross_weights,
    ) = by_pair(
        functools.partial(cross_part, plans[0]),
        [
            spot, tokens, mixed_low, memory, gain_two, weights[3], gain_three, see_cross,
            *cross_chunk,
        ],
        [(tile, full)] + [(tile, low)] * 4 + [(probs, low), (tile, low), (tile, full), (tile, low)]
        + [square] * 4,
        [],
        (probs,),
        "cross_part",
    )
    attn_full = weights + cross_weights
    if tiled:
        inner.take(third_low)
        outer.take(third_low)
        in_parts, out_parts = inner.parts, outer.parts
    else:
        in_parts = [lax.all_gather(w_in, AXES, axis=0, tiled=True)]
        out_parts = [lax.all_gather(w_out, AXES, axis=0, tiled=True)]
    layer_out, grad_third, *rest = ffn(
        spot, plans, third_low, upper, cotangent, in_parts, out_parts
    )
    half = len(rest) // 2
    parts = rest if tiled else [part[None] for part in rest]
    in_sums = product_sums(cube, cube.plan_b, parts[:half])
    out_sums = product_sums(cube, cube.plan_a, parts[half:])
    grad_upper, grad_cross_branch, grad_crossed, grad_gain_third = fused(
        third_back,
        [(tile, full), (tile, low), (tile, low), ((1, D), full)],
        grad_third,
        upper,
        cotangent,
        gain_three,
        attn_full[7],
    )
    in_sums.take(grad_crossed)
    out_sums.take(grad_crossed)
    grad_crossed = after(grad_crossed, *send_all((in_sums, out_sums)))
    sums_scratch = [pltpu.VMEM((tile[0], LANES), full)] * 2
    memory_key_low, memory_value_low, grad_middle, grad_self_branch, grad_mixed, *rest = by_pair(
        functools.partial(cross_back, rows, plans),
        [
            core[None],
            cross_query,
            memory_keys,
            memory_values,
            grad_crossed,
            cross_probs,
            second_low,
            memory,
            crossed_low,
            grad_cross_branch,
            middle,
            grad_upper,
            gain_two,
            attn_full[4],
            attn_full[3],
        ],
        [(tile, low)] * 2
        + [(tile, full), (tile, low), (tile, low), ((1, D), full)]
        + product_outs(cube, 4),
        [pltpu.VMEM(tile, low)] + sums_scratch,
        (probs,),
        "cross_back",
    )
    grad_gain_second = rest[0]
    for each in (in_sums, out_sums):
        each.take(grad_mixed)
    arrived = in_sums.terms[-1][0], out_sums.terms[-1][0]
    cross_sums = product_sums(cube, cube.plan_a, rest[1:], *arrived)
    started = send_all((in_sums, out_sums))
    cross_sums.take(*started)
    grad_mixed = after(grad_mixed, *started, *send_all((cross_sums,)))
    lots = (PAIRS, 8, 2 * LANES)
    outs = product_outs(cube, 2)
    query_low, key_low, value_low, score_sums, *rest = by_pair(
        functools.partial(self_back, rows, plans),
        [
            core[None],
            query,
            keys,
            values,
            grad_mixed,
            self_probs,
            first_low,
            mixed_low,
            grad_self_branch,
        ],
        [(tile, low)] * 3 + [(lots, full)] + outs[:1] * 2 + outs[1:] * 2,
        sums_scratch,
        (probs, lots),
        "self_back",
    )
    for each in (in_sums, out_sums):
        each.take(query_low)
    arrived = in_sums.terms[-1][0], out_sums.terms[-1][0]
    late_sums = product_sums(cube, cube.plan_b, rest[::2], *arrived)
    early_sums = product_sums(cube, cube.plan_a, rest[1::2], *arrived)
    cross_sums.take(query_low)
    started = send_all((out_sums, in_sums, cross_sums))
    late_sums.take(*started)
    early_sums.take(*started)
    started = started + send_all((early_sums, late_sums))
    query_low = after(query_low, *started)
    grad_tokens, grad_memory, extra = fused(
        last_back,
        [(tile, full), (tile, full), ((8, D), full)],
        query_low,
        key_low,
        value_low,
        memory_key_low,
        memory_value_low,
        tokens,
        grad_middle,
        gain_one,
        *attn_full[:3],
        *attn_full[5:7],
        score_sums,
        places,
        grad_gain_second,
        grad_gain_third,
    )

    def move(chains, *behind):
        for each in chains:
            each.take(*behind)
        return send_all(chains)

    started = move((early_sums, late_sums, out_sums, in_sums), grad_tokens)
    move((cross_sums,), *started)
    started = move((early_sums, late_sums))
    while in_sums.going():
        move((out_sums, in_sums))
    while cross_sums.going():
        started = started + move((cross_sums,), *started)
    for each in (out_sums, in_sums):
        each.take(*started)
    grad_in, in_rows, grad_out, out_rows, ffn_columns = last_terms(
        ffn_last, spot, [in_sums, out_sums], [(1, rows, FF), (1, FF // cube.count, D)], [], 8
    )
    while early_sums.going():
        move((early_sums, late_sums), ffn_columns)
    cross_sums.take()
    cross_grads, cross_rows, cross_columns = last_terms(
        cross_last, spot, [cross_sums], [(4, rows, D)], [], 8
    )
    early_sums.take(cross_columns)
    late_sums.take(cross_columns)
    early_grads, early_rows, late_grads, late_rows, columns = last_terms(
        self_last,
        spot,
        [early_sums, late_sums],
        [(2, rows, D)] * 2,
        [cross_columns, ffn_columns, extra],
        24,
    )
    grad_attn = jnp.concatenate([early_grads, late_grads, cross_grads], axis=0)
    grad_in, grad_out = grad_in[0], grad_out[0]
    row_means = jnp.concatenate([early_rows, late_rows, cross_rows, in_rows], axis=0)
    new_row_main = DECAY * row_main + (1.0 - DECAY) * row_means
    new_row_out = DECAY * row_out + (1.0 - DECAY) * out_rows[0]
    columns = cube.total(columns)
    col_means = jnp.concatenate([columns[:8] / D, columns[8:9] / FF], axis=0)
    new_col_main = DECAY * col_main + (1.0 - DECAY) * col_means
    new_col_in = DECAY * col_in + (1.0 - DECAY) * (columns[9 : 9 + FF // D].reshape(FF) / D)
    grad_gains = lax.dynamic_slice_in_dim(columns[16:19], cube.me * rows, rows, 1)
    grad_table = columns[19, : BUCKETS * HEADS].reshape(BUCKETS, HEADS)
    return (
        layer_out,
        grad_tokens,
        grad_memory,
        grad_attn,
        grad_in,
        grad_out,
        grad_gains,
        grad_table,
        new_row_main,
        new_row_out,
        new_col_main,
        new_col_in,
    )


def solution(mesh):
    placed = (
        P(("wide", "narrow"), None),
        P(("wide", "narrow"), None),
        P(("wide", "narrow"), None),
        P(("wide", "narrow"), None),
        P(("wide", "narrow"), None),
        P(("wide", "narrow"), None),
        P(None, ("wide", "narrow"), None),
        P(("wide", "narrow"), None),
        P(("wide", "narrow"), None),
        P(None, ("wide", "narrow")),
        P(),
        P(None, ("wide", "narrow")),
        P(("wide", "narrow")),
        P(),
        P(),
    )
    return jax.shard_map(
        on_device,
        mesh=mesh,
        in_specs=placed,
        out_specs=(
            P(("wide", "narrow"), None),
            P(("wide", "narrow"), None),
            P(("wide", "narrow"), None),
            P(None, ("wide", "narrow"), None),
            P(("wide", "narrow"), None),
            P(("wide", "narrow"), None),
            P(None, ("wide", "narrow")),
            P(),
            P(None, ("wide", "narrow")),
            P(("wide", "narrow")),
            P(),
            P(),
        ),
        check_vma=False,
    )
```

```python
import functools
import math

import jax
import jax.numpy as jnp
import numpy as np
from jax import lax
from jax.experimental import pallas as pl
from jax.experimental.pallas import tpu as pltpu
from jax.sharding import PartitionSpec as P

D = 768
HEADS = 12
HEAD = 64
FF = 3072
BUCKETS = 32
MAXDIST = 128


EPSILON = 1e-06
DECAY = 0.8
NEGATIVE = -1e30


def thresholds():
    exact_count = BUCKETS // 2
    limits = list(range(1, exact_count + 1))
    for bucket_level in range(exact_count + 1, BUCKETS):
        limits.append(
            int(
                math.ceil(
                    exact_count
                    * (MAXDIST / exact_count) ** ((bucket_level - exact_count) / exact_count)
                )
            )
        )
    return limits


def bucket_table(distance, number_type):
    level_count = jnp.zeros(distance.shape, jnp.int32)
    for threshold in thresholds():
        level_count = level_count + (distance >= threshold).astype(jnp.int32)
    return (level_count[..., None] == jnp.arange(BUCKETS, dtype=jnp.int32)).astype(number_type)


def weight_grad(left_side, gradient):
    return lax.dot_general(
        left_side, gradient, (((0,), (0,)), ((), ())), preferred_element_type=jnp.float32
    )


LANES = 128
GROUP = LANES // HEAD
CUT = 256
VMEM_BYTES = 56 * 1024 * 1024

NT = (((1,), (1,)), ((), ()))
TN = (((0,), (0,)), ((), ()))


def dot(left, right, dims=(((1,), (0,)), ((), ()))):
    return lax.dot_general(left, right, dims, preferred_element_type=jnp.float32)


def spans(rows, causal):
    return [(at, at + CUT if causal else rows) for at in range(0, rows, CUT)]


def lane_mask(head):
    lanes = lax.broadcasted_iota(jnp.int32, (1, LANES), 1)
    return ((lanes // HEAD) == head).astype(jnp.float32)


def only_head(block, head, scale):
    return (block.astype(jnp.float32) * (lane_mask(head) * scale)).astype(jnp.bfloat16)


def near_bias(line_ref, head):
    line = jnp.broadcast_to(line_ref[0, head : head + 1], (LANES, 2 * LANES))
    return pltpu.roll(line, 0, 1, stride=1, stride_axis=0)


def add_bias(scores, bias, at):
    columns = []
    for first in range(0, CUT, LANES):
        rows = []
        for key in range(0, scores.shape[0], LANES):
            apart = at + first - key
            block = scores[key : key + LANES, first : first + LANES]
            if apart >= 2 * LANES:
                block = block + bias[:1, 2 * LANES - 1 :]
            elif apart >= 0:
                block = block + bias[:, apart : apart + LANES]
            rows.append(block)
        columns.append(jnp.concatenate(rows, axis=0))
    return jnp.concatenate(columns, axis=1)


def attend_pair(causal, pair, q_ref, k_ref, v_ref, mask_ref, line_ref, probs_ref, out_ref):
    rows = q_ref.shape[0]
    lanes = pl.ds(pl.multiple_of(pair * LANES, LANES), LANES)
    biases = [near_bias(line_ref, head) for head in range(GROUP)] if causal else None
    for at, depth in spans(rows, causal):
        keys, values = k_ref[:depth, lanes], v_ref[:depth, lanes]
        total = jnp.zeros((CUT, LANES), jnp.float32)
        for head in range(GROUP):
            query = only_head(q_ref[at : at + CUT, lanes], head, HEAD**-0.5)
            scores = dot(keys, query, NT)
            if causal:
                scores = add_bias(scores, biases[head], at)
            scores = scores + mask_ref[:depth, at : at + CUT]
            weights = jnp.exp(scores - jnp.max(scores, axis=0, keepdims=True))
            weights = weights * (1.0 / jnp.sum(weights, axis=0, keepdims=True))
            low = weights.astype(jnp.bfloat16)
            probs_ref[head, :depth, at : at + CUT] = low
            total = total + dot(low, values, TN) * lane_mask(head)
        out_ref[at : at + CUT, lanes] = total.astype(jnp.bfloat16)


def diagonal_sums(block):
    width = block.shape[1]
    slabs = [block[at : at + 8] for at in range(0, block.shape[0], 8)]
    total = slabs[0]
    for at, slab in enumerate(slabs[1:], 1):
        total = total + pltpu.roll(slab, width - 8 * at, 1)
    row = lax.broadcasted_iota(jnp.int32, total.shape, 0)
    for step in (1, 2, 4):
        total = jnp.where((row & step) != 0, pltpu.roll(total, width - step, 1), total)
    return jnp.sum(total, axis=0, keepdims=True)


def attend_back_pair(
    causal, pair, q_ref, k_ref, v_ref, g_ref, probs_ref, dq_ref, dk_ref, dv_ref, sums_ref,
    dk_sum, dv_sum,
):
    rows = q_ref.shape[0]
    lanes = pl.ds(pl.multiple_of(pair * LANES, LANES), LANES)
    dk_sum[...] = jnp.zeros_like(dk_sum)
    dv_sum[...] = jnp.zeros_like(dv_sum)
    near = [[], []]
    far = [[], []]
    for at, depth in spans(rows, causal):
        dq = jnp.zeros((CUT, LANES), jnp.float32)
        for head in range(GROUP):
            grad = only_head(g_ref[at : at + CUT, lanes], head, 1.0)
            query = only_head(q_ref[at : at + CUT, lanes], head, HEAD**-0.5)
            keys = only_head(k_ref[:depth, lanes], head, HEAD**-0.5)
            low = probs_ref[head, :depth, at : at + CUT]
            probs = low.astype(jnp.float32)
            scaled = probs * dot(v_ref[:depth, lanes], grad, NT)
            centre = jnp.sum(scaled, axis=0, keepdims=True)
            grad_scores = (scaled - probs * centre).astype(jnp.bfloat16)
            dv_sum[:depth] += dot(low, grad)
            dk_sum[:depth] += dot(grad_scores, query)
            dq = dq + dot(grad_scores, keys, TN)
            if causal:
                parts = grad_scores.astype(jnp.float32)
                for first in range(0, CUT, LANES):
                    own = at + first
                    column = parts[:, first : first + LANES]
                    if own:
                        before = column[own - LANES : own]
                    else:
                        before = jnp.zeros((LANES, LANES), jnp.float32)
                    near[head].append((column[own : own + LANES], before))
                    if own > LANES:
                        far[head].append(jnp.sum(column[: own - LANES], axis=0, keepdims=True))
        dq_ref[at : at + CUT, lanes] = dq.astype(jnp.bfloat16)
    dk_ref[:, lanes] = dk_sum[...].astype(jnp.bfloat16)
    dv_ref[:, lanes] = dv_sum[...].astype(jnp.bfloat16)
    if causal:
        lines = []
        for head in range(GROUP):
            own = sum(pair[0] for pair in near[head][1:]) + near[head][0][0]
            before = sum(pair[1] for pair in near[head][1:]) + near[head][0][1]
            lines.append(diagonal_sums(jnp.concatenate([own, before], axis=1)))
        for head in range(GROUP):
            line = sum(far[head][1:]) + far[head][0]
            lines.append(jnp.concatenate([line, jnp.zeros_like(line)], axis=1))
        lines.append(jnp.zeros((8 - len(lines), 2 * LANES), jnp.float32))
        sums_ref[0] = jnp.concatenate(lines, axis=0)


def self_mask(segment, key_valid):
    rows = segment.shape[0]
    index = jnp.arange(rows, dtype=jnp.int32)
    distance = index[None, :] - index[:, None]
    allowed = (
        (segment[:, None] == segment[None, :])
        & (distance >= 0)
        & ((key_valid[:, None] > 0) | (distance == 0))
    )
    return jnp.where(allowed, 0.0, NEGATIVE).astype(jnp.float32)


def cross_mask(segment, mem_segment):
    allowed = mem_segment[:, None] == segment[None, :]
    return jnp.where(allowed, 0.0, NEGATIVE).astype(jnp.float32)


def bias_lines(table):
    places = bucket_table(jnp.arange(2 * LANES, dtype=jnp.int32), jnp.float32)
    lines = jnp.einsum(
        "nb,bh->hn", places, table.astype(jnp.float32), precision=lax.Precision.HIGHEST
    )
    lines = lines.reshape(HEADS // GROUP, GROUP, 2 * LANES)
    return jnp.pad(lines, ((0, 0), (0, 8 - GROUP), (0, 0)))


GELU_SCALE = math.sqrt(2.0 / math.pi)
GELU_CUBE = 0.044715
BLOCK = 768
CUTS = FF // (2 * BLOCK)


def chip_of(chip, place, plan):
    bits = [which for group in plan for which in group]
    flip = sum(((place >> k) & 1) << (which - 1) for k, which in enumerate(bits))
    return chip ^ flip


def halves_of(core):
    half = D // 2
    mine = pl.ds(pl.multiple_of(core * half, half), half)
    return mine, pl.ds(pl.multiple_of((1 - core) * half, half), half)


def fill_weight(weight_ref, parts, at, spot_ref, plan):
    if len(parts) == 1:
        weight_ref[...] = parts[0][at]
        return
    blocks, rows = parts[0].shape[0], D // (2 * parts[0].shape[0])
    mine, other = halves_of(spot_ref[1])
    for place in range(2 * blocks):
        chip = chip_of(spot_ref[0], place, plan)
        lines = pl.ds(pl.multiple_of(chip * rows, rows), rows)
        which, block = divmod(place, blocks)
        weight_ref[lines, mine] = parts[which][block, at * rows : (at + 1) * rows]
        weight_ref[lines, other] = parts[2 + which][block, at * rows : (at + 1) * rows]


def sums_order(plan):
    bits = [which for group in plan for which in group]
    count = 1 << len(bits)
    return [sum(((k >> at) & 1) << (which - 1) for at, which in enumerate(bits)) for k in range(count)]


def divided(grads, rows, core):
    grads = grads.reshape(-1, 2, rows, grads.shape[1])
    even, odd = grads[:, 0], grads[:, 1]
    return jnp.where(core == 0, odd, even), jnp.where(core == 0, even, odd)


def ffn_kernel(tiled, plans, spot_ref, third_ref, upper_ref, cot_ref, *refs):
    step = pl.program_id(0)
    if tiled:
        own_in, other_in, out_parts, refs = refs[:2], refs[2:4], refs[4:8], refs[8:]
        layer_ref, gthird_ref, gin_ref, kept_gin_ref, gout_ref, kept_gout_ref = refs[:6]
        total, third_turned, in_block, out_block = refs[6:]
    else:
        in_block, out_block, layer_ref, gthird_ref, gin_ref, gout_ref = refs[:6]
        total, third_turned = refs[6:]

    @pl.when(step == 0)
    def _():
        total[...] = upper_ref[...]
        gthird_ref[...] = jnp.zeros_like(gthird_ref)
        third_turned[...] = third_ref[...].T

    def fill_in(parts):
        blocks, rows, _ = parts[0].shape
        for place in range(2 * blocks):
            chip = chip_of(spot_ref[0], place, plans[1])
            lines = pl.ds(pl.multiple_of(chip * rows, rows), rows)
            in_block[lines, :] = parts[place // blocks][place % blocks]

    if tiled:
        pl.when(step < CUTS)(lambda: fill_in(other_in))
        pl.when(step >= CUTS)(lambda: fill_in(own_in))
        mine, other = halves_of(spot_ref[1])
        rows = out_parts[0].shape[2]
        for place in range(4):
            chip = (spot_ref[0] & 3) ^ place
            lines = pl.ds(pl.multiple_of(chip * rows, rows), rows)
            out_block[lines, mine] = out_parts[place % 2][place // 2, 0]
            out_block[lines, other] = out_parts[2 + place % 2][place // 2, 0]

    inner = dot(third_ref[...], in_block[...])
    square = inner * inner
    slope = jnp.tanh(inner * (GELU_SCALE + (GELU_SCALE * GELU_CUBE) * square))
    half_up = 0.5 + 0.5 * slope
    active = (inner * half_up).astype(jnp.bfloat16)
    total[...] += dot(active, out_block[...])
    grad_active = dot(cot_ref[...], out_block[...], NT)
    bend = (0.5 * inner) * (1.0 - slope * slope)
    bend = bend * (GELU_SCALE + (3.0 * GELU_SCALE * GELU_CUBE) * square)
    grad_inner = (grad_active * (half_up + bend)).astype(jnp.bfloat16)
    gthird_ref[...] += dot(grad_inner, in_block[...], NT)
    grad_in = dot(third_turned[...], grad_inner)
    grad_out = dot(active, cot_ref[...], TN)
    if tiled:
        chips = 2 * own_in[0].shape[0]
        order = sums_order(plans[1])
        parts = divided(grad_in, D // (2 * chips), spot_ref[1])
        for part, result in zip(parts, (gin_ref, kept_gin_ref)):
            part = jnp.concatenate([part[chip] for chip in order], axis=0)
            result[...] = part.astype(jnp.bfloat16)
        parts = divided(grad_out, FF // (2 * chips), spot_ref[1])
        for part, result in zip(parts, (gout_ref, kept_gout_ref)):
            for place in range(4):
                chip = (place >> 1) | ((place & 1) << 1)
                result[place, 0] = part[chip].astype(jnp.bfloat16)
    else:
        gin_ref[...] = grad_in.astype(jnp.bfloat16)
        gout_ref[...] = grad_out.astype(jnp.bfloat16)

    @pl.when(step == 2 * CUTS - 1)
    def _():
        layer_ref[...] = total[...].astype(jnp.bfloat16)


def ffn(spot, plans, third, upper, cotangent, in_parts, out_parts):
    rows = third.shape[0]
    tiled = len(in_parts) > 1

    def block(step, spot_ref):
        return ((1 - spot_ref[1]) * CUTS + step) % (2 * CUTS)

    def line(step, spot_ref):
        flips = block(step, spot_ref) ^ (spot_ref[0] >> 2)
        return (0, (flips >> 1) + 2 * (flips & 1), 0, 0)

    whole = pl.BlockSpec((rows, D), lambda step, spot_ref: (0, 0))
    across = lambda step, spot_ref: (0, block(step, spot_ref))
    down = lambda step, spot_ref: (block(step, spot_ref), 0)
    scratch = [pltpu.VMEM((rows, D), jnp.float32), pltpu.VMEM((D, rows), jnp.bfloat16)]
    if tiled:
        chips, lines, _ = in_parts[0].shape
        late = lambda step, spot_ref: (0, 0, jnp.maximum(step - CUTS, 0))
        early = lambda step, spot_ref: (0, 0, jnp.minimum(step, CUTS - 1))
        in_specs = [pl.BlockSpec((chips, lines, BLOCK), late)] * 2
        in_specs += [pl.BlockSpec((chips, lines, BLOCK), early)] * 2
        out_parts = [part.reshape(2, 4, -1, D // 2) for part in out_parts]
        in_specs += [pl.BlockSpec((2, 1) + out_parts[0].shape[2:], line)] * 4
        out_specs = [pl.BlockSpec((D // 2, BLOCK), across)] * 2
        own = lambda step, spot_ref: (0, (b := block(step, spot_ref)) // 2 + 2 * (b % 2), 0, 0)
        out_specs += [pl.BlockSpec((4, 1, FF // (4 * chips), D), own)] * 2
        shapes = [(D // 2, FF)] * 2 + [(4, 4, FF // (4 * chips), D)] * 2
        scratch += [pltpu.VMEM((D, BLOCK), jnp.bfloat16), pltpu.VMEM((BLOCK, D), jnp.bfloat16)]
    else:
        in_specs = [pl.BlockSpec((D, BLOCK), across), pl.BlockSpec((BLOCK, D), down)]
        out_specs, shapes = in_specs, [(D, FF), (FF, D)]
    return pl.pallas_call(
        functools.partial(ffn_kernel, tiled, plans),
        grid_spec=pltpu.PrefetchScalarGridSpec(
            num_scalar_prefetch=1,
            grid=(2 * CUTS,),
            in_specs=[whole, whole, whole] + in_specs,
            out_specs=[whole, whole] + out_specs,
            scratch_shapes=scratch,
        ),
        out_shape=[
            jax.ShapeDtypeStruct((rows, D), jnp.bfloat16),
            jax.ShapeDtypeStruct((rows, D), jnp.float32),
        ]
        + [jax.ShapeDtypeStruct(shape, jnp.bfloat16) for shape in shapes],
        compiler_params=pltpu.CompilerParams(vmem_limit_bytes=VMEM_BYTES),
        name="ffn",
    )(spot, third, upper, cotangent, *in_parts, *out_parts)


def scale_of(hidden):
    return lax.rsqrt(jnp.mean(hidden * hidden, axis=-1, keepdims=True) + EPSILON)


def norm_back(hidden, gain, grad):
    scale = scale_of(hidden)
    grown = grad * gain
    inner = jnp.mean(grown * hidden, axis=-1, keepdims=True)
    gain_grad = jnp.sum(grad * (hidden * scale), axis=0, keepdims=True)
    return scale * grown - hidden * (scale * scale * scale * inner), gain_grad


def fused(kernel, outs, *args):
    space = pl.BlockSpec(memory_space=pltpu.VMEM)
    return pl.pallas_call(
        kernel,
        in_specs=[space] * len(args),
        out_specs=[space] * len(outs),
        out_shape=[jax.ShapeDtypeStruct(shape, held_as) for shape, held_as in outs],
        compiler_params=pltpu.CompilerParams(vmem_limit_bytes=VMEM_BYTES),

        name=kernel.__name__,
    )(*args)


PAIRS = HEADS // GROUP


def whole_spec(array, space=None):
    rank = len(array.shape)
    return pl.BlockSpec(array.shape, lambda pair: (0,) * rank, pipeline_mode=space)


def by_pair(kernel, args, outs, scratch, by_step, name, late=(), early=()):
    held = [jax.ShapeDtypeStruct(shape, held_as) for shape, held_as in outs]
    beside = pl.BlockSpec(memory_space=pl.ANY)
    buffers = [args[k] for k in late] + [held[k] for k in early]
    count = len(args) + len(held) + len(scratch)

    def body(*refs):
        pair = pl.program_id(0)
        refs, places, arrived = list(refs[:count]), refs[count:-1], refs[-1]
        wanted = list(late) + [len(args) + k for k in early]
        copies = []
        for k, (at, place) in enumerate(zip(wanted, places)):
            ends = (refs[at], place) if k < len(late) else (place, refs[at])
            copies.append(pltpu.make_async_copy(*ends, arrived.at[k]))
            refs[at] = place
        loads, stores = copies[: len(late)], copies[len(late) :]

        @pl.when(pair == 0)
        def _():
            for copy in loads:
                copy.start()

        @pl.when(pair == PAIRS - 1)
        def _():
            for copy in loads:
                copy.wait()

        kernel(*refs)

        @pl.when(pair == 0)
        def _():
            for copy in stores:
                copy.start()

        @pl.when(pair == PAIRS - 1)
        def _():
            for copy in stores:
                copy.wait()

    def spec(array, once):
        if len(array.shape) == 3 and array.shape in by_step:
            block = (array.shape[0] // PAIRS,) + array.shape[1:]
            return pl.BlockSpec(block, lambda pair: (pair, 0, 0))
        if len(array.shape) == 1:
            return pl.BlockSpec(memory_space=pltpu.SMEM)
        return whole_spec(array, pl.Buffered(1) if once else None)

    in_specs = [beside if k in late else spec(array, True) for k, array in enumerate(args)]
    out_specs = [beside if k in early else spec(array, False) for k, array in enumerate(held)]
    if not buffers:
        body = kernel
    else:
        scratch = scratch + [pltpu.VMEM(array.shape, array.dtype) for array in buffers]
        scratch.append(pltpu.SemaphoreType.DMA((len(buffers),)))
    return pl.pallas_call(
        body,
        grid=(PAIRS,),
        in_specs=in_specs,
        out_specs=out_specs,
        out_shape=held,
        scratch_shapes=scratch,
        compiler_params=pltpu.CompilerParams(vmem_limit_bytes=VMEM_BYTES),
        name=name,
    )(*args)


def self_part(plans, spot_ref, tokens_ref, gain_ref, mask_ref, line_ref, *refs):
    count = (len(refs) - 10) // 2
    one, two, refs = refs[:count], refs[count : 2 * count], refs[2 * count :]
    first_ref, q_ref, k_ref, v_ref, probs_ref, mixed_ref, wq_ref, wk_ref, wv_ref, wo_ref = refs
    pair = pl.program_id(0)

    @pl.when(pair == 0)
    def _():
        hidden = tokens_ref[...].astype(jnp.float32)
        first = (hidden * scale_of(hidden) * gain_ref[...]).astype(jnp.bfloat16)
        first_ref[...] = first
        weights = [(wq_ref, one, 0, q_ref), (wk_ref, one, 1, k_ref), (wv_ref, two, 0, v_ref)]
        for weight_ref, parts, at, result in weights:
            fill_weight(weight_ref, parts, at, spot_ref, plans[parts is two])
            result[...] = dot(first, weight_ref[...]).astype(jnp.bfloat16)
        fill_weight(wo_ref, two, 1, spot_ref, plans[1])

    attend_pair(True, pair, q_ref, k_ref, v_ref, mask_ref, line_ref, probs_ref, mixed_ref)


def cross_part(
    plan, spot_ref, tokens_ref, mixed_ref, memory_ref, gain_ref, wso_ref, next_gain_ref, mask_ref,
    *refs,
):
    parts, refs = refs[:-13], refs[-13:]
    middle_ref, second_ref, q_ref, k_ref, v_ref, probs_ref, crossed_ref = refs[:7]
    upper_ref, third_ref, wq_ref, wk_ref, wv_ref, wo_ref = refs[7:]
    pair = pl.program_id(0)

    @pl.when(pair == 0)
    def _():
        for at, weight_ref in enumerate((wq_ref, wk_ref, wv_ref, wo_ref)):
            fill_weight(weight_ref, parts, at, spot_ref, plan)
        middle = tokens_ref[...].astype(jnp.float32) + dot(mixed_ref[...], wso_ref[...])
        middle_ref[...] = middle
        second = (middle * scale_of(middle) * gain_ref[...]).astype(jnp.bfloat16)
        second_ref[...] = second
        q_ref[...] = dot(second, wq_ref[...]).astype(jnp.bfloat16)
        k_ref[...] = dot(memory_ref[...], wk_ref[...]).astype(jnp.bfloat16)
        v_ref[...] = dot(memory_ref[...], wv_ref[...]).astype(jnp.bfloat16)

    attend_pair(False, pair, q_ref, k_ref, v_ref, mask_ref, None, probs_ref, crossed_ref)

    @pl.when(pair == PAIRS - 1)
    def _():
        upper = middle_ref[...] + dot(crossed_ref[...], wo_ref[...])
        upper_ref[...] = upper
        third = upper * scale_of(upper) * next_gain_ref[...]
        third_ref[...] = third.astype(jnp.bfloat16)


def third_back(
    gthird_ref, upper_ref, cot_ref, gain_ref, wo_ref, gupper_ref, branch_ref, gmix_ref, ggain_ref
):
    grad, ggain_ref[...] = norm_back(upper_ref[...], gain_ref[...], gthird_ref[...])
    grad = cot_ref[...].astype(jnp.float32) + grad
    gupper_ref[...] = grad
    low = grad.astype(jnp.bfloat16)
    branch_ref[...] = low
    gmix_ref[...] = dot(low, wo_ref[...], NT).astype(jnp.bfloat16)


def last_back(
    gq_ref, gk_ref, gv_ref, gmk_ref, gmv_ref, tokens_ref, gmiddle_ref, gain_ref,
    wq_ref, wk_ref, wv_ref, wmk_ref, wmv_ref,
    sums_ref, places_ref, ggain_two_ref, ggain_three_ref, gtokens_ref, gmemory_ref, extra_ref,
):
    near = sums_ref[:, :GROUP].reshape(HEADS, 2 * LANES)
    far = jnp.sum(sums_ref[:, GROUP : 2 * GROUP].reshape(HEADS, 2 * LANES), axis=1, keepdims=True)
    high = near.astype(jnp.bfloat16)
    left = near - high.astype(jnp.float32)
    middle = left.astype(jnp.bfloat16)
    least = (left - middle.astype(jnp.float32)).astype(jnp.bfloat16)
    places = places_ref[...]
    lane = lax.broadcasted_iota(jnp.int32, (HEADS, BUCKETS * HEADS), 1)
    head = lax.broadcasted_iota(jnp.int32, (HEADS, BUCKETS * HEADS), 0)
    table = dot(high, places) + dot(middle, places) + dot(least, places)
    table = table + jnp.where(lane // HEADS == BUCKETS - 1, far, 0.0)
    table = jnp.sum(jnp.where(lane % HEADS == head, table, 0.0), axis=0, keepdims=True)
    table = jnp.concatenate([table, jnp.zeros((1, D - table.shape[1]), jnp.float32)], axis=1)
    gmemory_ref[...] = dot(gmk_ref[...], wmk_ref[...], NT) + dot(gmv_ref[...], wmv_ref[...], NT)
    gfirst = dot(gq_ref[...], wq_ref[...], NT) + dot(gk_ref[...], wk_ref[...], NT)
    gfirst = gfirst + dot(gv_ref[...], wv_ref[...], NT)
    hidden = tokens_ref[...].astype(jnp.float32)
    grad, ggain = norm_back(hidden, gain_ref[...], gfirst)
    gtokens_ref[...] = gmiddle_ref[...] + grad
    lines = [ggain, ggain_two_ref[...], ggain_three_ref[...], table] + zero_rows(4)
    extra_ref[...] = jnp.concatenate(lines, axis=0)


def put_products(core_ref, rows, plan, pairs, sent_ref, kept_ref):
    if kept_ref is None:
        for k, (left, right) in enumerate(pairs):
            sent_ref[k] = dot(left[...], right[...], TN).astype(jnp.bfloat16)
        return
    parts = [divided(dot(left[...], right[...], TN), rows, core_ref[0]) for left, right in pairs]
    for which, result in enumerate((sent_ref, kept_ref)):
        for place, chip in enumerate(sums_order(plan)):
            lines = jnp.concatenate([part[which][chip] for part in parts], axis=0)
            result[place] = lines.astype(jnp.bfloat16)


def cross_back(
    rows, plans, core_ref, q_ref, k_ref, v_ref, gcrossed_ref, probs_ref,
    second_ref, memory_ref, crossed_ref, gcross_ref, middle_ref, gupper_ref, gain_ref,
    wq_ref, wso_ref,
    gk_ref, gv_ref, gmiddle_ref, branch_ref, gmix_ref, ggain_ref, sent_ref, *rest,
):
    kept_ref, (gq_ref, dk_sum, dv_sum) = rest[0] if len(rest) == 4 else None, rest[-3:]
    pair = pl.program_id(0)
    attend_back_pair(
        False, pair, q_ref, k_ref, v_ref, gcrossed_ref, probs_ref, gq_ref, gk_ref, gv_ref, None,
        dk_sum, dv_sum,
    )

    @pl.when(pair == PAIRS - 1)
    def _():
        pairs = [
            (second_ref, gq_ref),
            (memory_ref, gk_ref),
            (memory_ref, gv_ref),
            (crossed_ref, gcross_ref),
        ]
        put_products(core_ref, rows, plans[0], pairs, sent_ref, kept_ref)
        gsecond = dot(gq_ref[...], wq_ref[...], NT)
        grad, ggain_ref[...] = norm_back(middle_ref[...], gain_ref[...], gsecond)
        grad = gupper_ref[...] + grad
        gmiddle_ref[...] = grad
        low = grad.astype(jnp.bfloat16)
        branch_ref[...] = low
        gmix_ref[...] = dot(low, wso_ref[...], NT).astype(jnp.bfloat16)


def self_back(
    rows, plans, core_ref, q_ref, k_ref, v_ref, gmixed_ref, probs_ref, first_ref, mixed_ref, gself_ref,
    gq_ref, gk_ref, gv_ref, sums_ref, late_sent_ref, early_sent_ref, *rest,
):
    kept, (dk_sum, dv_sum) = rest[:2] if len(rest) == 4 else (None, None), rest[-2:]
    pair = pl.program_id(0)
    attend_back_pair(
        True, pair, q_ref, k_ref, v_ref, gmixed_ref, probs_ref, gq_ref, gk_ref, gv_ref, sums_ref,
        dk_sum, dv_sum,
    )

    @pl.when(pair == PAIRS - 1)
    def _():
        late = [(first_ref, gv_ref), (mixed_ref, gself_ref)]
        early = [(first_ref, gq_ref), (first_ref, gk_ref)]
        put_products(core_ref, rows, plans[1], late, late_sent_ref, kept[0])
        put_products(core_ref, rows, plans[0], early, early_sent_ref, kept[1])


def term_specs(chains):
    specs = []
    for terms in chains:
        for term, at in terms:

            def place(step, spot_ref, at=at):
                bits = [((spot_ref[0] >> (which - 1)) & 1) * weight for which, _, weight in at]
                return (sum(bits, step), 0, 0)

            specs.append(pl.BlockSpec((1,) + term.shape[1:], place))
    return specs


def row_sums(squares):
    ones = jnp.ones((8, squares.shape[1]), jnp.bfloat16)
    high = squares.astype(jnp.bfloat16)
    left = (squares - high.astype(jnp.float32)).astype(jnp.bfloat16)
    return (dot(ones, high, NT) + dot(ones, left, NT))[:1]


def finish(terms, value_ref, rows_ref):
    count, rows, columns = value_ref.shape
    value = sum(term[0].astype(jnp.float32) for term in terms).reshape(count, rows, columns)
    value_ref[...] = value
    lines = []
    for k in range(count):
        squares = value[k] * value[k]
        rows_ref[k : k + 1] = row_sums(squares) * (1.0 / columns)
        lines.append(jnp.sum(squares, axis=0, keepdims=True))
    return lines


def zero_rows(count):
    return [jnp.zeros((1, D), jnp.float32)] * count


def ffn_last(counts, spot_ref, *refs):
    ins, outs, refs = refs[: counts[0]], refs[counts[0] : sum(counts)], refs[sum(counts) :]
    in_ref, in_rows_ref, out_ref, out_rows_ref, columns_ref = refs
    (wide,) = finish(ins, in_ref, in_rows_ref)
    lines = finish(outs, out_ref, out_rows_ref)
    lines = lines + [wide[:, at : at + D] for at in range(0, FF, D)]
    columns_ref[...] = jnp.concatenate(lines + zero_rows(8 - len(lines)), axis=0)


def cross_last(counts, spot_ref, *refs):
    value_ref, rows_ref, columns_ref = refs[counts[0] :]
    lines = finish(refs[: counts[0]], value_ref, rows_ref)
    columns_ref[...] = jnp.concatenate(lines + zero_rows(8 - len(lines)), axis=0)


def self_last(counts, spot_ref, *refs):
    one, two, refs = refs[: counts[0]], refs[counts[0] : sum(counts)], refs[sum(counts) :]
    cross_ref, ffn_ref, extra_ref, early_ref, early_rows_ref, late_ref, late_rows_ref, all_ref = refs
    lines = finish(one, early_ref, early_rows_ref) + finish(two, late_ref, late_rows_ref)
    all_ref[:8] = jnp.concatenate(lines + [cross_ref[:4]], axis=0)
    all_ref[8:16] = ffn_ref[...]
    all_ref[16:] = extra_ref[...]


def last_terms(kernel, spot, chains, shapes, extras, lines):
    asked = [chain.terms for chain in chains]
    outs = []
    for shape in shapes:
        outs += [shape, shape[:2]]
    outs.append((lines, D))
    whole = lambda shape: pl.BlockSpec(shape, lambda step, _: (0,) * len(shape))
    return pl.pallas_call(
        functools.partial(kernel, [len(terms) for terms in asked]),
        grid_spec=pltpu.PrefetchScalarGridSpec(
            num_scalar_prefetch=1,
            grid=(1,),
            in_specs=term_specs(asked) + [whole(extra.shape) for extra in extras],
            out_specs=[whole(shape) for shape in outs],
        ),
        out_shape=[jax.ShapeDtypeStruct(shape, jnp.float32) for shape in outs],
        compiler_params=pltpu.CompilerParams(vmem_limit_bytes=VMEM_BYTES),
        name=kernel.__name__,
    )(spot, *[term for terms in asked for term, _ in terms], *extras)


AXES = ("wide", "narrow")


def after(value, *others):
    return lax.optimization_barrier((value,) + others)[0]


class Cube:
    def __init__(self):
        self.count = lax.axis_size("wide") * lax.axis_size("narrow")
        self.bits = self.count.bit_length() - 1
        self.me = lax.axis_index("wide") * lax.axis_size("narrow") + lax.axis_index("narrow")
        high = [[which] for which in range(self.bits - 1, 1, -1)]
        self.plan_a = high + [[1]]
        self.plan_b = [[1]] + high
        self.plan_d = high[:1] + high[2:] + high[1:2] + [[1]]
        self.plan_e = [[1]] + high[:1] + high[2:] + high[1:2]
        self.plan_c = high[:1] + [[1]] + high[2:] + high[1:2]

    def bit(self, which):
        return (self.me >> which) & 1

    def swap(self, value, flip):
        return lax.ppermute(value, AXES, [(i, i ^ flip) for i in range(self.count)])

    def place(self, mine, theirs, axis):
        first = self.bit(0) == 0
        return jnp.where(
            first, jnp.concatenate([mine, theirs], axis), jnp.concatenate([theirs, mine], axis)
        )

    def half(self, value, whose):
        size = value.shape[-1] // 2
        return lax.dynamic_slice_in_dim(value, whose * size, size, value.ndim - 1)

    def total(self, value):
        for low in [0] + list(range(1, self.bits, 2)):
            top = 1 if low == 0 else min(2, self.bits - low)
            flips = [flip << low for flip in range(1, 1 << top)]
            value = value + sum(self.swap(value, flip) for flip in flips)
        return value


def flips_of(group):
    picks = range(1, 1 << len(group))
    return [sum(((pick >> k) & 1) << which for k, which in enumerate(group)) for pick in picks]


class Gather:
    def __init__(self, cube, value, plan):
        self.cube, self.plan, self.steps = cube, plan, 0
        self.held, self.parts = value[None], []

    def send(self, *behind):
        sent = after(self.held, *behind) if behind else self.held
        self.theirs = [self.cube.swap(sent, flip) for flip in flips_of(self.plan[self.steps])]
        self.steps += 1
        if self.steps == len(self.plan):
            self.parts = [self.held, self.cube.swap(sent, 1)]
        return sent

    def take(self, *behind):
        theirs = [after(their, *behind) if behind else their for their in self.theirs]
        if self.parts:
            self.parts = [self.parts[0], *theirs, self.parts[1], self.cube.swap(theirs[0], 1)]
        else:
            self.held = jnp.concatenate([self.held, *theirs], axis=0)


def pair_columns(cube, value, *behind):
    core = cube.bit(0)
    sent = cube.half(value, 1 - core)
    theirs = cube.swap(after(sent, *behind) if behind else sent, 1)
    return cube.half(value, core), theirs


class Sums:
    def __init__(self, cube, plan, sent, kept):
        self.cube, self.bits = cube, [which for group in reversed(plan) for which in group]
        self.blocks, self.theirs = cube.count // 2, cube.swap(sent, 1)
        self.terms = [(kept, [])]

    def take(self, *behind):
        self.terms.append((after(self.theirs, *behind) if behind else self.theirs, []))

    def begin(self, at):
        bits = [(self.cube.bit(which) ^ flip) * weight for which, flip, weight in at]
        return sum(bits, jnp.int32(0))

    def send(self):
        which = self.bits.pop(0)
        self.blocks //= 2
        parts = [
            lax.dynamic_slice_in_dim(
                term, self.begin(at + [(which, 1, self.blocks)]), self.blocks, 0
            ).astype(jnp.float32)
            for term, at in self.terms
        ]
        sent = sum(parts).astype(jnp.bfloat16)
        self.terms = [(term, at + [(which, 0, self.blocks)]) for term, at in self.terms]
        self.theirs = self.cube.swap(sent, 1 << which)
        return sent

    def going(self):
        return len(self.bits) > 0


def send_all(chains):
    return tuple([chain.send() for chain in chains])


def whole_tiles(cube):
    return cube.bits == 5


def product_outs(cube, count):
    if whole_tiles(cube):
        return [((cube.count // 2, count * (D // cube.count), D), jnp.bfloat16)] * 2
    return [((count, D, D), jnp.bfloat16)]


def product_sums(cube, plan, parts, *behind):
    chips = cube.count // 2
    if len(parts) == 1:
        count, _, columns = parts[0].shape
        grads = parts[0].reshape(count, chips, 2, -1, columns).transpose(2, 1, 0, 3, 4)
        grads = grads.reshape(2, chips, -1, columns)
        grads = jnp.take(grads, np.array(sums_order(plan)), axis=1)
        core = cube.bit(0)
        parts = [lax.dynamic_index_in_dim(grads, core ^ k, 0, False) for k in (1, 0)]
    sent, kept = [part.reshape(chips, -1, part.shape[-1]) for part in parts]
    return Sums(cube, plan, after(sent, *behind) if behind else sent, kept)


def chip_order(cube, parts, plan):
    places = jnp.concatenate(parts, axis=0)
    chips = chip_of(cube.me >> 1, jnp.arange(places.shape[0], dtype=jnp.int32), plan)
    moves = jnp.arange(places.shape[0], dtype=jnp.int32)[:, None] == chips[None, :]
    moved = jnp.dot(moves.astype(places.dtype), places.reshape(places.shape[0], -1))
    return moved.reshape(places.shape)


def on_device(
    tokens,
    memory,
    cotangent,
    dec_segments,
    enc_segments,
    dec_valid,
    attn_weights,
    w_in,
    w_out,
    norm_gains,
    rel_table,
    row_main,
    row_out,
    col_main,
    col_in,
):
    cube = Cube()
    core = cube.bit(0)
    spot = jnp.stack([cube.me >> 1, core])
    rows = attn_weights.shape[1]
    tiled = whole_tiles(cube)
    plans = cube.plan_a, cube.plan_b
    segment = dec_segments[0]
    see_self = self_mask(segment, dec_valid[0])
    see_cross = cross_mask(segment, enc_segments[0])
    lines = bias_lines(rel_table)
    distances = np.arange(2 * LANES)[:, None]
    places = (distances >= np.array(thresholds())[None, :]).sum(axis=1, keepdims=True)
    places = np.repeat(places == np.arange(BUCKETS)[None, :], HEADS, axis=1)
    places = jnp.asarray(places.astype(np.float32), jnp.bfloat16)
    tile, low, full = tokens.shape, jnp.bfloat16, jnp.float32
    square = ((D, D), low)
    probs = (HEADS, segment.shape[0], segment.shape[0])
    if tiled:
        attn_rows = attn_weights[:4].reshape(-1, D)
        gain_rows = jnp.pad(norm_gains, ((0, 5), (0, D // 2 - rows)))
        sent = jnp.concatenate([cube.half(attn_rows, 1 - core), gain_rows], axis=0)
        theirs = cube.swap(sent, 1)
        pairs = cube.place(
            cube.half(attn_rows, core).reshape(4, rows, -1),
            theirs[: 4 * rows].reshape(4, rows, -1),
            1,
        ).reshape(4 * 2 * rows, -1)
        gain_pair = cube.place(gain_rows, theirs[4 * rows :], 0)
        one = Gather(cube, jnp.concatenate([pairs[: 4 * rows], gain_pair], axis=0), cube.plan_a)
        two = Gather(cube, pairs[4 * rows :], cube.plan_c)
        ahead = one.send(), two.send()
        cross = pair_columns(cube, attn_weights[4:], *ahead)
        inner = pair_columns(cube, w_in, *ahead)
        outer = pair_columns(cube, w_out, *ahead)
        three = Gather(cube, cube.place(*cross, 1).reshape(8 * rows, -1), cube.plan_a)
        inner = Gather(cube, cube.place(*inner, 0), cube.plan_b)
        outer = Gather(cube, cube.place(*outer, 0), cube.plan_a)
        last = len(cube.plan_a) - 1
        for step in range(last):
            one.take()
            two.take()
            ahead = one.send(), two.send()
            if step > 0:
                three.take(*ahead)
            ahead = ahead + (three.send(*ahead),)
            if step > 1:
                inner.take(*ahead)
                outer.take(*ahead)
            if step > 0:
                inner.send(*ahead)
                outer.send(*ahead)
        one.take()
        two.take()
        ahead = one.parts[2], two.parts[2]
        three.take(*ahead)
        ahead = ahead + (three.send(*ahead),)
        inner.take(*ahead)
        outer.take(*ahead)
        ahead = ahead + (inner.send(*ahead), outer.send(*ahead))
        gain_full = chip_order(cube, [part[:, 4 * rows :, :rows] for part in one.parts[:2]], plans[0])
        gain_full = gain_full.reshape(-1, 2, 8, rows)[:, :, :3].transpose(2, 0, 1, 3)
        gain_full = gain_full.reshape(3, D)
        first_chunk, second_chunk = one.parts, two.parts
        gain_full = after(gain_full, *ahead)
    else:
        attn_full = lax.all_gather(attn_weights, AXES, axis=1, tiled=True)
        gain_full = lax.all_gather(norm_gains, AXES, axis=1, tiled=True)
        first_chunk, second_chunk = [attn_full[:2]], [attn_full[2:4]]
    gain_one, gain_two, gain_three = [gain_full[k : k + 1].astype(full) for k in range(3)]
    first_low, query, keys, values, self_probs, mixed_low, *weights = by_pair(
        functools.partial(self_part, (cube.plan_a, cube.plan_c)),
        [spot, tokens, gain_one, see_self, lines, *first_chunk, *second_chunk],
        [(tile, low)] * 4 + [(probs, low), (tile, low)] + [square] * 4,
        [],
        (probs, lines.shape),
        "self_part",
        early=(0, 1, 2, 3, 6, 7, 8, 9),
    )
    if tiled:
        three.take(mixed_low)
        cross_chunk = three.parts
        inner.take(mixed_low)
        outer.take(mixed_low)
        weights[3] = after(weights[3], inner.send(), outer.send())
    else:
        cross_chunk = [attn_full[4:]]
    (
        middle, second_low, cross_query, memory_keys, memory_values, cross_probs, crossed_low,
        upper, third_low, *cross_weights,
    ) = by_pair(
        functools.partial(cross_part, plans[0]),
        [
            spot, tokens, mixed_low, memory, gain_two, weights[3], gain_three, see_cross,
            *cross_chunk,
        ],
        [(tile, full)] + [(tile, low)] * 4 + [(probs, low), (tile, low), (tile, full), (tile, low)]
        + [square] * 4,
        [],
        (probs,),
        "cross_part",
        early=(0, 1, 2, 3, 4, 9, 10, 11, 12),
    )
    attn_full = weights + cross_weights
    if tiled:
        inner.take(third_low)
        outer.take(third_low)
        in_parts, out_parts = inner.parts, outer.parts
    else:
        in_parts = [lax.all_gather(w_in, AXES, axis=0, tiled=True)]
        out_parts = [lax.all_gather(w_out, AXES, axis=0, tiled=True)]
    layer_out, grad_third, *rest = ffn(
        spot, plans, third_low, upper, cotangent, in_parts, out_parts
    )
    half = len(rest) // 2
    parts = rest if tiled else [part[None] for part in rest]
    in_sums = product_sums(cube, cube.plan_b, parts[:half])
    out_sums = product_sums(cube, cube.plan_a, parts[half:])
    grad_upper, grad_cross_branch, grad_crossed, grad_gain_third = fused(
        third_back,
        [(tile, full), (tile, low), (tile, low), ((1, D), full)],
        grad_third,
        upper,
        cotangent,
        gain_three,
        attn_full[7],
    )
    in_sums.take(grad_crossed)
    started = send_all((in_sums,))
    out_sums.take(*started)
    grad_crossed = after(grad_crossed, *started, *send_all((out_sums,)))
    sums_scratch = [pltpu.VMEM((tile[0], LANES), full)] * 2
    memory_key_low, memory_value_low, grad_middle, grad_self_branch, grad_mixed, *rest = by_pair(
        functools.partial(cross_back, rows, plans),
        [
            core[None],
            cross_query,
            memory_keys,
            memory_values,
            grad_crossed,
            cross_probs,
            second_low,
            memory,
            crossed_low,
            grad_cross_branch,
            middle,
            grad_upper,
            gain_two,
            attn_full[4],
            attn_full[3],
        ],
        [(tile, low)] * 2
        + [(tile, full), (tile, low), (tile, low), ((1, D), full)]
        + product_outs(cube, 4),
        [pltpu.VMEM(tile, low)] + sums_scratch,
        (probs,),
        "cross_back",
        late=(6, 7, 8, 9, 10, 11, 13, 14),
    )
    grad_gain_second = rest[0]
    for each in (in_sums, out_sums):
        each.take(grad_mixed)
    arrived = in_sums.terms[-1][0], out_sums.terms[-1][0]
    cross_sums = product_sums(cube, cube.plan_a, rest[1:], *arrived)
    started = send_all((in_sums, out_sums))
    cross_sums.take(*started)
    grad_mixed = after(grad_mixed, *started, *send_all((cross_sums,)))
    lots = (PAIRS, 8, 2 * LANES)
    outs = product_outs(cube, 2)
    query_low, key_low, value_low, score_sums, *rest = by_pair(
        functools.partial(self_back, rows, (cube.plan_d, cube.plan_c)),
        [
            core[None],
            query,
            keys,
            values,
            grad_mixed,
            self_probs,
            first_low,
            mixed_low,
            grad_self_branch,
        ],
        [(tile, low)] * 3 + [(lots, full)] + outs[:1] * 2 + outs[1:] * 2,
        sums_scratch,
        (probs, lots),
        "self_back",
        late=(6, 7, 8),
    )
    for each in (in_sums, out_sums):
        each.take(query_low)
    arrived = in_sums.terms[-1][0], out_sums.terms[-1][0]
    late_sums = product_sums(cube, cube.plan_c, rest[::2], *arrived)
    early_sums = product_sums(cube, cube.plan_d, rest[1::2], *arrived)
    cross_sums.take(query_low)
    started = send_all((out_sums, in_sums, cross_sums))
    late_sums.take(*started)
    early_sums.take(*started)
    started = started + send_all((early_sums, late_sums))
    query_low = after(query_low, *started)
    grad_tokens, grad_memory, extra = fused(
        last_back,
        [(tile, full), (tile, full), ((8, D), full)],
        query_low,
        key_low,
        value_low,
        memory_key_low,
        memory_value_low,
        tokens,
        grad_middle,
        gain_one,
        *attn_full[:3],
        *attn_full[5:7],
        score_sums,
        places,
        grad_gain_second,
        grad_gain_third,
    )

    def move(chains, *behind):
        for each in chains:
            each.take(*behind)
        return send_all(chains)

    started = move((early_sums, late_sums, out_sums, in_sums), grad_tokens)
    move((cross_sums,), *started)
    started = move((early_sums, late_sums))
    while in_sums.going():
        move((out_sums, in_sums))
    while cross_sums.going():
        started = started + move((cross_sums,), *started)
    for each in (out_sums, in_sums):
        each.take(*started)
    grad_in, in_rows, grad_out, out_rows, ffn_columns = last_terms(
        ffn_last, spot, [in_sums, out_sums], [(1, rows, FF), (1, FF // cube.count, D)], [], 8
    )
    while early_sums.going():
        move((early_sums, late_sums), ffn_columns)
    cross_sums.take()
    cross_grads, cross_rows, cross_columns = last_terms(
        cross_last, spot, [cross_sums], [(4, rows, D)], [], 8
    )
    early_sums.take(cross_columns)
    late_sums.take(cross_columns)
    early_grads, early_rows, late_grads, late_rows, columns = last_terms(
        self_last,
        spot,
        [early_sums, late_sums],
        [(2, rows, D)] * 2,
        [cross_columns, ffn_columns, extra],
        24,
    )
    grad_attn = jnp.concatenate([early_grads, late_grads, cross_grads], axis=0)
    grad_in, grad_out = grad_in[0], grad_out[0]
    row_means = jnp.concatenate([early_rows, late_rows, cross_rows, in_rows], axis=0)
    new_row_main = DECAY * row_main + (1.0 - DECAY) * row_means
    new_row_out = DECAY * row_out + (1.0 - DECAY) * out_rows[0]
    columns = cube.total(columns)
    col_means = jnp.concatenate([columns[:8] / D, columns[8:9] / FF], axis=0)
    new_col_main = DECAY * col_main + (1.0 - DECAY) * col_means
    new_col_in = DECAY * col_in + (1.0 - DECAY) * (columns[9 : 9 + FF // D].reshape(FF) / D)
    grad_gains = lax.dynamic_slice_in_dim(columns[16:19], cube.me * rows, rows, 1)
    grad_table = columns[19, : BUCKETS * HEADS].reshape(BUCKETS, HEADS)
    return (
        layer_out,
        grad_tokens,
        grad_memory,
        grad_attn,
        grad_in,
        grad_out,
        grad_gains,
        grad_table,
        new_row_main,
        new_row_out,
        new_col_main,
        new_col_in,
    )


def solution(mesh):
    placed = (
        P(("wide", "narrow"), None),
        P(("wide", "narrow"), None),
        P(("wide", "narrow"), None),
        P(("wide", "narrow"), None),
        P(("wide", "narrow"), None),
        P(("wide", "narrow"), None),
        P(None, ("wide", "narrow"), None),
        P(("wide", "narrow"), None),
        P(("wide", "narrow"), None),
        P(None, ("wide", "narrow")),
        P(),
        P(None, ("wide", "narrow")),
        P(("wide", "narrow")),
        P(),
        P(),
    )
    return jax.shard_map(
        on_device,
        mesh=mesh,
        in_specs=placed,
        out_specs=(
            P(("wide", "narrow"), None),
            P(("wide", "narrow"), None),
            P(("wide", "narrow"), None),
            P(None, ("wide", "narrow"), None),
            P(("wide", "narrow"), None),
            P(("wide", "narrow"), None),
            P(None, ("wide", "narrow")),
            P(),
            P(None, ("wide", "narrow")),
            P(("wide", "narrow")),
            P(),
            P(),
        ),
        check_vma=False,
    )
```

```python
import functools
import math

import jax
import jax.numpy as jnp
import numpy as np
from jax import lax
from jax.experimental import pallas as pl
from jax.experimental.pallas import tpu as pltpu
from jax.sharding import PartitionSpec as P

D = 768
HEADS = 12
HEAD = 64
FF = 3072
BUCKETS = 32
MAXDIST = 128


EPSILON = 1e-06
DECAY = 0.8
NEGATIVE = -1e30


def thresholds():
    exact_count = BUCKETS // 2
    limits = list(range(1, exact_count + 1))
    for bucket_level in range(exact_count + 1, BUCKETS):
        limits.append(
            int(
                math.ceil(
                    exact_count
                    * (MAXDIST / exact_count) ** ((bucket_level - exact_count) / exact_count)
                )
            )
        )
    return limits


def bucket_table(distance, number_type):
    level_count = jnp.zeros(distance.shape, jnp.int32)
    for threshold in thresholds():
        level_count = level_count + (distance >= threshold).astype(jnp.int32)
    return (level_count[..., None] == jnp.arange(BUCKETS, dtype=jnp.int32)).astype(number_type)


def weight_grad(left_side, gradient):
    return lax.dot_general(
        left_side, gradient, (((0,), (0,)), ((), ())), preferred_element_type=jnp.float32
    )


LANES = 128
GROUP = LANES // HEAD
CUT = 256
VMEM_BYTES = 60 * 1024 * 1024

NT = (((1,), (1,)), ((), ()))
TN = (((0,), (0,)), ((), ()))


def dot(left, right, dims=(((1,), (0,)), ((), ()))):
    return lax.dot_general(left, right, dims, preferred_element_type=jnp.float32)


def spans(rows, causal):
    return [(at, at + CUT if causal else rows) for at in range(0, rows, CUT)]


def lane_mask(head):
    lanes = lax.broadcasted_iota(jnp.int32, (1, LANES), 1)
    return ((lanes // HEAD) == head).astype(jnp.float32)


def only_head(block, head, scale):
    return (block.astype(jnp.float32) * (lane_mask(head) * scale)).astype(jnp.bfloat16)


def near_bias(line_ref, head):
    line = jnp.broadcast_to(line_ref[0, head : head + 1], (LANES, 2 * LANES))
    return pltpu.roll(line, 0, 1, stride=1, stride_axis=0)


def add_bias(scores, bias, at):
    columns = []
    for first in range(0, CUT, LANES):
        rows = []
        for key in range(0, scores.shape[0], LANES):
            apart = at + first - key
            block = scores[key : key + LANES, first : first + LANES]
            if apart >= 2 * LANES:
                block = block + bias[:1, 2 * LANES - 1 :]
            elif apart >= 0:
                block = block + bias[:, apart : apart + LANES]
            rows.append(block)
        columns.append(jnp.concatenate(rows, axis=0))
    return jnp.concatenate(columns, axis=1)


def attend_pair(causal, pair, q_ref, k_ref, v_ref, mask_ref, line_ref, probs_ref, out_ref):
    rows = q_ref.shape[0]
    lanes = pl.ds(pl.multiple_of(pair * LANES, LANES), LANES)
    biases = [near_bias(line_ref, head) for head in range(GROUP)] if causal else None
    for at, depth in spans(rows, causal):
        keys, values = k_ref[:depth, lanes], v_ref[:depth, lanes]
        total = jnp.zeros((CUT, LANES), jnp.float32)
        for head in range(GROUP):
            query = only_head(q_ref[at : at + CUT, lanes], head, HEAD**-0.5)
            scores = dot(keys, query, NT)
            if causal:
                scores = add_bias(scores, biases[head], at)
            scores = scores + mask_ref[:depth, at : at + CUT]
            weights = jnp.exp(scores - jnp.max(scores, axis=0, keepdims=True))
            weights = weights * (1.0 / jnp.sum(weights, axis=0, keepdims=True))
            low = weights.astype(jnp.bfloat16)
            probs_ref[head, :depth, at : at + CUT] = low
            total = total + dot(low, values, TN) * lane_mask(head)
        out_ref[at : at + CUT, lanes] = total.astype(jnp.bfloat16)


def diagonal_sums(block):
    width = block.shape[1]
    slabs = [block[at : at + 8] for at in range(0, block.shape[0], 8)]
    total = slabs[0]
    for at, slab in enumerate(slabs[1:], 1):
        total = total + pltpu.roll(slab, width - 8 * at, 1)
    row = lax.broadcasted_iota(jnp.int32, total.shape, 0)
    for step in (1, 2, 4):
        total = jnp.where((row & step) != 0, pltpu.roll(total, width - step, 1), total)
    return jnp.sum(total, axis=0, keepdims=True)


def attend_back_pair(
    causal, pair, q_ref, k_ref, v_ref, g_ref, probs_ref, dq_ref, dk_ref, dv_ref, sums_ref,
    dk_sum, dv_sum,
):
    rows = q_ref.shape[0]
    lanes = pl.ds(pl.multiple_of(pair * LANES, LANES), LANES)
    dk_sum[...] = jnp.zeros_like(dk_sum)
    dv_sum[...] = jnp.zeros_like(dv_sum)
    near = [[], []]
    far = [[], []]
    for at, depth in spans(rows, causal):
        dq = jnp.zeros((CUT, LANES), jnp.float32)
        for head in range(GROUP):
            grad = only_head(g_ref[at : at + CUT, lanes], head, 1.0)
            query = only_head(q_ref[at : at + CUT, lanes], head, HEAD**-0.5)
            keys = only_head(k_ref[:depth, lanes], head, HEAD**-0.5)
            low = probs_ref[head, :depth, at : at + CUT]
            probs = low.astype(jnp.float32)
            scaled = probs * dot(v_ref[:depth, lanes], grad, NT)
            centre = jnp.sum(scaled, axis=0, keepdims=True)
            grad_scores = (scaled - probs * centre).astype(jnp.bfloat16)
            dv_sum[:depth] += dot(low, grad)
            dk_sum[:depth] += dot(grad_scores, query)
            dq = dq + dot(grad_scores, keys, TN)
            if causal:
                parts = grad_scores.astype(jnp.float32)
                for first in range(0, CUT, LANES):
                    own = at + first
                    column = parts[:, first : first + LANES]
                    if own:
                        before = column[own - LANES : own]
                    else:
                        before = jnp.zeros((LANES, LANES), jnp.float32)
                    near[head].append((column[own : own + LANES], before))
                    if own > LANES:
                        far[head].append(jnp.sum(column[: own - LANES], axis=0, keepdims=True))
        dq_ref[at : at + CUT, lanes] = dq.astype(jnp.bfloat16)
    dk_ref[:, lanes] = dk_sum[...].astype(jnp.bfloat16)
    dv_ref[:, lanes] = dv_sum[...].astype(jnp.bfloat16)
    if causal:
        lines = []
        for head in range(GROUP):
            own = sum(pair[0] for pair in near[head][1:]) + near[head][0][0]
            before = sum(pair[1] for pair in near[head][1:]) + near[head][0][1]
            lines.append(diagonal_sums(jnp.concatenate([own, before], axis=1)))
        for head in range(GROUP):
            line = sum(far[head][1:]) + far[head][0]
            lines.append(jnp.concatenate([line, jnp.zeros_like(line)], axis=1))
        lines.append(jnp.zeros((8 - len(lines), 2 * LANES), jnp.float32))
        sums_ref[0] = jnp.concatenate(lines, axis=0)


def self_mask(segment, key_valid):
    rows = segment.shape[0]
    index = jnp.arange(rows, dtype=jnp.int32)
    distance = index[None, :] - index[:, None]
    allowed = (
        (segment[:, None] == segment[None, :])
        & (distance >= 0)
        & ((key_valid[:, None] > 0) | (distance == 0))
    )
    return jnp.where(allowed, 0.0, NEGATIVE).astype(jnp.float32)


def cross_mask(segment, mem_segment):
    allowed = mem_segment[:, None] == segment[None, :]
    return jnp.where(allowed, 0.0, NEGATIVE).astype(jnp.float32)


def bias_lines(table):
    places = bucket_table(jnp.arange(2 * LANES, dtype=jnp.int32), jnp.float32)
    lines = jnp.einsum(
        "nb,bh->hn", places, table.astype(jnp.float32), precision=lax.Precision.HIGHEST
    )
    lines = lines.reshape(HEADS // GROUP, GROUP, 2 * LANES)
    return jnp.pad(lines, ((0, 0), (0, 8 - GROUP), (0, 0)))


GELU_SCALE = math.sqrt(2.0 / math.pi)
GELU_CUBE = 0.044715
BLOCK = 768
CUTS = FF // (2 * BLOCK)


def chip_of(chip, place, plan):
    bits = [which for group in plan for which in group]
    flip = sum(((place >> k) & 1) << (which - 1) for k, which in enumerate(bits))
    return chip ^ flip


def halves_of(core):
    half = D // 2
    mine = pl.ds(pl.multiple_of(core * half, half), half)
    return mine, pl.ds(pl.multiple_of((1 - core) * half, half), half)


def fill_weight(weight_ref, parts, at, spot_ref, plan):
    if len(parts) == 1:
        weight_ref[...] = parts[0][at]
        return
    blocks, rows = parts[0].shape[0], D // (2 * parts[0].shape[0])
    mine, other = halves_of(spot_ref[1])
    for place in range(2 * blocks):
        chip = chip_of(spot_ref[0], place, plan)
        lines = pl.ds(pl.multiple_of(chip * rows, rows), rows)
        which, block = divmod(place, blocks)
        weight_ref[lines, mine] = parts[which][block, at * rows : (at + 1) * rows]
        weight_ref[lines, other] = parts[2 + which][block, at * rows : (at + 1) * rows]


def sums_order(plan):
    bits = [which for group in plan for which in group]
    count = 1 << len(bits)
    return [sum(((k >> at) & 1) << (which - 1) for at, which in enumerate(bits)) for k in range(count)]


def divided(grads, rows, core):
    grads = grads.reshape(-1, 2, rows, grads.shape[1])
    even, odd = grads[:, 0], grads[:, 1]
    return jnp.where(core == 0, odd, even), jnp.where(core == 0, even, odd)


def ffn_kernel(tiled, plans, spot_ref, third_ref, upper_ref, cot_ref, *refs):
    step = pl.program_id(0)
    if tiled:
        own_in, other_in, out_parts, refs = refs[:2], refs[2:4], refs[4:8], refs[8:]
        layer_ref, gthird_ref, gin_ref, kept_gin_ref, gout_ref, kept_gout_ref = refs[:6]
        total, third_turned, in_block, out_block = refs[6:]
    else:
        in_block, out_block, layer_ref, gthird_ref, gin_ref, gout_ref = refs[:6]
        total, third_turned = refs[6:]

    @pl.when(step == 0)
    def _():
        total[...] = upper_ref[...]
        gthird_ref[...] = jnp.zeros_like(gthird_ref)
        third_turned[...] = third_ref[...].T

    def fill_in(parts):
        blocks, rows, _ = parts[0].shape
        for place in range(2 * blocks):
            chip = chip_of(spot_ref[0], place, plans[1])
            lines = pl.ds(pl.multiple_of(chip * rows, rows), rows)
            in_block[lines, :] = parts[place // blocks][place % blocks]

    if tiled:
        pl.when(step < CUTS)(lambda: fill_in(other_in))
        pl.when(step >= CUTS)(lambda: fill_in(own_in))
        mine, other = halves_of(spot_ref[1])
        rows = out_parts[0].shape[2]
        for place in range(4):
            chip = (spot_ref[0] & 3) ^ place
            lines = pl.ds(pl.multiple_of(chip * rows, rows), rows)
            out_block[lines, mine] = out_parts[place % 2][place // 2, 0]
            out_block[lines, other] = out_parts[2 + place % 2][place // 2, 0]

    inner = dot(third_ref[...], in_block[...])
    square = inner * inner
    slope = jnp.tanh(inner * (GELU_SCALE + (GELU_SCALE * GELU_CUBE) * square))
    half_up = 0.5 + 0.5 * slope
    active = (inner * half_up).astype(jnp.bfloat16)
    total[...] += dot(active, out_block[...])
    grad_active = dot(cot_ref[...], out_block[...], NT)
    bend = (0.5 * inner) * (1.0 - slope * slope)
    bend = bend * (GELU_SCALE + (3.0 * GELU_SCALE * GELU_CUBE) * square)
    grad_inner = (grad_active * (half_up + bend)).astype(jnp.bfloat16)
    gthird_ref[...] += dot(grad_inner, in_block[...], NT)
    grad_in = dot(third_turned[...], grad_inner)
    grad_out = dot(active, cot_ref[...], TN)
    if tiled:
        chips = 2 * own_in[0].shape[0]
        order = sums_order(plans[1])
        parts = divided(grad_in, D // (2 * chips), spot_ref[1])
        for part, result in zip(parts, (gin_ref, kept_gin_ref)):
            part = jnp.concatenate([part[chip] for chip in order], axis=0)
            result[...] = part.astype(jnp.bfloat16)
        parts = divided(grad_out, FF // (2 * chips), spot_ref[1])
        for part, result in zip(parts, (gout_ref, kept_gout_ref)):
            for place in range(4):
                chip = (place >> 1) | ((place & 1) << 1)
                result[place, 0] = part[chip].astype(jnp.bfloat16)
    else:
        gin_ref[...] = grad_in.astype(jnp.bfloat16)
        gout_ref[...] = grad_out.astype(jnp.bfloat16)

    @pl.when(step == 2 * CUTS - 1)
    def _():
        layer_ref[...] = total[...].astype(jnp.bfloat16)


def ffn(spot, plans, third, upper, cotangent, in_parts, out_parts):
    rows = third.shape[0]
    tiled = len(in_parts) > 1

    def block(step, spot_ref):
        return ((1 - spot_ref[1]) * CUTS + step) % (2 * CUTS)

    def line(step, spot_ref):
        flips = block(step, spot_ref) ^ (spot_ref[0] >> 2)
        return (0, (flips >> 1) + 2 * (flips & 1), 0, 0)

    whole = pl.BlockSpec((rows, D), lambda step, spot_ref: (0, 0))
    across = lambda step, spot_ref: (0, block(step, spot_ref))
    down = lambda step, spot_ref: (block(step, spot_ref), 0)
    scratch = [pltpu.VMEM((rows, D), jnp.float32), pltpu.VMEM((D, rows), jnp.bfloat16)]
    if tiled:
        chips, lines, _ = in_parts[0].shape
        late = lambda step, spot_ref: (0, 0, jnp.maximum(step - CUTS, 0))
        early = lambda step, spot_ref: (0, 0, jnp.minimum(step, CUTS - 1))
        in_specs = [pl.BlockSpec((chips, lines, BLOCK), late)] * 2
        in_specs += [pl.BlockSpec((chips, lines, BLOCK), early)] * 2
        out_parts = [part.reshape(2, 4, -1, D // 2) for part in out_parts]
        in_specs += [pl.BlockSpec((2, 1) + out_parts[0].shape[2:], line)] * 4
        out_specs = [pl.BlockSpec((D // 2, BLOCK), across)] * 2
        own = lambda step, spot_ref: (0, (b := block(step, spot_ref)) // 2 + 2 * (b % 2), 0, 0)
        out_specs += [pl.BlockSpec((4, 1, FF // (4 * chips), D), own)] * 2
        shapes = [(D // 2, FF)] * 2 + [(4, 4, FF // (4 * chips), D)] * 2
        scratch += [pltpu.VMEM((D, BLOCK), jnp.bfloat16), pltpu.VMEM((BLOCK, D), jnp.bfloat16)]
    else:
        in_specs = [pl.BlockSpec((D, BLOCK), across), pl.BlockSpec((BLOCK, D), down)]
        out_specs, shapes = in_specs, [(D, FF), (FF, D)]
    return pl.pallas_call(
        functools.partial(ffn_kernel, tiled, plans),
        grid_spec=pltpu.PrefetchScalarGridSpec(
            num_scalar_prefetch=1,
            grid=(2 * CUTS,),
            in_specs=[whole, whole, whole] + in_specs,
            out_specs=[whole, whole] + out_specs,
            scratch_shapes=scratch,
        ),
        out_shape=[
            jax.ShapeDtypeStruct((rows, D), jnp.bfloat16),
            jax.ShapeDtypeStruct((rows, D), jnp.float32),
        ]
        + [jax.ShapeDtypeStruct(shape, jnp.bfloat16) for shape in shapes],
        compiler_params=pltpu.CompilerParams(vmem_limit_bytes=VMEM_BYTES),
        name="ffn",
    )(spot, third, upper, cotangent, *in_parts, *out_parts)


def scale_of(hidden):
    return lax.rsqrt(jnp.mean(hidden * hidden, axis=-1, keepdims=True) + EPSILON)


def norm_back(hidden, gain, grad):
    scale = scale_of(hidden)
    grown = grad * gain
    inner = jnp.mean(grown * hidden, axis=-1, keepdims=True)
    gain_grad = jnp.sum(grad * (hidden * scale), axis=0, keepdims=True)
    return scale * grown - hidden * (scale * scale * scale * inner), gain_grad


def fused(kernel, outs, *args):
    space = pl.BlockSpec(memory_space=pltpu.VMEM)
    return pl.pallas_call(
        kernel,
        in_specs=[space] * len(args),
        out_specs=[space] * len(outs),
        out_shape=[jax.ShapeDtypeStruct(shape, held_as) for shape, held_as in outs],
        compiler_params=pltpu.CompilerParams(vmem_limit_bytes=VMEM_BYTES),

        name=kernel.__name__,
    )(*args)


PAIRS = HEADS // GROUP


def whole_spec(array, space=None):
    rank = len(array.shape)
    return pl.BlockSpec(array.shape, lambda pair: (0,) * rank, pipeline_mode=space)


def by_pair(kernel, args, outs, scratch, by_step, name, late=(), early=()):
    held = [jax.ShapeDtypeStruct(shape, held_as) for shape, held_as in outs]
    beside = pl.BlockSpec(memory_space=pl.ANY)
    buffers = [args[k] for k in late] + [held[k] for k in early]
    count = len(args) + len(held) + len(scratch)

    def body(*refs):
        pair = pl.program_id(0)
        refs, places, arrived = list(refs[:count]), refs[count:-1], refs[-1]
        wanted = list(late) + [len(args) + k for k in early]
        copies = []
        for k, (at, place) in enumerate(zip(wanted, places)):
            ends = (refs[at], place) if k < len(late) else (place, refs[at])
            copies.append(pltpu.make_async_copy(*ends, arrived.at[k]))
            refs[at] = place
        loads, stores = copies[: len(late)], copies[len(late) :]

        @pl.when(pair == 0)
        def _():
            for copy in loads:
                copy.start()

        @pl.when(pair == PAIRS - 1)
        def _():
            for copy in loads:
                copy.wait()

        kernel(*refs)

        @pl.when(pair == 0)
        def _():
            for copy in stores:
                copy.start()

        @pl.when(pair == PAIRS - 1)
        def _():
            for copy in stores:
                copy.wait()

    def spec(array, once):
        if len(array.shape) == 3 and array.shape in by_step:
            block = (array.shape[0] // PAIRS,) + array.shape[1:]
            return pl.BlockSpec(block, lambda pair: (pair, 0, 0))
        if len(array.shape) == 1:
            return pl.BlockSpec(memory_space=pltpu.SMEM)
        return whole_spec(array, pl.Buffered(1) if once else None)

    in_specs = [beside if k in late else spec(array, True) for k, array in enumerate(args)]
    out_specs = [beside if k in early else spec(array, False) for k, array in enumerate(held)]
    if not buffers:
        body = kernel
    else:
        scratch = scratch + [pltpu.VMEM(array.shape, array.dtype) for array in buffers]
        scratch.append(pltpu.SemaphoreType.DMA((len(buffers),)))
    return pl.pallas_call(
        body,
        grid=(PAIRS,),
        in_specs=in_specs,
        out_specs=out_specs,
        out_shape=held,
        scratch_shapes=scratch,
        compiler_params=pltpu.CompilerParams(vmem_limit_bytes=VMEM_BYTES),
        name=name,
    )(*args)


def self_part(plans, spot_ref, tokens_ref, gain_ref, mask_ref, line_ref, *refs):
    count = (len(refs) - 10) // 2
    one, two, refs = refs[:count], refs[count : 2 * count], refs[2 * count :]
    first_ref, q_ref, k_ref, v_ref, probs_ref, mixed_ref, wq_ref, wk_ref, wv_ref, wo_ref = refs
    pair = pl.program_id(0)

    @pl.when(pair == 0)
    def _():
        hidden = tokens_ref[...].astype(jnp.float32)
        first = (hidden * scale_of(hidden) * gain_ref[...]).astype(jnp.bfloat16)
        first_ref[...] = first
        weights = [(wq_ref, one, 0, q_ref), (wk_ref, one, 1, k_ref), (wv_ref, two, 0, v_ref)]
        for weight_ref, parts, at, result in weights:
            fill_weight(weight_ref, parts, at, spot_ref, plans[parts is two])
            result[...] = dot(first, weight_ref[...]).astype(jnp.bfloat16)
        fill_weight(wo_ref, two, 1, spot_ref, plans[1])

    attend_pair(True, pair, q_ref, k_ref, v_ref, mask_ref, line_ref, probs_ref, mixed_ref)


def cross_part(
    plan, spot_ref, tokens_ref, mixed_ref, memory_ref, gain_ref, wso_ref, next_gain_ref, mask_ref,
    *refs,
):
    parts, refs = refs[:-13], refs[-13:]
    middle_ref, second_ref, q_ref, k_ref, v_ref, probs_ref, crossed_ref = refs[:7]
    upper_ref, third_ref, wq_ref, wk_ref, wv_ref, wo_ref = refs[7:]
    pair = pl.program_id(0)

    @pl.when(pair == 0)
    def _():
        for at, weight_ref in enumerate((wq_ref, wk_ref, wv_ref, wo_ref)):
            fill_weight(weight_ref, parts, at, spot_ref, plan)
        middle = tokens_ref[...].astype(jnp.float32) + dot(mixed_ref[...], wso_ref[...])
        middle_ref[...] = middle
        second = (middle * scale_of(middle) * gain_ref[...]).astype(jnp.bfloat16)
        second_ref[...] = second
        q_ref[...] = dot(second, wq_ref[...]).astype(jnp.bfloat16)
        k_ref[...] = dot(memory_ref[...], wk_ref[...]).astype(jnp.bfloat16)
        v_ref[...] = dot(memory_ref[...], wv_ref[...]).astype(jnp.bfloat16)

    attend_pair(False, pair, q_ref, k_ref, v_ref, mask_ref, None, probs_ref, crossed_ref)

    @pl.when(pair == PAIRS - 1)
    def _():
        upper = middle_ref[...] + dot(crossed_ref[...], wo_ref[...])
        upper_ref[...] = upper
        third = upper * scale_of(upper) * next_gain_ref[...]
        third_ref[...] = third.astype(jnp.bfloat16)


def third_back(
    gthird_ref, upper_ref, cot_ref, gain_ref, wo_ref, gupper_ref, branch_ref, gmix_ref, ggain_ref
):
    grad, ggain_ref[...] = norm_back(upper_ref[...], gain_ref[...], gthird_ref[...])
    grad = cot_ref[...].astype(jnp.float32) + grad
    gupper_ref[...] = grad
    low = grad.astype(jnp.bfloat16)
    branch_ref[...] = low
    gmix_ref[...] = dot(low, wo_ref[...], NT).astype(jnp.bfloat16)


def last_back(
    gq_ref, gk_ref, gv_ref, gmk_ref, gmv_ref, tokens_ref, gmiddle_ref, gain_ref,
    wq_ref, wk_ref, wv_ref, wmk_ref, wmv_ref,
    sums_ref, places_ref, ggain_two_ref, ggain_three_ref, gtokens_ref, gmemory_ref, extra_ref,
):
    near = sums_ref[:, :GROUP].reshape(HEADS, 2 * LANES)
    far = jnp.sum(sums_ref[:, GROUP : 2 * GROUP].reshape(HEADS, 2 * LANES), axis=1, keepdims=True)
    high = near.astype(jnp.bfloat16)
    left = near - high.astype(jnp.float32)
    middle = left.astype(jnp.bfloat16)
    least = (left - middle.astype(jnp.float32)).astype(jnp.bfloat16)
    places = places_ref[...]
    lane = lax.broadcasted_iota(jnp.int32, (HEADS, BUCKETS * HEADS), 1)
    head = lax.broadcasted_iota(jnp.int32, (HEADS, BUCKETS * HEADS), 0)
    table = dot(high, places) + dot(middle, places) + dot(least, places)
    table = table + jnp.where(lane // HEADS == BUCKETS - 1, far, 0.0)
    table = jnp.sum(jnp.where(lane % HEADS == head, table, 0.0), axis=0, keepdims=True)
    table = jnp.concatenate([table, jnp.zeros((1, D - table.shape[1]), jnp.float32)], axis=1)
    gmemory_ref[...] = dot(gmk_ref[...], wmk_ref[...], NT) + dot(gmv_ref[...], wmv_ref[...], NT)
    gfirst = dot(gq_ref[...], wq_ref[...], NT) + dot(gk_ref[...], wk_ref[...], NT)
    gfirst = gfirst + dot(gv_ref[...], wv_ref[...], NT)
    hidden = tokens_ref[...].astype(jnp.float32)
    grad, ggain = norm_back(hidden, gain_ref[...], gfirst)
    gtokens_ref[...] = gmiddle_ref[...] + grad
    lines = [ggain, ggain_two_ref[...], ggain_three_ref[...], table] + zero_rows(4)
    extra_ref[...] = jnp.concatenate(lines, axis=0)


def put_products(core_ref, rows, plan, pairs, sent_ref, kept_ref):
    if kept_ref is None:
        for k, (left, right) in enumerate(pairs):
            sent_ref[k] = dot(left[...], right[...], TN).astype(jnp.bfloat16)
        return
    parts = [divided(dot(left[...], right[...], TN), rows, core_ref[0]) for left, right in pairs]
    for which, result in enumerate((sent_ref, kept_ref)):
        for place, chip in enumerate(sums_order(plan)):
            lines = jnp.concatenate([part[which][chip] for part in parts], axis=0)
            result[place] = lines.astype(jnp.bfloat16)


def cross_back(
    rows, plans, core_ref, q_ref, k_ref, v_ref, gcrossed_ref, probs_ref,
    second_ref, memory_ref, crossed_ref, gcross_ref, middle_ref, gupper_ref, gain_ref,
    wq_ref, wso_ref,
    gk_ref, gv_ref, gmiddle_ref, branch_ref, gmix_ref, ggain_ref, sent_ref, *rest,
):
    kept_ref, (gq_ref, dk_sum, dv_sum) = rest[0] if len(rest) == 4 else None, rest[-3:]
    pair = pl.program_id(0)
    attend_back_pair(
        False, pair, q_ref, k_ref, v_ref, gcrossed_ref, probs_ref, gq_ref, gk_ref, gv_ref, None,
        dk_sum, dv_sum,
    )

    @pl.when(pair == PAIRS - 1)
    def _():
        pairs = [
            (second_ref, gq_ref),
            (memory_ref, gk_ref),
            (memory_ref, gv_ref),
            (crossed_ref, gcross_ref),
        ]
        put_products(core_ref, rows, plans[0], pairs, sent_ref, kept_ref)
        gsecond = dot(gq_ref[...], wq_ref[...], NT)
        grad, ggain_ref[...] = norm_back(middle_ref[...], gain_ref[...], gsecond)
        grad = gupper_ref[...] + grad
        gmiddle_ref[...] = grad
        low = grad.astype(jnp.bfloat16)
        branch_ref[...] = low
        gmix_ref[...] = dot(low, wso_ref[...], NT).astype(jnp.bfloat16)


def self_back(
    rows, plans, core_ref, q_ref, k_ref, v_ref, gmixed_ref, probs_ref, first_ref, mixed_ref, gself_ref,
    gq_ref, gk_ref, gv_ref, sums_ref, late_sent_ref, early_sent_ref, *rest,
):
    kept, (dk_sum, dv_sum) = rest[:2] if len(rest) == 4 else (None, None), rest[-2:]
    pair = pl.program_id(0)
    attend_back_pair(
        True, pair, q_ref, k_ref, v_ref, gmixed_ref, probs_ref, gq_ref, gk_ref, gv_ref, sums_ref,
        dk_sum, dv_sum,
    )

    @pl.when(pair == PAIRS - 1)
    def _():
        late = [(first_ref, gv_ref), (mixed_ref, gself_ref)]
        early = [(first_ref, gq_ref), (first_ref, gk_ref)]
        put_products(core_ref, rows, plans[1], late, late_sent_ref, kept[0])
        put_products(core_ref, rows, plans[0], early, early_sent_ref, kept[1])


def term_specs(chains):
    specs = []
    for terms in chains:
        for term, at in terms:

            def place(step, spot_ref, at=at):
                bits = [((spot_ref[0] >> (which - 1)) & 1) * weight for which, _, weight in at]
                return (sum(bits, step), 0, 0)

            specs.append(pl.BlockSpec((1,) + term.shape[1:], place))
    return specs


def row_sums(squares):
    ones = jnp.ones((8, squares.shape[1]), jnp.bfloat16)
    high = squares.astype(jnp.bfloat16)
    left = (squares - high.astype(jnp.float32)).astype(jnp.bfloat16)
    return (dot(ones, high, NT) + dot(ones, left, NT))[:1]


def finish(terms, value_ref, rows_ref):
    count, rows, columns = value_ref.shape
    value = sum(term[0].astype(jnp.float32) for term in terms).reshape(count, rows, columns)
    value_ref[...] = value
    lines = []
    for k in range(count):
        squares = value[k] * value[k]
        rows_ref[k : k + 1] = row_sums(squares) * (1.0 / columns)
        lines.append(jnp.sum(squares, axis=0, keepdims=True))
    return lines


def zero_rows(count):
    return [jnp.zeros((1, D), jnp.float32)] * count


def ffn_last(counts, spot_ref, *refs):
    ins, outs, refs = refs[: counts[0]], refs[counts[0] : sum(counts)], refs[sum(counts) :]
    in_ref, in_rows_ref, out_ref, out_rows_ref, columns_ref = refs
    (wide,) = finish(ins, in_ref, in_rows_ref)
    lines = finish(outs, out_ref, out_rows_ref)
    lines = lines + [wide[:, at : at + D] for at in range(0, FF, D)]
    columns_ref[...] = jnp.concatenate(lines + zero_rows(8 - len(lines)), axis=0)


def cross_last(counts, spot_ref, *refs):
    value_ref, rows_ref, columns_ref = refs[counts[0] :]
    lines = finish(refs[: counts[0]], value_ref, rows_ref)
    columns_ref[...] = jnp.concatenate(lines + zero_rows(8 - len(lines)), axis=0)


def self_last(counts, spot_ref, *refs):
    one, two, refs = refs[: counts[0]], refs[counts[0] : sum(counts)], refs[sum(counts) :]
    cross_ref, ffn_ref, extra_ref, early_ref, early_rows_ref, late_ref, late_rows_ref, all_ref = refs
    lines = finish(one, early_ref, early_rows_ref) + finish(two, late_ref, late_rows_ref)
    all_ref[:8] = jnp.concatenate(lines + [cross_ref[:4]], axis=0)
    all_ref[8:16] = ffn_ref[...]
    all_ref[16:] = extra_ref[...]


def last_terms(kernel, spot, chains, shapes, extras, lines):
    asked = [chain.terms for chain in chains]
    outs = []
    for shape in shapes:
        outs += [shape, shape[:2]]
    outs.append((lines, D))
    whole = lambda shape: pl.BlockSpec(shape, lambda step, _: (0,) * len(shape))
    return pl.pallas_call(
        functools.partial(kernel, [len(terms) for terms in asked]),
        grid_spec=pltpu.PrefetchScalarGridSpec(
            num_scalar_prefetch=1,
            grid=(1,),
            in_specs=term_specs(asked) + [whole(extra.shape) for extra in extras],
            out_specs=[whole(shape) for shape in outs],
        ),
        out_shape=[jax.ShapeDtypeStruct(shape, jnp.float32) for shape in outs],
        compiler_params=pltpu.CompilerParams(vmem_limit_bytes=VMEM_BYTES),
        name=kernel.__name__,
    )(spot, *[term for terms in asked for term, _ in terms], *extras)


AXES = ("wide", "narrow")


def after(value, *others):
    return lax.optimization_barrier((value,) + others)[0]


class Cube:
    def __init__(self):
        self.count = lax.axis_size("wide") * lax.axis_size("narrow")
        self.bits = self.count.bit_length() - 1
        self.me = lax.axis_index("wide") * lax.axis_size("narrow") + lax.axis_index("narrow")
        high = [[which] for which in range(self.bits - 1, 1, -1)]
        self.plan_a = high + [[1]]
        self.plan_b = [[1]] + high
        self.plan_d = high[:1] + high[2:] + high[1:2] + [[1]]
        self.plan_e = [[1]] + high[:1] + high[2:] + high[1:2]
        self.plan_c = high[:1] + [[1]] + high[2:] + high[1:2]

    def bit(self, which):
        return (self.me >> which) & 1

    def swap(self, value, flip):
        return lax.ppermute(value, AXES, [(i, i ^ flip) for i in range(self.count)])

    def place(self, mine, theirs, axis):
        first = self.bit(0) == 0
        return jnp.where(
            first, jnp.concatenate([mine, theirs], axis), jnp.concatenate([theirs, mine], axis)
        )

    def half(self, value, whose):
        size = value.shape[-1] // 2
        return lax.dynamic_slice_in_dim(value, whose * size, size, value.ndim - 1)

    def total(self, value):
        for low in [0] + list(range(1, self.bits, 2)):
            top = 1 if low == 0 else min(2, self.bits - low)
            flips = [flip << low for flip in range(1, 1 << top)]
            value = value + sum(self.swap(value, flip) for flip in flips)
        return value


def flips_of(group):
    picks = range(1, 1 << len(group))
    return [sum(((pick >> k) & 1) << which for k, which in enumerate(group)) for pick in picks]


class Gather:
    def __init__(self, cube, value, plan):
        self.cube, self.plan, self.steps = cube, plan, 0
        self.held, self.parts = value[None], []

    def send(self, *behind):
        sent = after(self.held, *behind) if behind else self.held
        self.theirs = [self.cube.swap(sent, flip) for flip in flips_of(self.plan[self.steps])]
        self.steps += 1
        if self.steps == len(self.plan):
            self.parts = [self.held, self.cube.swap(sent, 1)]
        return sent

    def take(self, *behind):
        theirs = [after(their, *behind) if behind else their for their in self.theirs]
        if self.parts:
            self.parts = [self.parts[0], *theirs, self.parts[1], self.cube.swap(theirs[0], 1)]
        else:
            self.held = jnp.concatenate([self.held, *theirs], axis=0)


def pair_columns(cube, value, *behind):
    core = cube.bit(0)
    sent = cube.half(value, 1 - core)
    theirs = cube.swap(after(sent, *behind) if behind else sent, 1)
    return cube.half(value, core), theirs


class Sums:
    def __init__(self, cube, plan, sent, kept):
        self.cube, self.bits = cube, [which for group in reversed(plan) for which in group]
        self.blocks, self.theirs = cube.count // 2, cube.swap(sent, 1)
        self.terms = [(kept, [])]

    def take(self, *behind):
        self.terms.append((after(self.theirs, *behind) if behind else self.theirs, []))

    def begin(self, at):
        bits = [(self.cube.bit(which) ^ flip) * weight for which, flip, weight in at]
        return sum(bits, jnp.int32(0))

    def send(self):
        which = self.bits.pop(0)
        self.blocks //= 2
        parts = [
            lax.dynamic_slice_in_dim(
                term, self.begin(at + [(which, 1, self.blocks)]), self.blocks, 0
            ).astype(jnp.float32)
            for term, at in self.terms
        ]
        sent = sum(parts).astype(jnp.bfloat16)
        self.terms = [(term, at + [(which, 0, self.blocks)]) for term, at in self.terms]
        self.theirs = self.cube.swap(sent, 1 << which)
        return sent

    def going(self):
        return len(self.bits) > 0


def send_all(chains):
    return tuple([chain.send() for chain in chains])


def whole_tiles(cube):
    return cube.bits == 5


def product_outs(cube, count):
    if whole_tiles(cube):
        return [((cube.count // 2, count * (D // cube.count), D), jnp.bfloat16)] * 2
    return [((count, D, D), jnp.bfloat16)]


def product_sums(cube, plan, parts, *behind):
    chips = cube.count // 2
    if len(parts) == 1:
        count, _, columns = parts[0].shape
        grads = parts[0].reshape(count, chips, 2, -1, columns).transpose(2, 1, 0, 3, 4)
        grads = grads.reshape(2, chips, -1, columns)
        grads = jnp.take(grads, np.array(sums_order(plan)), axis=1)
        core = cube.bit(0)
        parts = [lax.dynamic_index_in_dim(grads, core ^ k, 0, False) for k in (1, 0)]
    sent, kept = [part.reshape(chips, -1, part.shape[-1]) for part in parts]
    return Sums(cube, plan, after(sent, *behind) if behind else sent, kept)


def chip_order(cube, parts, plan):
    places = jnp.concatenate(parts, axis=0)
    chips = chip_of(cube.me >> 1, jnp.arange(places.shape[0], dtype=jnp.int32), plan)
    moves = jnp.arange(places.shape[0], dtype=jnp.int32)[:, None] == chips[None, :]
    moved = jnp.dot(moves.astype(places.dtype), places.reshape(places.shape[0], -1))
    return moved.reshape(places.shape)


def on_device(
    tokens,
    memory,
    cotangent,
    dec_segments,
    enc_segments,
    dec_valid,
    attn_weights,
    w_in,
    w_out,
    norm_gains,
    rel_table,
    row_main,
    row_out,
    col_main,
    col_in,
):
    cube = Cube()
    core = cube.bit(0)
    spot = jnp.stack([cube.me >> 1, core])
    rows = attn_weights.shape[1]
    tiled = whole_tiles(cube)
    plans = cube.plan_a, cube.plan_b
    segment = dec_segments[0]
    see_self = self_mask(segment, dec_valid[0])
    see_cross = cross_mask(segment, enc_segments[0])
    lines = bias_lines(rel_table)
    distances = np.arange(2 * LANES)[:, None]
    places = (distances >= np.array(thresholds())[None, :]).sum(axis=1, keepdims=True)
    places = np.repeat(places == np.arange(BUCKETS)[None, :], HEADS, axis=1)
    places = jnp.asarray(places.astype(np.float32), jnp.bfloat16)
    tile, low, full = tokens.shape, jnp.bfloat16, jnp.float32
    square = ((D, D), low)
    probs = (HEADS, segment.shape[0], segment.shape[0])
    if tiled:
        attn_rows = attn_weights[:4].reshape(-1, D)
        gain_rows = jnp.pad(norm_gains, ((0, 5), (0, D // 2 - rows)))
        sent = jnp.concatenate([cube.half(attn_rows, 1 - core), gain_rows], axis=0)
        theirs = cube.swap(sent, 1)
        pairs = cube.place(
            cube.half(attn_rows, core).reshape(4, rows, -1),
            theirs[: 4 * rows].reshape(4, rows, -1),
            1,
        ).reshape(4 * 2 * rows, -1)
        gain_pair = cube.place(gain_rows, theirs[4 * rows :], 0)
        one = Gather(cube, jnp.concatenate([pairs[: 4 * rows], gain_pair], axis=0), cube.plan_a)
        two = Gather(cube, pairs[4 * rows :], cube.plan_c)
        ahead = one.send(), two.send()
        cross = pair_columns(cube, attn_weights[4:], *ahead)
        inner = pair_columns(cube, w_in, *ahead)
        outer = pair_columns(cube, w_out, *ahead)
        three = Gather(cube, cube.place(*cross, 1).reshape(8 * rows, -1), cube.plan_a)
        inner = Gather(cube, cube.place(*inner, 0), cube.plan_b)
        outer = Gather(cube, cube.place(*outer, 0), cube.plan_a)
        last = len(cube.plan_a) - 1
        for step in range(last):
            one.take()
            two.take()
            ahead = one.send(), two.send()
            if step > 0:
                three.take(*ahead)
            ahead = ahead + (three.send(*ahead),)
            if step > 1:
                inner.take(*ahead)
                outer.take(*ahead)
            if step > 0:
                inner.send(*ahead)
                outer.send(*ahead)
        one.take()
        two.take()
        ahead = one.parts[2], two.parts[2]
        three.take(*ahead)
        ahead = ahead + (three.send(*ahead),)
        inner.take(*ahead)
        outer.take(*ahead)
        ahead = ahead + (inner.send(*ahead), outer.send(*ahead))
        gain_full = chip_order(cube, [part[:, 4 * rows :, :rows] for part in one.parts[:2]], plans[0])
        gain_full = gain_full.reshape(-1, 2, 8, rows)[:, :, :3].transpose(2, 0, 1, 3)
        gain_full = gain_full.reshape(3, D)
        first_chunk, second_chunk = one.parts, two.parts
        gain_full = after(gain_full, *ahead)
    else:
        attn_full = lax.all_gather(attn_weights, AXES, axis=1, tiled=True)
        gain_full = lax.all_gather(norm_gains, AXES, axis=1, tiled=True)
        first_chunk, second_chunk = [attn_full[:2]], [attn_full[2:4]]
    gain_one, gain_two, gain_three = [gain_full[k : k + 1].astype(full) for k in range(3)]
    first_low, query, keys, values, self_probs, mixed_low, *weights = by_pair(
        functools.partial(self_part, (cube.plan_a, cube.plan_c)),
        [spot, tokens, gain_one, see_self, lines, *first_chunk, *second_chunk],
        [(tile, low)] * 4 + [(probs, low), (tile, low)] + [square] * 4,
        [],
        (probs, lines.shape),
        "self_part",
        early=(0, 1, 2, 3, 6, 7, 8, 9),
    )
    if tiled:
        three.take(mixed_low)
        cross_chunk = three.parts
        inner.take(mixed_low)
        outer.take(mixed_low)
        weights[3] = after(weights[3], inner.send(), outer.send())
    else:
        cross_chunk = [attn_full[4:]]
    (
        middle, second_low, cross_query, memory_keys, memory_values, cross_probs, crossed_low,
        upper, third_low, *cross_weights,
    ) = by_pair(
        functools.partial(cross_part, plans[0]),
        [
            spot, tokens, mixed_low, memory, gain_two, weights[3], gain_three, see_cross,
            *cross_chunk,
        ],
        [(tile, full)] + [(tile, low)] * 4 + [(probs, low), (tile, low), (tile, full), (tile, low)]
        + [square] * 4,
        [],
        (probs,),
        "cross_part",
        early=(0, 1, 2, 3, 4, 9, 10, 11, 12),
    )
    attn_full = weights + cross_weights
    if tiled:
        inner.take(third_low)
        outer.take(third_low)
        in_parts, out_parts = inner.parts, outer.parts
    else:
        in_parts = [lax.all_gather(w_in, AXES, axis=0, tiled=True)]
        out_parts = [lax.all_gather(w_out, AXES, axis=0, tiled=True)]
    layer_out, grad_third, *rest = ffn(
        spot, plans, third_low, upper, cotangent, in_parts, out_parts
    )
    half = len(rest) // 2
    parts = rest if tiled else [part[None] for part in rest]
    in_sums = product_sums(cube, cube.plan_b, parts[:half])
    out_sums = product_sums(cube, cube.plan_a, parts[half:])
    grad_upper, grad_cross_branch, grad_crossed, grad_gain_third = fused(
        third_back,
        [(tile, full), (tile, low), (tile, low), ((1, D), full)],
        grad_third,
        upper,
        cotangent,
        gain_three,
        attn_full[7],
    )
    in_sums.take(grad_crossed)
    started = send_all((in_sums,))
    out_sums.take(*started)
    grad_crossed = after(grad_crossed, *started, *send_all((out_sums,)))
    sums_scratch = [pltpu.VMEM((tile[0], LANES), full)] * 2
    memory_key_low, memory_value_low, grad_middle, grad_self_branch, grad_mixed, *rest = by_pair(
        functools.partial(cross_back, rows, plans),
        [
            core[None],
            cross_query,
            memory_keys,
            memory_values,
            grad_crossed,
            cross_probs,
            second_low,
            memory,
            crossed_low,
            grad_cross_branch,
            middle,
            grad_upper,
            gain_two,
            attn_full[4],
            attn_full[3],
        ],
        [(tile, low)] * 2
        + [(tile, full), (tile, low), (tile, low), ((1, D), full)]
        + product_outs(cube, 4),
        [pltpu.VMEM(tile, low)] + sums_scratch,
        (probs,),
        "cross_back",
        late=(6, 7, 8, 9, 10, 11, 13, 14),
    )
    grad_gain_second = rest[0]
    for each in (in_sums, out_sums):
        each.take(grad_mixed)
    arrived = in_sums.terms[-1][0], out_sums.terms[-1][0]
    cross_sums = product_sums(cube, cube.plan_a, rest[1:], *arrived)
    started = send_all((in_sums, out_sums))
    cross_sums.take(*started)
    grad_mixed = after(grad_mixed, *started, *send_all((cross_sums,)))
    lots = (PAIRS, 8, 2 * LANES)
    outs = product_outs(cube, 2)
    query_low, key_low, value_low, score_sums, *rest = by_pair(
        functools.partial(self_back, rows, (cube.plan_d, cube.plan_c)),
        [
            core[None],
            query,
            keys,
            values,
            grad_mixed,
            self_probs,
            first_low,
            mixed_low,
            grad_self_branch,
        ],
        [(tile, low)] * 3 + [(lots, full)] + outs[:1] * 2 + outs[1:] * 2,
        sums_scratch,
        (probs, lots),
        "self_back",
        late=(6, 7, 8),
    )
    for each in (in_sums, out_sums):
        each.take(query_low)
    arrived = in_sums.terms[-1][0], out_sums.terms[-1][0]
    late_sums = product_sums(cube, cube.plan_c, rest[::2], *arrived)
    early_sums = product_sums(cube, cube.plan_d, rest[1::2], *arrived)
    cross_sums.take(query_low)
    started = send_all((out_sums, in_sums, cross_sums))
    late_sums.take(*started)
    early_sums.take(*started)
    started = started + send_all((early_sums, late_sums))
    query_low = after(query_low, *started)
    grad_tokens, grad_memory, extra = fused(
        last_back,
        [(tile, full), (tile, full), ((8, D), full)],
        query_low,
        key_low,
        value_low,
        memory_key_low,
        memory_value_low,
        tokens,
        grad_middle,
        gain_one,
        *attn_full[:3],
        *attn_full[5:7],
        score_sums,
        places,
        grad_gain_second,
        grad_gain_third,
    )

    def move(chains, *behind):
        for each in chains:
            each.take(*behind)
        return send_all(chains)

    started = move((early_sums, late_sums, out_sums, in_sums), grad_tokens)
    move((cross_sums,), *started)
    started = move((early_sums, late_sums))
    while in_sums.going():
        move((out_sums, in_sums))
    while cross_sums.going():
        started = started + move((cross_sums,), *started)
    for each in (out_sums, in_sums):
        each.take(*started)
    grad_in, in_rows, grad_out, out_rows, ffn_columns = last_terms(
        ffn_last, spot, [in_sums, out_sums], [(1, rows, FF), (1, FF // cube.count, D)], [], 8
    )
    while early_sums.going():
        move((early_sums, late_sums), ffn_columns)
    cross_sums.take()
    cross_grads, cross_rows, cross_columns = last_terms(
        cross_last, spot, [cross_sums], [(4, rows, D)], [], 8
    )
    early_sums.take(cross_columns)
    late_sums.take(cross_columns)
    early_grads, early_rows, late_grads, late_rows, columns = last_terms(
        self_last,
        spot,
        [early_sums, late_sums],
        [(2, rows, D)] * 2,
        [cross_columns, ffn_columns, extra],
        24,
    )
    grad_attn = jnp.concatenate([early_grads, late_grads, cross_grads], axis=0)
    grad_in, grad_out = grad_in[0], grad_out[0]
    row_means = jnp.concatenate([early_rows, late_rows, cross_rows, in_rows], axis=0)
    new_row_main = DECAY * row_main + (1.0 - DECAY) * row_means
    new_row_out = DECAY * row_out + (1.0 - DECAY) * out_rows[0]
    columns = cube.total(columns)
    col_means = jnp.concatenate([columns[:8] / D, columns[8:9] / FF], axis=0)
    new_col_main = DECAY * col_main + (1.0 - DECAY) * col_means
    new_col_in = DECAY * col_in + (1.0 - DECAY) * (columns[9 : 9 + FF // D].reshape(FF) / D)
    grad_gains = lax.dynamic_slice_in_dim(columns[16:19], cube.me * rows, rows, 1)
    grad_table = columns[19, : BUCKETS * HEADS].reshape(BUCKETS, HEADS)
    return (
        layer_out,
        grad_tokens,
        grad_memory,
        grad_attn,
        grad_in,
        grad_out,
        grad_gains,
        grad_table,
        new_row_main,
        new_row_out,
        new_col_main,
        new_col_in,
    )


def solution(mesh):
    placed = (
        P(("wide", "narrow"), None),
        P(("wide", "narrow"), None),
        P(("wide", "narrow"), None),
        P(("wide", "narrow"), None),
        P(("wide", "narrow"), None),
        P(("wide", "narrow"), None),
        P(None, ("wide", "narrow"), None),
        P(("wide", "narrow"), None),
        P(("wide", "narrow"), None),
        P(None, ("wide", "narrow")),
        P(),
        P(None, ("wide", "narrow")),
        P(("wide", "narrow")),
        P(),
        P(),
    )
    return jax.shard_map(
        on_device,
        mesh=mesh,
        in_specs=placed,
        out_specs=(
            P(("wide", "narrow"), None),
            P(("wide", "narrow"), None),
            P(("wide", "narrow"), None),
            P(None, ("wide", "narrow"), None),
            P(("wide", "narrow"), None),
            P(("wide", "narrow"), None),
            P(None, ("wide", "narrow")),
            P(),
            P(None, ("wide", "narrow")),
            P(("wide", "narrow")),
            P(),
            P(),
        ),
        check_vma=False,
    )
```

```python
import functools
import math

import jax
import jax.numpy as jnp
import numpy as np
from jax import lax
from jax.experimental import pallas as pl
from jax.experimental.pallas import tpu as pltpu
from jax.sharding import PartitionSpec as P

D = 768
HEADS = 12
HEAD = 64
FF = 3072
BUCKETS = 32
MAXDIST = 128


EPSILON = 1e-06
DECAY = 0.8
NEGATIVE = -1e30


def thresholds():
    exact_count = BUCKETS // 2
    limits = list(range(1, exact_count + 1))
    for bucket_level in range(exact_count + 1, BUCKETS):
        limits.append(
            int(
                math.ceil(
                    exact_count
                    * (MAXDIST / exact_count) ** ((bucket_level - exact_count) / exact_count)
                )
            )
        )
    return limits


def bucket_table(distance, number_type):
    level_count = jnp.zeros(distance.shape, jnp.int32)
    for threshold in thresholds():
        level_count = level_count + (distance >= threshold).astype(jnp.int32)
    return (level_count[..., None] == jnp.arange(BUCKETS, dtype=jnp.int32)).astype(number_type)


def weight_grad(left_side, gradient):
    return lax.dot_general(
        left_side, gradient, (((0,), (0,)), ((), ())), preferred_element_type=jnp.float32
    )


LANES = 128
GROUP = LANES // HEAD
CUT = 256
VMEM_BYTES = 62 * 1024 * 1024

NT = (((1,), (1,)), ((), ()))
TN = (((0,), (0,)), ((), ()))


def dot(left, right, dims=(((1,), (0,)), ((), ()))):
    return lax.dot_general(left, right, dims, preferred_element_type=jnp.float32)


def spans(rows, causal):
    return [(at, at + CUT if causal else rows) for at in range(0, rows, CUT)]


def lane_mask(head):
    lanes = lax.broadcasted_iota(jnp.int32, (1, LANES), 1)
    return ((lanes // HEAD) == head).astype(jnp.float32)


def only_head(block, head, scale):
    return (block.astype(jnp.float32) * (lane_mask(head) * scale)).astype(jnp.bfloat16)


def near_bias(line_ref, head):
    line = jnp.broadcast_to(line_ref[0, head : head + 1], (LANES, 2 * LANES))
    return pltpu.roll(line, 0, 1, stride=1, stride_axis=0)


def add_bias(scores, bias, at):
    columns = []
    for first in range(0, CUT, LANES):
        rows = []
        for key in range(0, scores.shape[0], LANES):
            apart = at + first - key
            block = scores[key : key + LANES, first : first + LANES]
            if apart >= 2 * LANES:
                block = block + bias[:1, 2 * LANES - 1 :]
            elif apart >= 0:
                block = block + bias[:, apart : apart + LANES]
            rows.append(block)
        columns.append(jnp.concatenate(rows, axis=0))
    return jnp.concatenate(columns, axis=1)


def attend_pair(causal, pair, q_ref, k_ref, v_ref, mask_ref, line_ref, probs_ref, out_ref):
    rows = q_ref.shape[0]
    lanes = pl.ds(pl.multiple_of(pair * LANES, LANES), LANES)
    biases = [near_bias(line_ref, head) for head in range(GROUP)] if causal else None
    for at, depth in spans(rows, causal):
        keys, values = k_ref[:depth, lanes], v_ref[:depth, lanes]
        total = jnp.zeros((CUT, LANES), jnp.float32)
        for head in range(GROUP):
            query = only_head(q_ref[at : at + CUT, lanes], head, HEAD**-0.5)
            scores = dot(keys, query, NT)
            if causal:
                scores = add_bias(scores, biases[head], at)
            scores = scores + mask_ref[:depth, at : at + CUT]
            weights = jnp.exp(scores - jnp.max(scores, axis=0, keepdims=True))
            weights = weights * (1.0 / jnp.sum(weights, axis=0, keepdims=True))
            low = weights.astype(jnp.bfloat16)
            probs_ref[head, :depth, at : at + CUT] = low
            total = total + dot(low, values, TN) * lane_mask(head)
        out_ref[at : at + CUT, lanes] = total.astype(jnp.bfloat16)


def diagonal_sums(block):
    width = block.shape[1]
    slabs = [block[at : at + 8] for at in range(0, block.shape[0], 8)]
    total = slabs[0]
    for at, slab in enumerate(slabs[1:], 1):
        total = total + pltpu.roll(slab, width - 8 * at, 1)
    row = lax.broadcasted_iota(jnp.int32, total.shape, 0)
    for step in (1, 2, 4):
        total = jnp.where((row & step) != 0, pltpu.roll(total, width - step, 1), total)
    return jnp.sum(total, axis=0, keepdims=True)


def attend_back_pair(
    causal, pair, q_ref, k_ref, v_ref, g_ref, probs_ref, dq_ref, dk_ref, dv_ref, sums_ref,
    dk_sum, dv_sum,
):
    rows = q_ref.shape[0]
    lanes = pl.ds(pl.multiple_of(pair * LANES, LANES), LANES)
    dk_sum[...] = jnp.zeros_like(dk_sum)
    dv_sum[...] = jnp.zeros_like(dv_sum)
    near = [[], []]
    far = [[], []]
    for at, depth in spans(rows, causal):
        dq = jnp.zeros((CUT, LANES), jnp.float32)
        for head in range(GROUP):
            grad = only_head(g_ref[at : at + CUT, lanes], head, 1.0)
            query = only_head(q_ref[at : at + CUT, lanes], head, HEAD**-0.5)
            keys = only_head(k_ref[:depth, lanes], head, HEAD**-0.5)
            low = probs_ref[head, :depth, at : at + CUT]
            probs = low.astype(jnp.float32)
            scaled = probs * dot(v_ref[:depth, lanes], grad, NT)
            centre = jnp.sum(scaled, axis=0, keepdims=True)
            grad_scores = (scaled - probs * centre).astype(jnp.bfloat16)
            dv_sum[:depth] += dot(low, grad)
            dk_sum[:depth] += dot(grad_scores, query)
            dq = dq + dot(grad_scores, keys, TN)
            if causal:
                parts = grad_scores.astype(jnp.float32)
                for first in range(0, CUT, LANES):
                    own = at + first
                    column = parts[:, first : first + LANES]
                    if own:
                        before = column[own - LANES : own]
                    else:
                        before = jnp.zeros((LANES, LANES), jnp.float32)
                    near[head].append((column[own : own + LANES], before))
                    if own > LANES:
                        far[head].append(jnp.sum(column[: own - LANES], axis=0, keepdims=True))
        dq_ref[at : at + CUT, lanes] = dq.astype(jnp.bfloat16)
    dk_ref[:, lanes] = dk_sum[...].astype(jnp.bfloat16)
    dv_ref[:, lanes] = dv_sum[...].astype(jnp.bfloat16)
    if causal:
        lines = []
        for head in range(GROUP):
            own = sum(pair[0] for pair in near[head][1:]) + near[head][0][0]
            before = sum(pair[1] for pair in near[head][1:]) + near[head][0][1]
            lines.append(diagonal_sums(jnp.concatenate([own, before], axis=1)))
        for head in range(GROUP):
            line = sum(far[head][1:]) + far[head][0]
            lines.append(jnp.concatenate([line, jnp.zeros_like(line)], axis=1))
        lines.append(jnp.zeros((8 - len(lines), 2 * LANES), jnp.float32))
        sums_ref[0] = jnp.concatenate(lines, axis=0)


def self_mask(segment, key_valid):
    rows = segment.shape[0]
    index = jnp.arange(rows, dtype=jnp.int32)
    distance = index[None, :] - index[:, None]
    allowed = (
        (segment[:, None] == segment[None, :])
        & (distance >= 0)
        & ((key_valid[:, None] > 0) | (distance == 0))
    )
    return jnp.where(allowed, 0.0, NEGATIVE).astype(jnp.float32)


def cross_mask(segment, mem_segment):
    allowed = mem_segment[:, None] == segment[None, :]
    return jnp.where(allowed, 0.0, NEGATIVE).astype(jnp.float32)


def bias_lines(table):
    places = bucket_table(jnp.arange(2 * LANES, dtype=jnp.int32), jnp.float32)
    lines = jnp.einsum(
        "nb,bh->hn", places, table.astype(jnp.float32), precision=lax.Precision.HIGHEST
    )
    lines = lines.reshape(HEADS // GROUP, GROUP, 2 * LANES)
    return jnp.pad(lines, ((0, 0), (0, 8 - GROUP), (0, 0)))


GELU_SCALE = math.sqrt(2.0 / math.pi)
GELU_CUBE = 0.044715
BLOCK = 768
CUTS = FF // (2 * BLOCK)


def chip_of(chip, place, plan):
    bits = [which for group in plan for which in group]
    flip = sum(((place >> k) & 1) << (which - 1) for k, which in enumerate(bits))
    return chip ^ flip


def halves_of(core):
    half = D // 2
    mine = pl.ds(pl.multiple_of(core * half, half), half)
    return mine, pl.ds(pl.multiple_of((1 - core) * half, half), half)


def fill_weight(weight_ref, parts, at, spot_ref, plan):
    if len(parts) == 1:
        weight_ref[...] = parts[0][at]
        return
    blocks, rows = parts[0].shape[0], D // (2 * parts[0].shape[0])
    mine, other = halves_of(spot_ref[1])
    for place in range(2 * blocks):
        chip = chip_of(spot_ref[0], place, plan)
        lines = pl.ds(pl.multiple_of(chip * rows, rows), rows)
        which, block = divmod(place, blocks)
        weight_ref[lines, mine] = parts[which][block, at * rows : (at + 1) * rows]
        weight_ref[lines, other] = parts[2 + which][block, at * rows : (at + 1) * rows]


def sums_order(plan):
    bits = [which for group in plan for which in group]
    count = 1 << len(bits)
    return [sum(((k >> at) & 1) << (which - 1) for at, which in enumerate(bits)) for k in range(count)]


def divided(grads, rows, core):
    grads = grads.reshape(-1, 2, rows, grads.shape[1])
    even, odd = grads[:, 0], grads[:, 1]
    return jnp.where(core == 0, odd, even), jnp.where(core == 0, even, odd)


def ffn_kernel(tiled, plans, spot_ref, third_ref, upper_ref, cot_ref, *refs):
    step = pl.program_id(0)
    if tiled:
        own_in, other_in, out_parts, refs = refs[:2], refs[2:4], refs[4:8], refs[8:]
        layer_ref, gthird_ref, gin_ref, kept_gin_ref, gout_ref, kept_gout_ref = refs[:6]
        total, third_turned, in_block, out_block = refs[6:]
    else:
        in_block, out_block, layer_ref, gthird_ref, gin_ref, gout_ref = refs[:6]
        total, third_turned = refs[6:]

    @pl.when(step == 0)
    def _():
        total[...] = upper_ref[...]
        gthird_ref[...] = jnp.zeros_like(gthird_ref)
        third_turned[...] = third_ref[...].T

    def fill_in(parts):
        blocks, rows, _ = parts[0].shape
        for place in range(2 * blocks):
            chip = chip_of(spot_ref[0], place, plans[1])
            lines = pl.ds(pl.multiple_of(chip * rows, rows), rows)
            in_block[lines, :] = parts[place // blocks][place % blocks]

    if tiled:
        pl.when(step < CUTS)(lambda: fill_in(other_in))
        pl.when(step >= CUTS)(lambda: fill_in(own_in))
        mine, other = halves_of(spot_ref[1])
        rows = out_parts[0].shape[2]
        for place in range(4):
            chip = (spot_ref[0] & 3) ^ place
            lines = pl.ds(pl.multiple_of(chip * rows, rows), rows)
            out_block[lines, mine] = out_parts[place % 2][place // 2, 0]
            out_block[lines, other] = out_parts[2 + place % 2][place // 2, 0]

    inner = dot(third_ref[...], in_block[...])
    square = inner * inner
    slope = jnp.tanh(inner * (GELU_SCALE + (GELU_SCALE * GELU_CUBE) * square))
    half_up = 0.5 + 0.5 * slope
    active = (inner * half_up).astype(jnp.bfloat16)
    total[...] += dot(active, out_block[...])
    grad_active = dot(cot_ref[...], out_block[...], NT)
    bend = (0.5 * inner) * (1.0 - slope * slope)
    bend = bend * (GELU_SCALE + (3.0 * GELU_SCALE * GELU_CUBE) * square)
    grad_inner = (grad_active * (half_up + bend)).astype(jnp.bfloat16)
    gthird_ref[...] += dot(grad_inner, in_block[...], NT)
    grad_in = dot(third_turned[...], grad_inner)
    grad_out = dot(active, cot_ref[...], TN)
    if tiled:
        chips = 2 * own_in[0].shape[0]
        order = sums_order(plans[1])
        parts = divided(grad_in, D // (2 * chips), spot_ref[1])
        for part, result in zip(parts, (gin_ref, kept_gin_ref)):
            part = jnp.concatenate([part[chip] for chip in order], axis=0)
            result[...] = part.astype(jnp.bfloat16)
        parts = divided(grad_out, FF // (2 * chips), spot_ref[1])
        for part, result in zip(parts, (gout_ref, kept_gout_ref)):
            for place in range(4):
                chip = (place >> 1) | ((place & 1) << 1)
                result[place, 0] = part[chip].astype(jnp.bfloat16)
    else:
        gin_ref[...] = grad_in.astype(jnp.bfloat16)
        gout_ref[...] = grad_out.astype(jnp.bfloat16)

    @pl.when(step == 2 * CUTS - 1)
    def _():
        layer_ref[...] = total[...].astype(jnp.bfloat16)


def ffn(spot, plans, third, upper, cotangent, in_parts, out_parts):
    rows = third.shape[0]
    tiled = len(in_parts) > 1

    def block(step, spot_ref):
        return ((1 - spot_ref[1]) * CUTS + step) % (2 * CUTS)

    def line(step, spot_ref):
        flips = block(step, spot_ref) ^ (spot_ref[0] >> 2)
        return (0, (flips >> 1) + 2 * (flips & 1), 0, 0)

    whole = pl.BlockSpec((rows, D), lambda step, spot_ref: (0, 0))
    across = lambda step, spot_ref: (0, block(step, spot_ref))
    down = lambda step, spot_ref: (block(step, spot_ref), 0)
    scratch = [pltpu.VMEM((rows, D), jnp.float32), pltpu.VMEM((D, rows), jnp.bfloat16)]
    if tiled:
        chips, lines, _ = in_parts[0].shape
        late = lambda step, spot_ref: (0, 0, jnp.maximum(step - CUTS, 0))
        early = lambda step, spot_ref: (0, 0, jnp.minimum(step, CUTS - 1))
        in_specs = [pl.BlockSpec((chips, lines, BLOCK), late)] * 2
        in_specs += [pl.BlockSpec((chips, lines, BLOCK), early)] * 2
        out_parts = [part.reshape(2, 4, -1, D // 2) for part in out_parts]
        in_specs += [pl.BlockSpec((2, 1) + out_parts[0].shape[2:], line)] * 4
        out_specs = [pl.BlockSpec((D // 2, BLOCK), across)] * 2
        own = lambda step, spot_ref: (0, (b := block(step, spot_ref)) // 2 + 2 * (b % 2), 0, 0)
        out_specs += [pl.BlockSpec((4, 1, FF // (4 * chips), D), own)] * 2
        shapes = [(D // 2, FF)] * 2 + [(4, 4, FF // (4 * chips), D)] * 2
        scratch += [pltpu.VMEM((D, BLOCK), jnp.bfloat16), pltpu.VMEM((BLOCK, D), jnp.bfloat16)]
    else:
        in_specs = [pl.BlockSpec((D, BLOCK), across), pl.BlockSpec((BLOCK, D), down)]
        out_specs, shapes = in_specs, [(D, FF), (FF, D)]
    return pl.pallas_call(
        functools.partial(ffn_kernel, tiled, plans),
        grid_spec=pltpu.PrefetchScalarGridSpec(
            num_scalar_prefetch=1,
            grid=(2 * CUTS,),
            in_specs=[whole, whole, whole] + in_specs,
            out_specs=[whole, whole] + out_specs,
            scratch_shapes=scratch,
        ),
        out_shape=[
            jax.ShapeDtypeStruct((rows, D), jnp.bfloat16),
            jax.ShapeDtypeStruct((rows, D), jnp.float32),
        ]
        + [jax.ShapeDtypeStruct(shape, jnp.bfloat16) for shape in shapes],
        compiler_params=pltpu.CompilerParams(vmem_limit_bytes=VMEM_BYTES),
        name="ffn",
    )(spot, third, upper, cotangent, *in_parts, *out_parts)


def scale_of(hidden):
    return lax.rsqrt(jnp.mean(hidden * hidden, axis=-1, keepdims=True) + EPSILON)


def norm_back(hidden, gain, grad):
    scale = scale_of(hidden)
    grown = grad * gain
    inner = jnp.mean(grown * hidden, axis=-1, keepdims=True)
    gain_grad = jnp.sum(grad * (hidden * scale), axis=0, keepdims=True)
    return scale * grown - hidden * (scale * scale * scale * inner), gain_grad


def fused(kernel, outs, *args):
    space = pl.BlockSpec(memory_space=pltpu.VMEM)
    return pl.pallas_call(
        kernel,
        in_specs=[space] * len(args),
        out_specs=[space] * len(outs),
        out_shape=[jax.ShapeDtypeStruct(shape, held_as) for shape, held_as in outs],
        compiler_params=pltpu.CompilerParams(vmem_limit_bytes=VMEM_BYTES),

        name=kernel.__name__,
    )(*args)


PAIRS = HEADS // GROUP


def whole_spec(array, space=None):
    rank = len(array.shape)
    return pl.BlockSpec(array.shape, lambda pair: (0,) * rank, pipeline_mode=space)


def by_pair(kernel, args, outs, scratch, by_step, name, late=(), early=()):
    held = [jax.ShapeDtypeStruct(shape, held_as) for shape, held_as in outs]
    beside = pl.BlockSpec(memory_space=pl.ANY)
    buffers = [args[k] for k in late] + [held[k] for k in early]
    count = len(args) + len(held) + len(scratch)

    def body(*refs):
        pair = pl.program_id(0)
        refs, places, arrived = list(refs[:count]), refs[count:-1], refs[-1]
        wanted = list(late) + [len(args) + k for k in early]
        copies = []
        for k, (at, place) in enumerate(zip(wanted, places)):
            ends = (refs[at], place) if k < len(late) else (place, refs[at])
            copies.append(pltpu.make_async_copy(*ends, arrived.at[k]))
            refs[at] = place
        loads, stores = copies[: len(late)], copies[len(late) :]

        @pl.when(pair == 0)
        def _():
            for copy in loads:
                copy.start()

        @pl.when(pair == PAIRS - 1)
        def _():
            for copy in loads:
                copy.wait()

        kernel(*refs)

        @pl.when(pair == 0)
        def _():
            for copy in stores:
                copy.start()

        @pl.when(pair == PAIRS - 1)
        def _():
            for copy in stores:
                copy.wait()

    def spec(array, once):
        if len(array.shape) == 3 and array.shape in by_step:
            block = (array.shape[0] // PAIRS,) + array.shape[1:]
            return pl.BlockSpec(block, lambda pair: (pair, 0, 0))
        if len(array.shape) == 1:
            return pl.BlockSpec(memory_space=pltpu.SMEM)
        return whole_spec(array, pl.Buffered(1) if once else None)

    in_specs = [beside if k in late else spec(array, True) for k, array in enumerate(args)]
    out_specs = [beside if k in early else spec(array, False) for k, array in enumerate(held)]
    if not buffers:
        body = kernel
    else:
        scratch = scratch + [pltpu.VMEM(array.shape, array.dtype) for array in buffers]
        scratch.append(pltpu.SemaphoreType.DMA((len(buffers),)))
    return pl.pallas_call(
        body,
        grid=(PAIRS,),
        in_specs=in_specs,
        out_specs=out_specs,
        out_shape=held,
        scratch_shapes=scratch,
        compiler_params=pltpu.CompilerParams(vmem_limit_bytes=VMEM_BYTES),
        name=name,
    )(*args)


def self_part(plans, spot_ref, tokens_ref, gain_ref, mask_ref, line_ref, *refs):
    count = (len(refs) - 10) // 2
    one, two, refs = refs[:count], refs[count : 2 * count], refs[2 * count :]
    first_ref, q_ref, k_ref, v_ref, probs_ref, mixed_ref, wq_ref, wk_ref, wv_ref, wo_ref = refs
    pair = pl.program_id(0)

    @pl.when(pair == 0)
    def _():
        hidden = tokens_ref[...].astype(jnp.float32)
        first = (hidden * scale_of(hidden) * gain_ref[...]).astype(jnp.bfloat16)
        first_ref[...] = first
        weights = [(wq_ref, one, 0, q_ref), (wk_ref, one, 1, k_ref), (wv_ref, two, 0, v_ref)]
        for weight_ref, parts, at, result in weights:
            fill_weight(weight_ref, parts, at, spot_ref, plans[parts is two])
            result[...] = dot(first, weight_ref[...]).astype(jnp.bfloat16)
        fill_weight(wo_ref, two, 1, spot_ref, plans[1])

    attend_pair(True, pair, q_ref, k_ref, v_ref, mask_ref, line_ref, probs_ref, mixed_ref)


def cross_part(
    plan, spot_ref, tokens_ref, mixed_ref, memory_ref, gain_ref, wso_ref, next_gain_ref, mask_ref,
    *refs,
):
    parts, refs = refs[:-13], refs[-13:]
    middle_ref, second_ref, q_ref, k_ref, v_ref, probs_ref, crossed_ref = refs[:7]
    upper_ref, third_ref, wq_ref, wk_ref, wv_ref, wo_ref = refs[7:]
    pair = pl.program_id(0)

    @pl.when(pair == 0)
    def _():
        for at, weight_ref in enumerate((wq_ref, wk_ref, wv_ref, wo_ref)):
            fill_weight(weight_ref, parts, at, spot_ref, plan)
        middle = tokens_ref[...].astype(jnp.float32) + dot(mixed_ref[...], wso_ref[...])
        middle_ref[...] = middle
        second = (middle * scale_of(middle) * gain_ref[...]).astype(jnp.bfloat16)
        second_ref[...] = second
        q_ref[...] = dot(second, wq_ref[...]).astype(jnp.bfloat16)
        k_ref[...] = dot(memory_ref[...], wk_ref[...]).astype(jnp.bfloat16)
        v_ref[...] = dot(memory_ref[...], wv_ref[...]).astype(jnp.bfloat16)

    attend_pair(False, pair, q_ref, k_ref, v_ref, mask_ref, None, probs_ref, crossed_ref)

    @pl.when(pair == PAIRS - 1)
    def _():
        upper = middle_ref[...] + dot(crossed_ref[...], wo_ref[...])
        upper_ref[...] = upper
        third = upper * scale_of(upper) * next_gain_ref[...]
        third_ref[...] = third.astype(jnp.bfloat16)


def third_back(
    gthird_ref, upper_ref, cot_ref, gain_ref, wo_ref, gupper_ref, branch_ref, gmix_ref, ggain_ref
):
    grad, ggain_ref[...] = norm_back(upper_ref[...], gain_ref[...], gthird_ref[...])
    grad = cot_ref[...].astype(jnp.float32) + grad
    gupper_ref[...] = grad
    low = grad.astype(jnp.bfloat16)
    branch_ref[...] = low
    gmix_ref[...] = dot(low, wo_ref[...], NT).astype(jnp.bfloat16)


def last_back(
    gq_ref, gk_ref, gv_ref, gmk_ref, gmv_ref, tokens_ref, gmiddle_ref, gain_ref,
    wq_ref, wk_ref, wv_ref, wmk_ref, wmv_ref,
    sums_ref, places_ref, ggain_two_ref, ggain_three_ref, gtokens_ref, gmemory_ref, extra_ref,
):
    near = sums_ref[:, :GROUP].reshape(HEADS, 2 * LANES)
    far = jnp.sum(sums_ref[:, GROUP : 2 * GROUP].reshape(HEADS, 2 * LANES), axis=1, keepdims=True)
    high = near.astype(jnp.bfloat16)
    left = near - high.astype(jnp.float32)
    middle = left.astype(jnp.bfloat16)
    least = (left - middle.astype(jnp.float32)).astype(jnp.bfloat16)
    places = places_ref[...]
    lane = lax.broadcasted_iota(jnp.int32, (HEADS, BUCKETS * HEADS), 1)
    head = lax.broadcasted_iota(jnp.int32, (HEADS, BUCKETS * HEADS), 0)
    table = dot(high, places) + dot(middle, places) + dot(least, places)
    table = table + jnp.where(lane // HEADS == BUCKETS - 1, far, 0.0)
    table = jnp.sum(jnp.where(lane % HEADS == head, table, 0.0), axis=0, keepdims=True)
    table = jnp.concatenate([table, jnp.zeros((1, D - table.shape[1]), jnp.float32)], axis=1)
    gmemory_ref[...] = dot(gmk_ref[...], wmk_ref[...], NT) + dot(gmv_ref[...], wmv_ref[...], NT)
    gfirst = dot(gq_ref[...], wq_ref[...], NT) + dot(gk_ref[...], wk_ref[...], NT)
    gfirst = gfirst + dot(gv_ref[...], wv_ref[...], NT)
    hidden = tokens_ref[...].astype(jnp.float32)
    grad, ggain = norm_back(hidden, gain_ref[...], gfirst)
    gtokens_ref[...] = gmiddle_ref[...] + grad
    lines = [ggain, ggain_two_ref[...], ggain_three_ref[...], table] + zero_rows(4)
    extra_ref[...] = jnp.concatenate(lines, axis=0)


def put_products(core_ref, rows, plan, pairs, sent_ref, kept_ref):
    if kept_ref is None:
        for k, (left, right) in enumerate(pairs):
            sent_ref[k] = dot(left[...], right[...], TN).astype(jnp.bfloat16)
        return
    parts = [divided(dot(left[...], right[...], TN), rows, core_ref[0]) for left, right in pairs]
    for which, result in enumerate((sent_ref, kept_ref)):
        for place, chip in enumerate(sums_order(plan)):
            lines = jnp.concatenate([part[which][chip] for part in parts], axis=0)
            result[place] = lines.astype(jnp.bfloat16)


def cross_back(
    rows, plans, core_ref, q_ref, k_ref, v_ref, gcrossed_ref, probs_ref,
    second_ref, memory_ref, crossed_ref, gcross_ref, middle_ref, gupper_ref, gain_ref,
    wq_ref, wso_ref,
    gk_ref, gv_ref, gmiddle_ref, branch_ref, gmix_ref, ggain_ref, sent_ref, *rest,
):
    kept_ref, (gq_ref, dk_sum, dv_sum) = rest[0] if len(rest) == 4 else None, rest[-3:]
    pair = pl.program_id(0)
    attend_back_pair(
        False, pair, q_ref, k_ref, v_ref, gcrossed_ref, probs_ref, gq_ref, gk_ref, gv_ref, None,
        dk_sum, dv_sum,
    )

    @pl.when(pair == PAIRS - 1)
    def _():
        pairs = [
            (second_ref, gq_ref),
            (memory_ref, gk_ref),
            (memory_ref, gv_ref),
            (crossed_ref, gcross_ref),
        ]
        put_products(core_ref, rows, plans[0], pairs, sent_ref, kept_ref)
        gsecond = dot(gq_ref[...], wq_ref[...], NT)
        grad, ggain_ref[...] = norm_back(middle_ref[...], gain_ref[...], gsecond)
        grad = gupper_ref[...] + grad
        gmiddle_ref[...] = grad
        low = grad.astype(jnp.bfloat16)
        branch_ref[...] = low
        gmix_ref[...] = dot(low, wso_ref[...], NT).astype(jnp.bfloat16)


def self_back(
    rows, plans, core_ref, q_ref, k_ref, v_ref, gmixed_ref, probs_ref, first_ref, mixed_ref, gself_ref,
    gq_ref, gk_ref, gv_ref, sums_ref, late_sent_ref, early_sent_ref, *rest,
):
    kept, (dk_sum, dv_sum) = rest[:2] if len(rest) == 4 else (None, None), rest[-2:]
    pair = pl.program_id(0)
    attend_back_pair(
        True, pair, q_ref, k_ref, v_ref, gmixed_ref, probs_ref, gq_ref, gk_ref, gv_ref, sums_ref,
        dk_sum, dv_sum,
    )

    @pl.when(pair == PAIRS - 1)
    def _():
        late = [(first_ref, gv_ref), (mixed_ref, gself_ref)]
        early = [(first_ref, gq_ref), (first_ref, gk_ref)]
        put_products(core_ref, rows, plans[1], late, late_sent_ref, kept[0])
        put_products(core_ref, rows, plans[0], early, early_sent_ref, kept[1])


def term_specs(chains):
    specs = []
    for terms in chains:
        for term, at in terms:

            def place(step, spot_ref, at=at):
                bits = [((spot_ref[0] >> (which - 1)) & 1) * weight for which, _, weight in at]
                return (sum(bits, step), 0, 0)

            specs.append(pl.BlockSpec((1,) + term.shape[1:], place))
    return specs


def row_sums(squares):
    ones = jnp.ones((8, squares.shape[1]), jnp.bfloat16)
    high = squares.astype(jnp.bfloat16)
    left = (squares - high.astype(jnp.float32)).astype(jnp.bfloat16)
    return (dot(ones, high, NT) + dot(ones, left, NT))[:1]


def finish(terms, value_ref, rows_ref):
    count, rows, columns = value_ref.shape
    value = sum(term[0].astype(jnp.float32) for term in terms).reshape(count, rows, columns)
    value_ref[...] = value
    lines = []
    for k in range(count):
        squares = value[k] * value[k]
        rows_ref[k : k + 1] = row_sums(squares) * (1.0 / columns)
        lines.append(jnp.sum(squares, axis=0, keepdims=True))
    return lines


def zero_rows(count):
    return [jnp.zeros((1, D), jnp.float32)] * count


def ffn_last(counts, spot_ref, *refs):
    ins, outs, refs = refs[: counts[0]], refs[counts[0] : sum(counts)], refs[sum(counts) :]
    in_ref, in_rows_ref, out_ref, out_rows_ref, columns_ref = refs
    (wide,) = finish(ins, in_ref, in_rows_ref)
    lines = finish(outs, out_ref, out_rows_ref)
    lines = lines + [wide[:, at : at + D] for at in range(0, FF, D)]
    columns_ref[...] = jnp.concatenate(lines + zero_rows(8 - len(lines)), axis=0)


def cross_last(counts, spot_ref, *refs):
    value_ref, rows_ref, columns_ref = refs[counts[0] :]
    lines = finish(refs[: counts[0]], value_ref, rows_ref)
    columns_ref[...] = jnp.concatenate(lines + zero_rows(8 - len(lines)), axis=0)


def self_last(counts, spot_ref, *refs):
    one, two, refs = refs[: counts[0]], refs[counts[0] : sum(counts)], refs[sum(counts) :]
    cross_ref, ffn_ref, extra_ref, early_ref, early_rows_ref, late_ref, late_rows_ref, all_ref = refs
    lines = finish(one, early_ref, early_rows_ref) + finish(two, late_ref, late_rows_ref)
    all_ref[:8] = jnp.concatenate(lines + [cross_ref[:4]], axis=0)
    all_ref[8:16] = ffn_ref[...]
    all_ref[16:] = extra_ref[...]


def last_terms(kernel, spot, chains, shapes, extras, lines):
    asked = [chain.terms for chain in chains]
    outs = []
    for shape in shapes:
        outs += [shape, shape[:2]]
    outs.append((lines, D))
    whole = lambda shape: pl.BlockSpec(shape, lambda step, _: (0,) * len(shape))
    return pl.pallas_call(
        functools.partial(kernel, [len(terms) for terms in asked]),
        grid_spec=pltpu.PrefetchScalarGridSpec(
            num_scalar_prefetch=1,
            grid=(1,),
            in_specs=term_specs(asked) + [whole(extra.shape) for extra in extras],
            out_specs=[whole(shape) for shape in outs],
        ),
        out_shape=[jax.ShapeDtypeStruct(shape, jnp.float32) for shape in outs],
        compiler_params=pltpu.CompilerParams(vmem_limit_bytes=VMEM_BYTES),
        name=kernel.__name__,
    )(spot, *[term for terms in asked for term, _ in terms], *extras)


AXES = ("wide", "narrow")


def after(value, *others):
    return lax.optimization_barrier((value,) + others)[0]


class Cube:
    def __init__(self):
        self.count = lax.axis_size("wide") * lax.axis_size("narrow")
        self.bits = self.count.bit_length() - 1
        self.me = lax.axis_index("wide") * lax.axis_size("narrow") + lax.axis_index("narrow")
        high = [[which] for which in range(self.bits - 1, 1, -1)]
        self.plan_a = high + [[1]]
        self.plan_b = [[1]] + high
        self.plan_d = high[:1] + high[2:] + high[1:2] + [[1]]
        self.plan_e = [[1]] + high[:1] + high[2:] + high[1:2]
        self.plan_c = high[:1] + [[1]] + high[2:] + high[1:2]

    def bit(self, which):
        return (self.me >> which) & 1

    def swap(self, value, flip):
        return lax.ppermute(value, AXES, [(i, i ^ flip) for i in range(self.count)])

    def place(self, mine, theirs, axis):
        first = self.bit(0) == 0
        return jnp.where(
            first, jnp.concatenate([mine, theirs], axis), jnp.concatenate([theirs, mine], axis)
        )

    def half(self, value, whose):
        size = value.shape[-1] // 2
        return lax.dynamic_slice_in_dim(value, whose * size, size, value.ndim - 1)

    def total(self, value):
        for low in [0] + list(range(1, self.bits, 2)):
            top = 1 if low == 0 else min(2, self.bits - low)
            flips = [flip << low for flip in range(1, 1 << top)]
            value = value + sum(self.swap(value, flip) for flip in flips)
        return value


def flips_of(group):
    picks = range(1, 1 << len(group))
    return [sum(((pick >> k) & 1) << which for k, which in enumerate(group)) for pick in picks]


class Gather:
    def __init__(self, cube, value, plan):
        self.cube, self.plan, self.steps = cube, plan, 0
        self.held, self.parts = value[None], []

    def send(self, *behind):
        sent = after(self.held, *behind) if behind else self.held
        self.theirs = [self.cube.swap(sent, flip) for flip in flips_of(self.plan[self.steps])]
        self.steps += 1
        if self.steps == len(self.plan):
            self.parts = [self.held, self.cube.swap(sent, 1)]
        return sent

    def take(self, *behind):
        theirs = [after(their, *behind) if behind else their for their in self.theirs]
        if self.parts:
            self.parts = [self.parts[0], *theirs, self.parts[1], self.cube.swap(theirs[0], 1)]
        else:
            self.held = jnp.concatenate([self.held, *theirs], axis=0)


def pair_columns(cube, value, *behind):
    core = cube.bit(0)
    sent = cube.half(value, 1 - core)
    theirs = cube.swap(after(sent, *behind) if behind else sent, 1)
    return cube.half(value, core), theirs


class Sums:
    def __init__(self, cube, plan, sent, kept):
        self.cube, self.bits = cube, [which for group in reversed(plan) for which in group]
        self.blocks, self.theirs = cube.count // 2, cube.swap(sent, 1)
        self.terms = [(kept, [])]

    def take(self, *behind):
        self.terms.append((after(self.theirs, *behind) if behind else self.theirs, []))

    def begin(self, at):
        bits = [(self.cube.bit(which) ^ flip) * weight for which, flip, weight in at]
        return sum(bits, jnp.int32(0))

    def send(self):
        which = self.bits.pop(0)
        self.blocks //= 2
        parts = [
            lax.dynamic_slice_in_dim(
                term, self.begin(at + [(which, 1, self.blocks)]), self.blocks, 0
            ).astype(jnp.float32)
            for term, at in self.terms
        ]
        sent = sum(parts).astype(jnp.bfloat16)
        self.terms = [(term, at + [(which, 0, self.blocks)]) for term, at in self.terms]
        self.theirs = self.cube.swap(sent, 1 << which)
        return sent

    def going(self):
        return len(self.bits) > 0


def send_all(chains):
    return tuple([chain.send() for chain in chains])


def whole_tiles(cube):
    return cube.bits == 5


def product_outs(cube, count):
    if whole_tiles(cube):
        return [((cube.count // 2, count * (D // cube.count), D), jnp.bfloat16)] * 2
    return [((count, D, D), jnp.bfloat16)]


def product_sums(cube, plan, parts, *behind):
    chips = cube.count // 2
    if len(parts) == 1:
        count, _, columns = parts[0].shape
        grads = parts[0].reshape(count, chips, 2, -1, columns).transpose(2, 1, 0, 3, 4)
        grads = grads.reshape(2, chips, -1, columns)
        grads = jnp.take(grads, np.array(sums_order(plan)), axis=1)
        core = cube.bit(0)
        parts = [lax.dynamic_index_in_dim(grads, core ^ k, 0, False) for k in (1, 0)]
    sent, kept = [part.reshape(chips, -1, part.shape[-1]) for part in parts]
    return Sums(cube, plan, after(sent, *behind) if behind else sent, kept)


def chip_order(cube, parts, plan):
    places = jnp.concatenate(parts, axis=0)
    chips = chip_of(cube.me >> 1, jnp.arange(places.shape[0], dtype=jnp.int32), plan)
    moves = jnp.arange(places.shape[0], dtype=jnp.int32)[:, None] == chips[None, :]
    moved = jnp.dot(moves.astype(places.dtype), places.reshape(places.shape[0], -1))
    return moved.reshape(places.shape)


def on_device(
    tokens,
    memory,
    cotangent,
    dec_segments,
    enc_segments,
    dec_valid,
    attn_weights,
    w_in,
    w_out,
    norm_gains,
    rel_table,
    row_main,
    row_out,
    col_main,
    col_in,
):
    cube = Cube()
    core = cube.bit(0)
    spot = jnp.stack([cube.me >> 1, core])
    rows = attn_weights.shape[1]
    tiled = whole_tiles(cube)
    plans = cube.plan_a, cube.plan_b
    segment = dec_segments[0]
    see_self = self_mask(segment, dec_valid[0])
    see_cross = cross_mask(segment, enc_segments[0])
    lines = bias_lines(rel_table)
    distances = np.arange(2 * LANES)[:, None]
    places = (distances >= np.array(thresholds())[None, :]).sum(axis=1, keepdims=True)
    places = np.repeat(places == np.arange(BUCKETS)[None, :], HEADS, axis=1)
    places = jnp.asarray(places.astype(np.float32), jnp.bfloat16)
    tile, low, full = tokens.shape, jnp.bfloat16, jnp.float32
    square = ((D, D), low)
    probs = (HEADS, segment.shape[0], segment.shape[0])
    if tiled:
        attn_rows = attn_weights[:4].reshape(-1, D)
        gain_rows = jnp.pad(norm_gains, ((0, 5), (0, D // 2 - rows)))
        sent = jnp.concatenate([cube.half(attn_rows, 1 - core), gain_rows], axis=0)
        theirs = cube.swap(sent, 1)
        pairs = cube.place(
            cube.half(attn_rows, core).reshape(4, rows, -1),
            theirs[: 4 * rows].reshape(4, rows, -1),
            1,
        ).reshape(4 * 2 * rows, -1)
        gain_pair = cube.place(gain_rows, theirs[4 * rows :], 0)
        one = Gather(cube, jnp.concatenate([pairs[: 4 * rows], gain_pair], axis=0), cube.plan_a)
        two = Gather(cube, pairs[4 * rows :], cube.plan_c)
        ahead = one.send(), two.send()
        cross = pair_columns(cube, attn_weights[4:], *ahead)
        inner = pair_columns(cube, w_in, *ahead)
        outer = pair_columns(cube, w_out, *ahead)
        three = Gather(cube, cube.place(*cross, 1).reshape(8 * rows, -1), cube.plan_a)
        inner = Gather(cube, cube.place(*inner, 0), cube.plan_b)
        outer = Gather(cube, cube.place(*outer, 0), cube.plan_a)
        last = len(cube.plan_a) - 1
        for step in range(last):
            one.take()
            two.take()
            ahead = one.send(), two.send()
            if step > 0:
                three.take(*ahead)
            ahead = ahead + (three.send(*ahead),)
            if step > 1:
                inner.take(*ahead)
                outer.take(*ahead)
            if step > 0:
                inner.send(*ahead)
                outer.send(*ahead)
        one.take()
        two.take()
        ahead = one.parts[2], two.parts[2]
        three.take(*ahead)
        ahead = ahead + (three.send(*ahead),)
        inner.take(*ahead)
        outer.take(*ahead)
        ahead = ahead + (inner.send(*ahead), outer.send(*ahead))
        gain_full = chip_order(cube, [part[:, 4 * rows :, :rows] for part in one.parts[:2]], plans[0])
        gain_full = gain_full.reshape(-1, 2, 8, rows)[:, :, :3].transpose(2, 0, 1, 3)
        gain_full = gain_full.reshape(3, D)
        first_chunk, second_chunk = one.parts, two.parts
        gain_full = after(gain_full, *ahead)
    else:
        attn_full = lax.all_gather(attn_weights, AXES, axis=1, tiled=True)
        gain_full = lax.all_gather(norm_gains, AXES, axis=1, tiled=True)
        first_chunk, second_chunk = [attn_full[:2]], [attn_full[2:4]]
    gain_one, gain_two, gain_three = [gain_full[k : k + 1].astype(full) for k in range(3)]
    first_low, query, keys, values, self_probs, mixed_low, *weights = by_pair(
        functools.partial(self_part, (cube.plan_a, cube.plan_c)),
        [spot, tokens, gain_one, see_self, lines, *first_chunk, *second_chunk],
        [(tile, low)] * 4 + [(probs, low), (tile, low)] + [square] * 4,
        [],
        (probs, lines.shape),
        "self_part",
        early=(0, 1, 2, 3, 6, 7, 8, 9),
    )
    if tiled:
        three.take(mixed_low)
        cross_chunk = three.parts
        inner.take(mixed_low)
        outer.take(mixed_low)
        weights[3] = after(weights[3], inner.send(), outer.send())
    else:
        cross_chunk = [attn_full[4:]]
    (
        middle, second_low, cross_query, memory_keys, memory_values, cross_probs, crossed_low,
        upper, third_low, *cross_weights,
    ) = by_pair(
        functools.partial(cross_part, plans[0]),
        [
            spot, tokens, mixed_low, memory, gain_two, weights[3], gain_three, see_cross,
            *cross_chunk,
        ],
        [(tile, full)] + [(tile, low)] * 4 + [(probs, low), (tile, low), (tile, full), (tile, low)]
        + [square] * 4,
        [],
        (probs,),
        "cross_part",
        early=(0, 1, 2, 3, 4, 9, 10, 11, 12),
    )
    attn_full = weights + cross_weights
    if tiled:
        inner.take(third_low)
        outer.take(third_low)
        in_parts, out_parts = inner.parts, outer.parts
    else:
        in_parts = [lax.all_gather(w_in, AXES, axis=0, tiled=True)]
        out_parts = [lax.all_gather(w_out, AXES, axis=0, tiled=True)]
    layer_out, grad_third, *rest = ffn(
        spot, plans, third_low, upper, cotangent, in_parts, out_parts
    )
    half = len(rest) // 2
    parts = rest if tiled else [part[None] for part in rest]
    in_sums = product_sums(cube, cube.plan_b, parts[:half])
    out_sums = product_sums(cube, cube.plan_a, parts[half:])
    grad_upper, grad_cross_branch, grad_crossed, grad_gain_third = fused(
        third_back,
        [(tile, full), (tile, low), (tile, low), ((1, D), full)],
        grad_third,
        upper,
        cotangent,
        gain_three,
        attn_full[7],
    )
    in_sums.take(grad_crossed)
    started = send_all((in_sums,))
    out_sums.take(*started)
    grad_crossed = after(grad_crossed, *started, *send_all((out_sums,)))
    sums_scratch = [pltpu.VMEM((tile[0], LANES), full)] * 2
    memory_key_low, memory_value_low, grad_middle, grad_self_branch, grad_mixed, *rest = by_pair(
        functools.partial(cross_back, rows, plans),
        [
            core[None],
            cross_query,
            memory_keys,
            memory_values,
            grad_crossed,
            cross_probs,
            second_low,
            memory,
            crossed_low,
            grad_cross_branch,
            middle,
            grad_upper,
            gain_two,
            attn_full[4],
            attn_full[3],
        ],
        [(tile, low)] * 2
        + [(tile, full), (tile, low), (tile, low), ((1, D), full)]
        + product_outs(cube, 4),
        [pltpu.VMEM(tile, low)] + sums_scratch,
        (probs,),
        "cross_back",
        late=(6, 7, 8, 9, 10, 11, 13, 14),
    )
    grad_gain_second = rest[0]
    for each in (in_sums, out_sums):
        each.take(grad_mixed)
    arrived = in_sums.terms[-1][0], out_sums.terms[-1][0]
    cross_sums = product_sums(cube, cube.plan_a, rest[1:], *arrived)
    started = send_all((in_sums, out_sums))
    cross_sums.take(*started)
    grad_mixed = after(grad_mixed, *started, *send_all((cross_sums,)))
    lots = (PAIRS, 8, 2 * LANES)
    outs = product_outs(cube, 2)
    query_low, key_low, value_low, score_sums, *rest = by_pair(
        functools.partial(self_back, rows, (cube.plan_d, cube.plan_c)),
        [
            core[None],
            query,
            keys,
            values,
            grad_mixed,
            self_probs,
            first_low,
            mixed_low,
            grad_self_branch,
        ],
        [(tile, low)] * 3 + [(lots, full)] + outs[:1] * 2 + outs[1:] * 2,
        sums_scratch,
        (probs, lots),
        "self_back",
        late=(6, 7, 8),
    )
    for each in (in_sums, out_sums):
        each.take(query_low)
    arrived = in_sums.terms[-1][0], out_sums.terms[-1][0]
    late_sums = product_sums(cube, cube.plan_c, rest[::2], *arrived)
    early_sums = product_sums(cube, cube.plan_d, rest[1::2], *arrived)
    cross_sums.take(query_low)
    started = send_all((out_sums, in_sums, cross_sums))
    late_sums.take(*started)
    early_sums.take(*started)
    started = started + send_all((early_sums, late_sums))
    query_low = after(query_low, *started)
    grad_tokens, grad_memory, extra = fused(
        last_back,
        [(tile, full), (tile, full), ((8, D), full)],
        query_low,
        key_low,
        value_low,
        memory_key_low,
        memory_value_low,
        tokens,
        grad_middle,
        gain_one,
        *attn_full[:3],
        *attn_full[5:7],
        score_sums,
        places,
        grad_gain_second,
        grad_gain_third,
    )

    def move(chains, *behind):
        for each in chains:
            each.take(*behind)
        return send_all(chains)

    started = move((early_sums, late_sums, out_sums, in_sums), grad_tokens)
    move((cross_sums,), *started)
    started = move((early_sums, late_sums))
    while in_sums.going():
        move((out_sums, in_sums))
    while cross_sums.going():
        started = started + move((cross_sums,), *started)
    for each in (out_sums, in_sums):
        each.take(*started)
    grad_in, in_rows, grad_out, out_rows, ffn_columns = last_terms(
        ffn_last, spot, [in_sums, out_sums], [(1, rows, FF), (1, FF // cube.count, D)], [], 8
    )
    while early_sums.going():
        move((early_sums, late_sums), ffn_columns)
    cross_sums.take()
    cross_grads, cross_rows, cross_columns = last_terms(
        cross_last, spot, [cross_sums], [(4, rows, D)], [], 8
    )
    early_sums.take(cross_columns)
    late_sums.take(cross_columns)
    early_grads, early_rows, late_grads, late_rows, columns = last_terms(
        self_last,
        spot,
        [early_sums, late_sums],
        [(2, rows, D)] * 2,
        [cross_columns, ffn_columns, extra],
        24,
    )
    grad_attn = jnp.concatenate([early_grads, late_grads, cross_grads], axis=0)
    grad_in, grad_out = grad_in[0], grad_out[0]
    row_means = jnp.concatenate([early_rows, late_rows, cross_rows, in_rows], axis=0)
    new_row_main = DECAY * row_main + (1.0 - DECAY) * row_means
    new_row_out = DECAY * row_out + (1.0 - DECAY) * out_rows[0]
    columns = cube.total(columns)
    col_means = jnp.concatenate([columns[:8] / D, columns[8:9] / FF], axis=0)
    new_col_main = DECAY * col_main + (1.0 - DECAY) * col_means
    new_col_in = DECAY * col_in + (1.0 - DECAY) * (columns[9 : 9 + FF // D].reshape(FF) / D)
    grad_gains = lax.dynamic_slice_in_dim(columns[16:19], cube.me * rows, rows, 1)
    grad_table = columns[19, : BUCKETS * HEADS].reshape(BUCKETS, HEADS)
    return (
        layer_out,
        grad_tokens,
        grad_memory,
        grad_attn,
        grad_in,
        grad_out,
        grad_gains,
        grad_table,
        new_row_main,
        new_row_out,
        new_col_main,
        new_col_in,
    )


def solution(mesh):
    placed = (
        P(("wide", "narrow"), None),
        P(("wide", "narrow"), None),
        P(("wide", "narrow"), None),
        P(("wide", "narrow"), None),
        P(("wide", "narrow"), None),
        P(("wide", "narrow"), None),
        P(None, ("wide", "narrow"), None),
        P(("wide", "narrow"), None),
        P(("wide", "narrow"), None),
        P(None, ("wide", "narrow")),
        P(),
        P(None, ("wide", "narrow")),
        P(("wide", "narrow")),
        P(),
        P(),
    )
    return jax.shard_map(
        on_device,
        mesh=mesh,
        in_specs=placed,
        out_specs=(
            P(("wide", "narrow"), None),
            P(("wide", "narrow"), None),
            P(("wide", "narrow"), None),
            P(None, ("wide", "narrow"), None),
            P(("wide", "narrow"), None),
            P(("wide", "narrow"), None),
            P(None, ("wide", "narrow")),
            P(),
            P(None, ("wide", "narrow")),
            P(("wide", "narrow")),
            P(),
            P(),
        ),
        check_vma=False,
    )
```
